32 devices in a mesh: section: 2 (over core), batch: 4 (over z), tensor: 4 (over y, x).
Axes of the slice: x: 2, y: 2, z: 4, core: 2. Of those that a mesh axis runs over, the one named last changes fastest.
Arguments:
- token_ids: int32 [8, 1024], P('batch'), may hold values from 0 to 32767
- seq_lengths: int32 [8], P('batch'), may hold values from 64 to 1024, as said below
- embed_table: float32 [32768, 768], P(('section', 'tensor'), 'batch'), may hold values from -0.21875 to 0.21875
- norm_gains: float32 [2, 2, 768], P(None, None, ('section', 'batch', 'tensor')), may hold values from 0.5 to 1.5
- final_gain: float32 [768], P(('section', 'batch', 'tensor')), may hold values from 0.5 to 1.5
- qkv_weight: float32 [2, 768, 3, 768], P('section', 'batch', None, 'tensor'), may hold values from -0.21875 to 0.21875
- qkv_conv: float32 [2, 3, 3, 12, 64], P('section', None, None, 'tensor', 'batch'), may hold values from -3 to 3
- out_weight: float32 [2, 768, 768], P('section', 'tensor', 'batch'), may hold values from -2.5 to 2.5
- up_weight: float32 [2, 768, 3072], P('section', 'batch', 'tensor'), may hold values from -0.21875 to 0.21875
- down_weight: float32 [2, 3072, 768], P('section', 'tensor', 'batch'), may hold values from -0.109375 to 0.109375
- logit_grad: bfloat16 [8, 1024, 32768], P('batch', None, ('section', 'tensor')), may hold values from -6 to 6
Outputs:
- logits: bfloat16 [8, 1024, 32768], P('batch', None, ('section', 'tensor'))
- table_grad: float32 [32768, 768], P(('section', 'tensor'), 'batch')
- gains_grad: float32 [2, 2, 768], P(None, None, ('section', 'batch', 'tensor'))
- final_gain_grad: float32 [768], P(('section', 'batch', 'tensor'))
- qkv_grad: float32 [2, 768, 3, 768], P('section', 'batch', None, 'tensor')
- conv_grad: float32 [2, 3, 3, 12, 64], P('section', None, None, 'tensor', 'batch')
- out_grad: float32 [2, 768, 768], P('section', 'tensor', 'batch')
- up_grad: float32 [2, 768, 3072], P('section', 'batch', 'tensor')
- down_grad: float32 [2, 3072, 768], P('section', 'tensor', 'batch')
The draws below stay inside these ranges and needn't reach their ends.
Inputs may be any that keep to these rules, and one draw needn't show every extreme that they name: `seq_lengths`: among the 2 sequences of each index of batch (aligned blocks of 2) at least one has length 1024.
All inputs are finite; a program needn't handle non-finite values.
Results may differ from the reference program's by a relative error of at most 0.025.
Values may be sent and summed in bfloat16 or wider, within the bound.
A program may use at most 192 MiB of HBM per device.

```python
import math
import jax
import jax.numpy as jnp
import numpy as np
from jax import lax

D = 768
HEADS = 12
HEAD = 64
FF = 3072
VOCAB = 32768
SEQ_LEN = 1024
MICRO = 2
SEQS = 8
N_SECTION = 2


def draw_seq_lengths(key, part):
    key = jax.random.fold_in(key, 7)
    first_key, second_key, pick_key = jax.random.split(key, 3)
    shortest = min(64, SEQ_LEN // 4)
    first_draw = jax.random.randint(first_key, (SEQS,), shortest, SEQ_LEN + 1)
    second_draw = jax.random.randint(second_key, (SEQS,), shortest, SEQ_LEN + 1)
    chosen = jax.random.randint(pick_key, (SEQS // MICRO,), 0, MICRO)
    slot = jnp.arange(SEQS) % MICRO
    longest = slot == jnp.repeat(chosen, MICRO)
    return jnp.where(longest, SEQ_LEN, jnp.minimum(first_draw, second_draw)).astype(jnp.int32)


def plant(result, stream_key, smallest, top_value):
    index_at = [jax.random.randint(jax.random.fold_in(stream_key, axis), (), 0, length) for axis, length in enumerate(result.shape)]
    main_axis = result.shape.index(max(result.shape))
    neighbour = index_at[:main_axis] + [(index_at[main_axis] + 1) % result.shape[main_axis]] + index_at[main_axis + 1:]
    return result.at[tuple(index_at)].set(smallest).at[tuple(neighbour)].set(top_value)


def shard_levels(rng, shape, cuts, smallest, largest):
    loudness, own = 1.0, jax.random.fold_in(rng, 6)
    for axis_at, parts in cuts:
        steps = jnp.exp(jax.random.uniform(jax.random.fold_in(own, axis_at), (parts,), jnp.float32, smallest / len(cuts), largest / len(cuts)))
        loudness = loudness * jnp.repeat(steps, shape[axis_at] // parts).reshape([-1 if axis == axis_at else 1 for axis in range(len(shape))])
    return loudness


def rank_table(count, lean):
    weights = [(1 << 20) // math.isqrt(standing ** lean) + 1 for standing in range(1, count + 1)]
    deviation = 1 + sum(weights) // (1 << 30)
    return np.cumsum(np.array([max(1, weight // deviation) for weight in weights]))


def ranked(rng, shape, amount, lean):
    table = rank_table(amount, lean)
    pick = jax.random.randint(jax.random.fold_in(rng, 1), shape, 0, int(table[amount - 1]))
    standing = jnp.searchsorted(jnp.asarray(table, jnp.int32), pick, side="right")
    return jax.random.permutation(jax.random.fold_in(rng, 2), amount)[standing].astype(jnp.int32)


def noise(rng, shape, spread, bound, shards=(), held_as=jnp.bfloat16):
    drawn = jax.random.normal(rng, shape, jnp.float32) * spread
    if len(shards) > 0:
        drawn = shard_levels(rng, shape, shards, -0.22, 0.18) * drawn
    return jnp.clip(drawn, min=-bound, max=bound).astype(held_as)


def setup_inputs(seed: int = 0) -> dict:
    streams_of = jax.random.split(jax.random.key(seed), 12)
    return {
        "token_ids": plant(ranked(streams_of[0], (SEQS, SEQ_LEN), VOCAB, 2), jax.random.fold_in(streams_of[0], 3), 0, VOCAB - 1).astype(jnp.int32),
        "seq_lengths": draw_seq_lengths(jax.random.fold_in(streams_of[11], 71), 0),
        "embed_table": noise(streams_of[2], (VOCAB, D), D ** -0.5, 0.21875, ((0, 8), (1, 4)), jnp.float32),
        "norm_gains": jnp.clip(1.0 + 0.1 * jax.random.normal(streams_of[3], (N_SECTION, 2, D), jnp.float32), 0.5, 1.5),
        "final_gain": jnp.clip(1.0 + 0.1 * jax.random.normal(streams_of[4], (D,), jnp.float32), 0.5, 1.5),
        "qkv_weight": noise(streams_of[5], (N_SECTION, D, 3, D), D ** -0.5, 0.21875, ((0, 2), (1, 4), (3, 4)), jnp.float32),
        "qkv_conv": noise(streams_of[6], (N_SECTION, 3, 3, HEADS, HEAD), 0.6, 3.0, ((0, 2), (3, 4), (4, 4)), jnp.float32),
        "out_weight": noise(streams_of[7], (N_SECTION, D, D), (max(1, 8 * D // SEQ_LEN)) ** -0.5, 2.5, ((0, 2), (1, 4), (2, 4)), jnp.float32),
        "up_weight": noise(streams_of[8], (N_SECTION, D, FF), D ** -0.5, 0.21875, ((0, 2), (1, 4), (2, 4)), jnp.float32),
        "down_weight": noise(streams_of[9], (N_SECTION, FF, D), FF ** -0.5, 0.109375, ((0, 2), (1, 4), (2, 4)), jnp.float32),
        "logit_grad": noise(streams_of[10], (SEQS, SEQ_LEN, VOCAB), 1.0, 6.0, ((0, 4), (2, 8))),
    }


@jax.custom_vjp
def low(v):
    return lax.optimization_barrier(v.astype(jnp.bfloat16)).astype(jnp.float32)

@jax.custom_vjp
def low_back(v):
    return v

def low_keep(v):
    return (low(v), None)

def low_pass(kept, grad):
    return (grad,)

def back_keep(v):
    return (v, None)

def back_low(kept, grad):
    return (low(grad),)
low.defvjp(low_keep, low_pass)
low_back.defvjp(back_keep, back_low)
highest = lax.Precision.HIGHEST
norm_eps = 1e-06
masked_score = -1e+30

def rms_norm(values, gain):
    factor = lax.rsqrt(lax.optimization_barrier(jnp.mean(values * values, axis=-1, keepdims=True)) + norm_eps)
    return values * factor * gain

def matmul(left, right):
    return jnp.dot(left, right, precision=highest, preferred_element_type=jnp.float32)

def causal_mix(projected, taps):
    once = jnp.pad(projected, ((1, 0), (0, 0)))[:-1]
    twice = jnp.pad(projected, ((2, 0), (0, 0)))[:-2]
    return taps[0] * projected + taps[1] * once + taps[2] * twice

def layer_forward(resid, length, gains, qkv_w, conv_w, out_w, up_w, down_w):
    positions = jnp.arange(resid.shape[0])
    normed = low(rms_norm(resid, low(gains[0])))
    projected = low_back(matmul(normed, low(qkv_w).reshape(D, 3 * D)))
    taps = low(conv_w).reshape(3, 3, D).transpose(1, 0, 2).reshape(3, 3 * D)
    mixed = low(causal_mix(projected, taps)).reshape(-1, 3, HEADS, HEAD)
    queries = mixed[:, 0]
    keys_all = mixed[:, 1]
    values_all = mixed[:, 2]
    scores = low_back(jnp.einsum('qhd,khd->hqk', queries, keys_all, precision=highest) * HEAD ** (-0.5))
    allowed = (positions[None, :] <= positions[:, None]) & (positions[None, :] < length)
    scores = jnp.where(allowed[None], scores, masked_score)
    peak = lax.optimization_barrier(jnp.max(scores, axis=-1, keepdims=True))
    raised = jnp.exp(scores - peak)
    probs = raised / lax.optimization_barrier(jnp.sum(raised, axis=-1, keepdims=True))
    context = jnp.einsum('hqk,khd->qhd', low(probs), values_all, precision=highest)
    context = low_back(low(context)).reshape(-1, D)
    middle = resid + low_back(matmul(context, low(out_w)))
    normed_ffn = low(rms_norm(middle, low(gains[1])))
    hidden = low_back(matmul(normed_ffn, low(up_w)))
    active = low(jnp.square(jnp.maximum(hidden, 0.0)))
    return middle + low_back(matmul(active, low(down_w)))

def sequence_logits(params, token_row, length):
    table, norm_gains, final_gain, qkv_weight, qkv_conv, out_weight, up_weight, down_weight = params
    table_low = low(table)
    resid = low_back(table_low[token_row]) * math.sqrt(D)
    resid = layer_forward(resid, length, norm_gains[0], qkv_weight[0], qkv_conv[0], out_weight[0], up_weight[0], down_weight[0])
    resid = low_back(low(resid))
    resid = layer_forward(resid, length, norm_gains[1], qkv_weight[1], qkv_conv[1], out_weight[1], up_weight[1], down_weight[1])
    final_rows = low(resid)
    normed = low(rms_norm(final_rows, low(final_gain)))
    return matmul(normed, table_low.T)

def reference(token_ids, seq_lengths, embed_table, norm_gains, final_gain, qkv_weight, qkv_conv, out_weight, up_weight, down_weight, logit_grad):
    params = (embed_table, norm_gains, final_gain, qkv_weight, qkv_conv, out_weight, up_weight, down_weight)
    positions = jnp.arange(SEQ_LEN)

    def one_sequence(totals, inputs):
        token_row, length, cotangent = inputs
        logits, pullback = jax.vjp(lambda weights: sequence_logits(weights, token_row, length), params)
        masked = jnp.where((positions < length)[:, None], cotangent.astype(jnp.float32), 0.0)
        grads = pullback(masked)[0]
        summed = jax.tree.map(lambda total, grad: total + grad, totals, grads)
        return (summed, logits.astype(jnp.bfloat16))
    zeros = jax.tree.map(jnp.zeros_like, params)
    totals, logits = lax.scan(one_sequence, zeros, (token_ids, seq_lengths, logit_grad))
    return (logits, totals[0], totals[1], totals[2], totals[3], totals[4], totals[5], totals[6], totals[7])
```

```python
import math

import jax
import jax.numpy as jnp
from jax import lax
from jax.sharding import PartitionSpec as P

D = 768
HEAD = 64

norm_eps = 1e-06
masked_score = -1e30
bf16 = jnp.bfloat16
f32 = jnp.float32


def mm(left, right, left_dim, right_dim):
    return lax.dot_general(
        left, right, (((left_dim,), (right_dim,)), ((), ())), preferred_element_type=f32
    )


def norm_factor(rows):
    return lax.rsqrt(jnp.mean(rows * rows, axis=-1, keepdims=True) + norm_eps)


def norm_back(grad, rows, gain):
    factor = norm_factor(rows)
    scaled = grad * gain
    inner = jnp.mean(scaled * rows, axis=-1, keepdims=True)
    grad_rows = factor * scaled - rows * (factor * factor * factor * inner)
    return grad_rows, jnp.sum(grad * rows * factor, axis=0)


def swap_core(block):
    return lax.ppermute(block, "section", [(0, 1), (1, 0)])


def from_peer(block, mask):
    count = lax.axis_size("tensor")
    return lax.ppermute(block, "tensor", [(at, at ^ mask) for at in range(count)])


def gather_rows(rows):
    count = lax.axis_size("tensor")
    return jnp.stack([rows] + [from_peer(rows, mask) for mask in range(1, count)])


def scatter_rows(parts):
    count = lax.axis_size("tensor")
    total = parts[0].astype(f32)
    for mask in range(1, count):
        total = total + from_peer(parts[mask], mask).astype(f32)
    return total


def in_order(parts, me):
    return jnp.concatenate([parts[me ^ at] for at in range(parts.shape[0])], 0)


def out_of_order(rows, me, count):
    split = rows.reshape(count, -1, rows.shape[-1])
    return jnp.stack([split[me ^ at] for at in range(count)])


def causal_mix(projected, taps):
    once = jnp.pad(projected, ((1, 0), (0, 0)))[:-1]
    twice = jnp.pad(projected, ((2, 0), (0, 0)))[:-2]
    return taps[0] * projected + taps[1] * once + taps[2] * twice


def causal_mix_back(grad, projected, taps):
    ahead_one = jnp.pad(grad, ((0, 1), (0, 0)))[1:]
    ahead_two = jnp.pad(grad, ((0, 2), (0, 0)))[2:]
    grad_in = taps[0] * grad + taps[1] * ahead_one + taps[2] * ahead_two
    once = jnp.pad(projected, ((1, 0), (0, 0)))[:-1]
    twice = jnp.pad(projected, ((2, 0), (0, 0)))[:-2]
    grad_taps = jnp.stack(
        [jnp.sum(grad * projected, 0), jnp.sum(grad * once, 0), jnp.sum(grad * twice, 0)]
    )
    return (grad_in, grad_taps)


def allowed_keys(lead, reach, length):
    query_at = jnp.arange(lead, reach)[:, None]
    key_at = jnp.arange(reach)[None, :]
    return (key_at <= query_at) & (key_at < length)


def attend(queries, keys_all, values_all, length):
    total = queries.shape[0]
    block = min(512, total)
    factor = queries.shape[-1] ** (-0.5)
    outputs = []
    totals = []
    for index in range(total // block):
        lead = index * block
        reach = lead + block
        scores = (
            jnp.einsum("qhd,khd->hqk", queries[lead:reach], keys_all[:reach], preferred_element_type=f32)
            * factor
        )
        scores = jnp.where(allowed_keys(lead, reach, length)[None], scores, masked_score)
        peak = jnp.max(scores, axis=-1, keepdims=True)
        raised = jnp.exp(scores - peak)
        weight_sum = jnp.sum(raised, axis=-1, keepdims=True)
        probs = (raised / weight_sum).astype(bf16)
        result = jnp.einsum("hqk,khd->qhd", probs, values_all[:reach], preferred_element_type=f32)
        outputs.append(result.astype(bf16))
        totals.append((peak + jnp.log(weight_sum))[..., 0])
    return (jnp.concatenate(outputs, 0), jnp.concatenate(totals, 1))


def attend_back(grad_out, queries, keys_all, values_all, length, totals):
    total = queries.shape[0]
    block = min(512, total)
    factor = queries.shape[-1] ** (-0.5)
    grad_queries = []
    grad_keys = jnp.zeros(keys_all.shape, f32)
    grad_values = jnp.zeros(values_all.shape, f32)
    for index in range(total // block):
        lead = index * block
        reach = lead + block
        scores = (
            jnp.einsum("qhd,khd->hqk", queries[lead:reach], keys_all[:reach], preferred_element_type=f32)
            * factor
        )
        allowed = allowed_keys(lead, reach, length)[None]
        probs = jnp.where(allowed, jnp.exp(scores - totals[:, lead:reach, None]), 0.0)
        grad_block = grad_out[lead:reach]
        grad_probs = jnp.einsum(
            "qhd,khd->hqk", grad_block, values_all[:reach], preferred_element_type=f32
        )
        inner = jnp.sum(probs * grad_probs, axis=-1, keepdims=True)
        grad_scores = (probs * (grad_probs - inner)).astype(bf16)
        grad_queries.append(
            jnp.einsum("hqk,khd->qhd", grad_scores, keys_all[:reach], preferred_element_type=f32)
            * factor
        )
        grad_keys = grad_keys.at[:reach].add(
            jnp.einsum("hqk,qhd->khd", grad_scores, queries[lead:reach], preferred_element_type=f32)
            * factor
        )
        grad_values = grad_values.at[:reach].add(
            jnp.einsum("hqk,qhd->khd", probs.astype(bf16), grad_block, preferred_element_type=f32)
        )
    return (jnp.concatenate(grad_queries, 0), grad_keys, grad_values)


def layer_forward(resid, length, weights, me):
    gain_attn, gain_ffn, qkv_mat, taps, out_turned, up_mat, down_turned = weights
    count = lax.axis_size("tensor")
    local_width = out_turned.shape[1]
    heads_here = local_width // HEAD
    normed = (resid * norm_factor(resid) * gain_attn).astype(bf16)
    gathered = in_order(gather_rows(normed), me)
    projected = mm(gathered, qkv_mat, 1, 0)
    mixed = causal_mix(projected, taps).astype(bf16)
    triple = mixed.reshape(-1, 3, heads_here, HEAD)
    context, totals = attend(triple[:, 0], triple[:, 1], triple[:, 2], length)
    context = context.reshape(-1, local_width)
    partial = out_of_order(mm(context, out_turned, 1, 1).astype(bf16), me, count)
    middle = resid + scatter_rows(partial)
    normed_ffn = (middle * norm_factor(middle) * gain_ffn).astype(bf16)
    gathered_ffn = gather_rows(normed_ffn).reshape(-1, D)
    hidden = mm(gathered_ffn, up_mat, 1, 0)
    active = jnp.square(jnp.maximum(hidden, 0.0)).astype(bf16)
    lowered = mm(active, down_turned, 1, 1).astype(bf16).reshape(count, -1, D)
    output = middle + scatter_rows(lowered)
    kept = (resid, gathered, projected, mixed, context, totals, middle, gathered_ffn, hidden, active)
    return (output, kept)


def layer_backward(grad_out, length, weights, kept, me):
    gain_attn, gain_ffn, qkv_mat, taps, out_turned, up_mat, down_turned = weights
    resid, gathered, projected, mixed, context, totals, middle, gathered_ffn, hidden, active = kept
    count = lax.axis_size("tensor")
    local_width = out_turned.shape[1]
    heads_here = local_width // HEAD
    grad_rows = gather_rows(grad_out.astype(bf16)).reshape(-1, D)
    grad_active = mm(grad_rows, down_turned, 1, 0)
    grad_hidden = (grad_active * 2.0 * jnp.maximum(hidden, 0.0)).astype(bf16)
    grad_normed_ffn = scatter_rows(mm(grad_hidden, up_mat, 1, 1).astype(bf16).reshape(count, -1, D))
    grad_down = mm(grad_rows, active, 0, 0)
    grad_up = mm(gathered_ffn, grad_hidden, 0, 0)
    grad_middle_norm, grad_gain_ffn = norm_back(grad_normed_ffn, middle, gain_ffn)
    grad_middle = grad_out + grad_middle_norm
    grad_rows_attn = in_order(gather_rows(grad_middle.astype(bf16)), me)
    grad_outmat = mm(grad_rows_attn, context, 0, 0)
    grad_context = mm(grad_rows_attn, out_turned, 1, 0).astype(bf16).reshape(-1, heads_here, HEAD)
    triple = mixed.reshape(-1, 3, heads_here, HEAD)
    grad_queries, grad_keys, grad_values = attend_back(
        grad_context, triple[:, 0], triple[:, 1], triple[:, 2], length, totals
    )
    grad_mixed = jnp.stack([grad_queries, grad_keys, grad_values], 1).reshape(-1, 3 * local_width)
    grad_projected, grad_taps = causal_mix_back(grad_mixed, projected, taps)
    grad_projected = grad_projected.astype(bf16)
    partial = mm(grad_projected, qkv_mat, 1, 1).astype(bf16)
    grad_normed = scatter_rows(out_of_order(partial, me, count))
    grad_qkv = mm(gathered, grad_projected, 0, 0)
    grad_resid_norm, grad_gain_attn = norm_back(grad_normed, resid, gain_attn)
    grad_in = grad_middle + grad_resid_norm
    attn_blob = jnp.concatenate([grad_qkv.astype(bf16), grad_outmat.astype(bf16)], 1)
    ffn_blob = jnp.concatenate([grad_up.astype(bf16), grad_down.astype(bf16)], 1)
    return (grad_in, attn_blob, ffn_blob, grad_gain_attn, grad_gain_ffn, grad_taps)


def both_layers(block):
    gathered = lax.all_gather(block, "batch", axis=0, tiled=True)
    return gathered, swap_core(gathered)


def on_device(
    token_ids,
    seq_lengths,
    embed_table,
    norm_gains,
    final_gain,
    qkv_weight,
    qkv_conv,
    out_weight,
    up_weight,
    down_weight,
    logit_grad,
):
    section = lax.axis_index("section")
    first = section == 0
    me = lax.axis_index("tensor")
    at_batch = lax.axis_index("batch")
    tensor_count = lax.axis_size("tensor")
    batch_count = lax.axis_size("batch")
    section_count = lax.axis_size("section")
    slot_length = token_ids.shape[1]
    shard_rows = slot_length // tensor_count
    local_width = out_weight.shape[1]
    heads_here = local_width // HEAD
    hidden_width = up_weight.shape[2]
    root_scale = math.sqrt(D)
    depth = D // batch_count
    length = seq_lengths[section]

    table_own = embed_table.astype(bf16).T
    attn_own = jnp.concatenate(
        [
            qkv_weight[0].reshape(depth, 3 * local_width).astype(bf16),
            out_weight[0].astype(bf16).T,
        ],
        1,
    )
    ffn_own = jnp.concatenate([up_weight[0].astype(bf16), down_weight[0].astype(bf16).T], 1)
    small = jnp.concatenate(
        [
            norm_gains.astype(bf16).reshape(-1),
            final_gain.astype(bf16),
            qkv_conv.astype(bf16).reshape(-1),
        ]
    )
    gain_width = final_gain.shape[0]
    small_all = lax.all_gather(small, ("section", "batch", "tensor"), axis=0, tiled=False)
    gains_all = small_all[:, : 5 * gain_width].astype(f32).reshape(-1, 5, gain_width)
    gains_all = gains_all.transpose(1, 0, 2).reshape(5, D)
    taps_all = small_all[:, 5 * gain_width :].reshape(
        section_count, batch_count, tensor_count, 3, 3, heads_here, -1
    )
    taps_here = lax.dynamic_index_in_dim(taps_all, me, 2, keepdims=False).astype(f32)
    taps_here = taps_here.transpose(0, 3, 2, 4, 1, 5).reshape(section_count, 3, 3 * local_width)
    final_scale = gains_all[4]

    attn_mine, attn_other = both_layers(attn_own)
    ffn_mine, ffn_other = both_layers(ffn_own)
    table_turned = lax.all_gather(table_own, "batch", axis=0, tiled=True)

    weights = []
    for layer in range(section_count):
        attn_layer = jnp.where(section == layer, attn_mine, attn_other)
        ffn_layer = jnp.where(section == layer, ffn_mine, ffn_other)
        weights.append(
            (
                gains_all[2 * layer],
                gains_all[2 * layer + 1],
                attn_layer[:, : 3 * local_width],
                taps_here[layer],
                attn_layer[:, 3 * local_width :],
                ffn_layer[:, :hidden_width],
                ffn_layer[:, hidden_width:],
            )
        )

    vocab_rows = embed_table.shape[0]
    all_ids = lax.all_gather(token_ids, "batch", axis=0, tiled=False)
    owner_start = (section * tensor_count + me) * vocab_rows
    local_ids = all_ids - owner_start
    inside = (local_ids >= 0) & (local_ids < vocab_rows)
    safe_ids = jnp.clip(local_ids, 0, vocab_rows - 1)
    picked = jnp.where(inside[..., None], embed_table.astype(bf16)[safe_ids], jnp.zeros((), bf16))
    picked = picked.reshape(batch_count, section_count, tensor_count, shard_rows, depth)
    mine = lax.dynamic_index_in_dim(picked, section, 1, keepdims=False)
    theirs = lax.dynamic_index_in_dim(picked, 1 - section, 1, keepdims=False)
    joined = mine + swap_core(theirs)
    total = lax.dynamic_index_in_dim(joined, me, 1, keepdims=False)
    for mask in range(1, tensor_count):
        total = total + from_peer(
            lax.dynamic_index_in_dim(joined, me ^ mask, 1, keepdims=False), mask
        )
    embedded = lax.all_to_all(total, "batch", 0, 0, tiled=False)
    embedded = embedded.transpose(1, 0, 2).reshape(shard_rows, D)

    resid = embedded.astype(f32) * root_scale
    output, kept_first = layer_forward(resid, length, weights[0], me)
    output, kept_second = layer_forward(output.astype(bf16).astype(f32), length, weights[1], me)
    final_rows = output.astype(bf16).astype(f32)

    valid = jnp.arange(slot_length)[None, :] < seq_lengths[:, None]
    grad_both = mm(logit_grad.reshape(-1, vocab_rows), table_turned, 1, 1).astype(bf16)
    grad_both = grad_both.reshape(section_count, slot_length, D)
    grad_both = jnp.where(valid[..., None], grad_both, jnp.zeros((), bf16))
    grad_mine = lax.dynamic_index_in_dim(grad_both, section, 0, keepdims=False)
    grad_theirs = lax.dynamic_index_in_dim(grad_both, 1 - section, 0, keepdims=False)
    grad_joined = (grad_mine.astype(f32) + swap_core(grad_theirs).astype(f32)).astype(bf16)
    grad_final = scatter_rows(out_of_order(grad_joined, me, tensor_count))

    normed_final = (final_rows * norm_factor(final_rows) * final_scale).astype(bf16)
    final_all = in_order(gather_rows(normed_final), me)
    final_other = swap_core(final_all)
    final_both = jnp.stack(
        [jnp.where(first, final_all, final_other), jnp.where(first, final_other, final_all)]
    )
    logits = jnp.einsum(
        "srd,dv->srv", final_both, table_turned, preferred_element_type=f32
    ).astype(bf16)
    masked_final = jnp.where(valid[..., None], final_both, jnp.zeros((), bf16))
    head_table = mm(masked_final.reshape(-1, D), logit_grad.reshape(-1, vocab_rows), 0, 0)
    head_done = lax.psum_scatter(head_table.astype(bf16), "batch", scatter_dimension=0, tiled=True)

    grad_rows, grad_final_gain = norm_back(grad_final, final_rows, final_scale)
    grad_rows, attn_second, ffn_second, gain_2a, gain_2f, taps_second = layer_backward(
        grad_rows, length, weights[1], kept_second, me
    )
    grad_rows = grad_rows.astype(bf16).astype(f32)
    grad_rows, attn_first, ffn_first, gain_1a, gain_1f, taps_first = layer_backward(
        grad_rows, length, weights[0], kept_first, me
    )
    embed_grad = (grad_rows * root_scale).astype(bf16)

    def reduced(blob):
        halves = blob.reshape(batch_count, section_count, depth // section_count, -1)
        keep = lax.dynamic_index_in_dim(halves, section, 1, keepdims=False)
        send = lax.dynamic_index_in_dim(halves, 1 - section, 1, keepdims=False)
        part = (keep.astype(f32) + swap_core(send).astype(f32)).astype(bf16)
        return lax.psum_scatter(part, "batch", scatter_dimension=0, tiled=False)

    def placed(first_part, second_part):
        keep = jnp.where(first, first_part, second_part)
        got = swap_core(jnp.where(first, second_part, first_part))
        return jnp.where(
            first, jnp.concatenate([keep, got], 0), jnp.concatenate([got, keep], 0)
        ).astype(f32)

    attn_done = placed(reduced(attn_first), reduced(attn_second))
    ffn_done = placed(reduced(ffn_first), reduced(ffn_second))
    qkv_done = attn_done[:, : 3 * local_width].reshape(1, depth, 3, local_width)
    out_done = attn_done[:, 3 * local_width :].T[None]
    up_done = ffn_done[:, :hidden_width][None]
    down_done = ffn_done[:, hidden_width:].T[None]

    gain_sums = lax.psum(
        jnp.stack([gain_1a, gain_1f, gain_2a, gain_2f, grad_final_gain]),
        ("section", "batch", "tensor"),
    )
    taps_sums = lax.psum(jnp.stack([taps_first, taps_second]), ("section", "batch"))
    whole_at = (section * batch_count + at_batch) * tensor_count + me
    gain_part = lax.dynamic_slice_in_dim(gain_sums, whole_at * gain_width, gain_width, 1)
    gains_done = gain_part[:4].reshape(2, 2, gain_width)
    final_done = gain_part[4]
    conv_part = lax.dynamic_index_in_dim(taps_sums, section, 0, keepdims=False)
    conv_part = conv_part.reshape(3, 3, heads_here, HEAD).transpose(1, 0, 2, 3)
    conv_done = lax.dynamic_slice_in_dim(
        conv_part, at_batch * qkv_conv.shape[4], qkv_conv.shape[4], 3
    )[None]

    spread = embed_grad.reshape(shard_rows, batch_count, depth).transpose(1, 0, 2)
    spread = lax.all_to_all(spread, "batch", 0, 0, tiled=False)
    around = gather_rows(spread)
    around = jnp.stack([around[me ^ at] for at in range(tensor_count)])
    other = swap_core(around)
    every = jnp.stack([jnp.where(first, around, other), jnp.where(first, other, around)])
    every = every.transpose(2, 0, 1, 3, 4).reshape(-1, depth)
    flat_ids = safe_ids.reshape(-1)
    embed_part = (
        jnp.zeros((vocab_rows, depth), f32)
        .at[flat_ids]
        .add(jnp.where(inside.reshape(-1)[:, None], every.astype(f32), 0.0))
    )
    table_done = head_done.astype(f32).T + embed_part
    return (
        logits,
        table_done,
        gains_done,
        final_done,
        qkv_done,
        conv_done,
        out_done,
        up_done,
        down_done,
    )


def solution(mesh):
    in_specs = (
        P("batch", None),
        P("batch"),
        P(("section", "tensor"), "batch"),
        P(None, None, ("section", "batch", "tensor")),
        P(("section", "batch", "tensor")),
        P("section", "batch", None, "tensor"),
        P("section", None, None, "tensor", "batch"),
        P("section", "tensor", "batch"),
        P("section", "batch", "tensor"),
        P("section", "tensor", "batch"),
        P("batch", None, ("section", "tensor")),
    )
    out_specs = (
        P("batch", None, ("section", "tensor")),
        P(("section", "tensor"), "batch"),
        P(None, None, ("section", "batch", "tensor")),
        P(("section", "batch", "tensor")),
        P("section", "batch", None, "tensor"),
        P("section", None, None, "tensor", "batch"),
        P("section", "tensor", "batch"),
        P("section", "batch", "tensor"),
        P("section", "tensor", "batch"),
    )
    return jax.shard_map(
        on_device, mesh=mesh, in_specs=in_specs, out_specs=out_specs, check_vma=False
    )
```

```python
import functools
import math

import jax
import jax.numpy as jnp
from jax import lax
from jax.experimental import pallas as pl
from jax.experimental.pallas import tpu as pltpu
from jax.sharding import PartitionSpec as P

D = 768
HEAD = 64

norm_eps = 1e-06
masked_score = -1e30
bf16 = jnp.bfloat16
f32 = jnp.float32


def mm(left, right, left_dim, right_dim):
    return lax.dot_general(
        left, right, (((left_dim,), (right_dim,)), ((), ())), preferred_element_type=f32
    )


def norm_factor(rows):
    return lax.rsqrt(jnp.mean(rows * rows, axis=-1, keepdims=True) + norm_eps)


def norm_back(grad, rows, gain):
    factor = norm_factor(rows)
    scaled = grad * gain
    inner = jnp.mean(scaled * rows, axis=-1, keepdims=True)
    grad_rows = factor * scaled - rows * (factor * factor * factor * inner)
    return grad_rows, jnp.sum(grad * rows * factor, axis=0)


MESH = pl.DeviceIdType.MESH


def place():
    core = lax.axis_index("section")
    tensor = lax.axis_index("tensor")
    return core, tensor // 2, tensor % 2, tensor


def remote(src, dst, send, recv, device):
    return pltpu.make_async_remote_copy(
        src_ref=src,
        dst_ref=dst,
        send_sem=send,
        recv_sem=recv,
        device_id=device,
        device_id_type=MESH,
    )


def greet(devices):
    barrier = pltpu.get_barrier_semaphore()
    for device in devices:
        pl.semaphore_signal(barrier, inc=1, device_id=device, device_id_type=MESH)
    pl.semaphore_wait(barrier, len(devices))


def comm_call(body, out_shape, scratch, collective_id, *operands, cargo=None):
    shapes = list(out_shape) if isinstance(out_shape, (list, tuple)) else [out_shape]
    in_specs = [pl.BlockSpec(memory_space=pltpu.VMEM)] * len(operands)
    out_specs = [pl.BlockSpec(memory_space=pltpu.VMEM)] * len(shapes)
    scratch = list(scratch)
    count_in, count_out = len(operands), len(shapes)
    if cargo is not None:
        kind, layer, array = cargo
        operands = operands + (array,)
        in_specs.append(pl.BlockSpec(memory_space=pl.ANY))
        if kind == "out":
            landing = [jax.ShapeDtypeStruct(array.shape, array.dtype)]
        else:
            batches, _, rows, width = array.shape
            landing = [jax.ShapeDtypeStruct((batches, rows, width), array.dtype)] * 2
        shapes += landing
        out_specs += [pl.BlockSpec(memory_space=pl.ANY)] * len(landing)
        scratch += [pltpu.SemaphoreType.DMA((3,))] * 2

    def kernel(*refs):
        ins, rest = refs[: len(operands)], refs[len(operands) :]
        outs, rest = rest[: len(shapes)], rest[len(shapes) :]
        if cargo is None:
            body(*ins, *outs, *rest)
            return
        send, recv = rest[-2:]
        load = functools.partial(
            Outward if kind == "out" else Inward, layer, ins[-1], outs[count_out:], send, recv
        )
        body(*ins[:-1], *outs[:count_out], *rest[:-2], load=load)

    results = pl.pallas_call(
        kernel,
        out_shape=shapes,
        in_specs=in_specs,
        out_specs=out_specs,
        scratch_shapes=scratch,
        compiler_params=pltpu.CompilerParams(
            collective_id=collective_id, has_side_effects=True, vmem_limit_bytes=40 << 20
        ),
    )(*operands)
    return results if len(shapes) > 1 else results[0]


class Outward:
    def __init__(self, layer, source, landing, send, recv):
        core, y, _, tensor = place()
        target = landing[0]
        self.layer, self.core, self.y = layer, core, y
        self.near = remote(source, target, send.at[0], recv.at[0], {"section": 1 - core})
        self.far = remote(
            source, target, send.at[1], recv.at[0], {"section": y, "tensor": tensor + 2 - 4 * y}
        )
        self.local = pltpu.make_async_copy(source, target, recv.at[1])

    def start(self):
        @pl.when(self.core == self.layer)
        def _():
            self.far.start()

            @pl.when(self.y == self.layer)
            def _():
                self.local.start()

            @pl.when(self.y != self.layer)
            def _():
                self.near.start()

    def wait(self):
        stays = (self.core == self.layer) & (self.y == self.layer)

        @pl.when(stays)
        def _():
            self.local.wait()

        @pl.when(jnp.logical_not(stays))
        def _():
            self.far.wait_recv()

        @pl.when(self.core == self.layer)
        def _():
            self.far.wait_send()

            @pl.when(self.y != self.layer)
            def _():
                self.near.wait_send()


class Inward:
    def __init__(self, layer, source, landing, send, recv):
        core, y, _, tensor = place()
        above = tensor + 2 - 4 * y
        self.near = core == y
        self.to_core = remote(
            source.at[:, 1 - y], landing[0], send.at[0], recv.at[0], {"section": 1 - core}
        )
        self.to_same = remote(
            source.at[:, 1 - y], landing[0], send.at[0], recv.at[0], {"tensor": above}
        )
        self.to_both = remote(
            source.at[:, y],
            landing[1],
            send.at[1],
            recv.at[1],
            {"section": 1 - core, "tensor": above},
        )
        self.fill = pltpu.make_async_copy(source.at[:, y], landing[1], recv.at[2])

    def start(self):
        @pl.when(self.near)
        def _():
            self.to_core.start()
            self.fill.start()

        @pl.when(jnp.logical_not(self.near))
        def _():
            self.to_same.start()
            self.to_both.start()

    def wait(self):
        @pl.when(self.near)
        def _():
            self.to_same.wait_recv()
            self.fill.wait()
            self.to_core.wait_send()

        @pl.when(jnp.logical_not(self.near))
        def _():
            self.to_core.wait_recv()
            self.to_both.wait_recv()
            self.to_same.wait_send()
            self.to_both.wait_send()


def greet_group(other, beside, load):
    if load is None:
        greet([other, beside])
        return None
    _, y, _, tensor = place()
    above = tensor + 2 - 4 * y
    greet([other, beside, {"section": 0, "tensor": above}, {"section": 1, "tensor": above}])
    made = load()
    made.start()
    return made


PIECES = 4


def group_gather_kernel(own, out, send, recv, load=None):
    core, _, x, tensor = place()
    other = {"section": 1 - core}
    beside = {"tensor": tensor + 1 - 2 * x}
    here = 2 * core + x
    there = 2 * core + 1 - x
    cargo = greet_group(other, beside, load)
    piece = own.shape[0] // PIECES
    cuts = [pl.ds(at * piece, piece) for at in range(PIECES)]
    across = []
    for at, cut in enumerate(cuts):
        copy = remote(own.at[cut], out.at[here, cut], send.at[at], recv.at[at], beside)
        copy.start()
        across.append(copy)
    last = 2 * PIECES
    direct = remote(own, out.at[here], send.at[last], recv.at[last], other)
    direct.start()
    out[here] = own[...]
    passed = []
    for at, cut in enumerate(cuts):
        across[at].wait_recv()
        copy = remote(
            out.at[there, cut],
            out.at[there, cut],
            send.at[PIECES + at],
            recv.at[PIECES + at],
            other,
        )
        copy.start()
        passed.append(copy)
    for copy in across:
        copy.wait_send()
    direct.wait()
    for copy in passed:
        copy.wait()
    if cargo is not None:
        cargo.wait()


def group_gather(rows, collective_id, cargo=None):
    count, width = rows.shape
    return comm_call(
        group_gather_kernel,
        jax.ShapeDtypeStruct((4, count, width), rows.dtype),
        [pltpu.SemaphoreType.DMA((2 * PIECES + 1,))] * 2,
        collective_id,
        rows,
        cargo=cargo,
    )


def group_reduce_kernel(parts, out, near, far, mixed, send, recv, load=None):
    core, _, x, tensor = place()
    other = {"section": 1 - core}
    beside = {"tensor": tensor + 1 - 2 * x}
    here = 2 * core + x
    there = 2 * core + 1 - x
    over_here = 2 * (1 - core) + x
    over_there = 2 * (1 - core) + 1 - x
    cargo = greet_group(other, beside, load)
    piece = out.shape[0] // PIECES
    cuts = [pl.ds(at * piece, piece) for at in range(PIECES)]
    first = []
    for at, cut in enumerate(cuts):
        copy = remote(
            parts.at[over_there, cut], near.at[1, cut], send.at[at], recv.at[at], other
        )
        copy.start()
        first.append(copy)
    last = 2 * PIECES
    direct = remote(parts.at[over_here], near.at[0], send.at[last], recv.at[last], other)
    direct.start()
    across = []
    for at, cut in enumerate(cuts):
        first[at].wait_recv()
        mixed[cut] = (parts[there, cut].astype(f32) + near[1, cut].astype(f32)).astype(bf16)
        copy = remote(
            mixed.at[cut], far.at[cut], send.at[PIECES + at], recv.at[PIECES + at], beside
        )
        copy.start()
        across.append(copy)
    direct.wait()
    for at, cut in enumerate(cuts):
        across[at].wait_recv()
        out[cut] = (
            parts[here, cut].astype(f32) + near[0, cut].astype(f32) + far[cut].astype(f32)
        )
    for copy in first + across:
        copy.wait_send()
    if cargo is not None:
        cargo.wait()


def group_reduce(parts, collective_id, cargo=None):
    _, count, width = parts.shape
    return comm_call(
        group_reduce_kernel,
        jax.ShapeDtypeStruct((count, width), f32),
        [
            pltpu.VMEM((2, count, width), bf16),
            pltpu.VMEM((count, width), bf16),
            pltpu.VMEM((count, width), bf16),
        ]
        + [pltpu.SemaphoreType.DMA((2 * PIECES + 1,))] * 2,
        collective_id,
        parts,
        cargo=cargo,
    )


def turn_kernel(backward, rounded, *refs, load=None):
    if backward:
        parts, rows, gain, passed, gathered, fresh, gain_grad, near, far, mixed, send, recv = refs
    else:
        parts, rows, gain, gathered, fresh, near, far, mixed, send, recv = refs
    core, _, x, tensor = place()
    other = {"section": 1 - core}
    beside = {"tensor": tensor + 1 - 2 * x}
    here = 2 * core + x
    there = 2 * core + 1 - x
    over_here = 2 * (1 - core) + x
    over_there = 2 * (1 - core) + 1 - x
    cargo = greet_group(other, beside, load)
    piece = fresh.shape[0] // PIECES
    cuts = [pl.ds(at * piece, piece) for at in range(PIECES)]

    def start(src, dst, kind, at, device):
        index = kind * PIECES + at
        made = remote(src, dst, send.at[index], recv.at[index], device)
        made.start()
        return made

    handed, direct = [], []
    for at, cut in enumerate(cuts):
        handed.append(start(parts.at[over_there, cut], near.at[1, cut], 0, at, other))
        direct.append(start(parts.at[over_here, cut], near.at[0, cut], 1, at, other))
    across = []
    for at, cut in enumerate(cuts):
        handed[at].wait_recv()
        mixed[cut] = (parts[there, cut].astype(f32) + near[1, cut].astype(f32)).astype(bf16)
        across.append(start(mixed.at[cut], far.at[cut], 2, at, beside))
    out_across, out_direct, onward = [], [], []
    gains = gain[...]
    for at in range(PIECES + 1):
        if at < PIECES:
            cut = cuts[at]
            direct[at].wait_recv()
            across[at].wait_recv()
            total = (
                parts[here, cut].astype(f32) + near[0, cut].astype(f32) + far[cut].astype(f32)
            )
            held = rows[cut]
            if backward:
                factor = norm_factor(held)
                scaled = total * gains
                inner = jnp.mean(scaled * held, axis=-1, keepdims=True)
                new = passed[cut] + factor * scaled - held * (factor * factor * factor * inner)
                gain_part = jnp.sum(total * held * factor, axis=0, keepdims=True)
                gain_grad[...] = gain_part if at == 0 else gain_grad[...] + gain_part
                if rounded:
                    new = new.astype(bf16).astype(f32)
                shown = new.astype(bf16)
            else:
                new = held + total
                if rounded:
                    new = new.astype(bf16).astype(f32)
                shown = (new * norm_factor(new) * gains).astype(bf16)
            fresh[cut] = new
            gathered[here, cut] = shown
            out_across.append(start(gathered.at[here, cut], gathered.at[here, cut], 3, at, beside))
            out_direct.append(start(gathered.at[here, cut], gathered.at[here, cut], 4, at, other))
        if at >= 1:
            cut = cuts[at - 1]
            out_across[at - 1].wait_recv()
            onward.append(start(gathered.at[there, cut], gathered.at[there, cut], 5, at - 1, other))
    for made in handed + direct + across + out_across:
        made.wait_send()
    for made in out_direct + onward:
        made.wait()
    if cargo is not None:
        cargo.wait()


def turn(parts, rows, gain, collective_id, rounded, passed=None, cargo=None):
    _, count, width = parts.shape
    backward = passed is not None
    shapes = [
        jax.ShapeDtypeStruct((4, count, width), bf16),
        jax.ShapeDtypeStruct((count, width), f32),
    ]
    operands = [parts, rows, gain.reshape(1, width)]
    if backward:
        shapes.append(jax.ShapeDtypeStruct((1, width), f32))
        operands.append(passed)
    return comm_call(
        functools.partial(turn_kernel, backward, rounded),
        shapes,
        [
            pltpu.VMEM((2, count, width), bf16),
            pltpu.VMEM((count, width), bf16),
            pltpu.VMEM((count, width), bf16),
        ]
        + [pltpu.SemaphoreType.DMA((6 * PIECES,))] * 2,
        collective_id,
        *operands,
        cargo=cargo,
    )


def plane_gather_kernel(own, out, send, recv):
    core, y, x, tensor = place()
    other = {"section": 1 - core}
    beside = {"tensor": tensor + 1 - 2 * x}
    above = {"tensor": tensor + 2 - 4 * y}
    greet([other, beside, above])
    half = own.shape[0] // 2
    cut = [pl.ds(0, half), pl.ds(half, half)]

    def slot(along_y, along_x):
        return 4 * along_y + 2 * core + along_x

    me = slot(y, x)
    at_x, at_y, at_both = slot(y, 1 - x), slot(1 - y, x), slot(1 - y, 1 - x)

    def copy(src, where, index, device):
        made = remote(src, out.at[where], send.at[index], recv.at[index], device)
        made.start()
        return made

    to_x = [remote(own.at[cut[h]], out.at[me, cut[h]], send.at[h], recv.at[h], beside) for h in (0, 1)]
    to_y = [remote(own.at[cut[h]], out.at[me, cut[h]], send.at[2 + h], recv.at[2 + h], above) for h in (0, 1)]
    to_x[0].start()
    to_y[1].start()
    to_x[1].start()
    to_y[0].start()
    pending = [copy(own, me, 4, other)]
    out[me] = own[...]

    def onward(where, h, index, device):
        made = remote(
            out.at[where, cut[h]], out.at[where, cut[h]], send.at[index], recv.at[index], device
        )
        made.start()
        return made

    to_x[0].wait_recv()
    diag_y = onward(at_x, 0, 5, above)
    pending.append(onward(at_x, 0, 6, other))
    to_y[1].wait_recv()
    diag_x = onward(at_y, 1, 7, beside)
    pending.append(onward(at_y, 1, 8, other))
    to_x[1].wait_recv()
    pending.append(onward(at_x, 1, 9, other))
    to_y[0].wait_recv()
    pending.append(onward(at_y, 0, 10, other))
    diag_y.wait_recv()
    pending.append(onward(at_both, 0, 11, other))
    diag_x.wait_recv()
    pending.append(onward(at_both, 1, 12, other))
    for made in to_x + to_y + [diag_x, diag_y]:
        made.wait_send()
    for made in pending:
        made.wait()


def plane_gather(block, collective_id):
    count, width = block.shape
    return comm_call(
        plane_gather_kernel,
        jax.ShapeDtypeStruct((8, count, width), block.dtype),
        [pltpu.SemaphoreType.DMA((13,))] * 2,
        collective_id,
        block,
    )


def plane_reduce_kernel(parts, out, near, mixed, via_x, via_y, from_x, from_y, hop_x, hop_y, send, recv):
    core, y, x, tensor = place()
    other = {"section": 1 - core}
    beside = {"tensor": tensor + 1 - 2 * x}
    above = {"tensor": tensor + 2 - 4 * y}
    greet([other, beside, above])
    half = out.shape[0] // 2
    cut = [pl.ds(0, half), pl.ds(half, half)]

    def slot(at_core, along_y, along_x):
        return 4 * along_y + 2 * at_core + along_x

    targets = [(1 - y, 1 - x), (y, 1 - x), (1 - y, x), (y, x)]
    handed = []
    for index, (along_y, along_x) in enumerate(targets):
        made = remote(
            parts.at[slot(1 - core, along_y, along_x)],
            near.at[index],
            send.at[index],
            recv.at[index],
            other,
        )
        made.start()
        handed.append(made)

    def joined(index, where=slice(None)):
        along_y, along_x = targets[index]
        mine = parts[slot(core, along_y, along_x), where]
        return mine.astype(f32) + near[index, where].astype(f32)

    def start(src, dst, index, device):
        made = remote(src, dst, send.at[index], recv.at[index], device)
        made.start()
        return made

    handed[0].wait_recv()
    mixed[0] = joined(0).astype(bf16)
    diag_x = start(mixed.at[0, cut[0]], via_x, 4, beside)
    diag_y = start(mixed.at[0, cut[1]], via_y, 5, above)
    handed[1].wait_recv()
    mixed[1] = joined(1).astype(bf16)
    straight_x = start(mixed.at[1, cut[0]], from_x.at[cut[0]], 6, beside)
    handed[2].wait_recv()
    mixed[2] = joined(2).astype(bf16)
    straight_y = start(mixed.at[2, cut[1]], from_y.at[cut[1]], 7, above)
    diag_x.wait_recv()
    hop_y[...] = (mixed[2, cut[0]].astype(f32) + via_x[...].astype(f32)).astype(bf16)
    turned_y = start(hop_y, from_y.at[cut[0]], 8, above)
    diag_y.wait_recv()
    hop_x[...] = (mixed[1, cut[1]].astype(f32) + via_y[...].astype(f32)).astype(bf16)
    turned_x = start(hop_x, from_x.at[cut[1]], 9, beside)
    handed[3].wait_recv()
    straight_x.wait_recv()
    turned_y.wait_recv()
    out[cut[0]] = joined(3, cut[0]) + from_x[cut[0]].astype(f32) + from_y[cut[0]].astype(f32)
    straight_y.wait_recv()
    turned_x.wait_recv()
    out[cut[1]] = joined(3, cut[1]) + from_x[cut[1]].astype(f32) + from_y[cut[1]].astype(f32)
    for made in handed + [diag_x, diag_y, straight_x, straight_y, turned_x, turned_y]:
        made.wait_send()


def plane_reduce(parts, collective_id):
    _, count, width = parts.shape
    half = count // 2
    return comm_call(
        plane_reduce_kernel,
        jax.ShapeDtypeStruct((count, width), f32),
        [
            pltpu.VMEM((4, count, width), bf16),
            pltpu.VMEM((3, count, width), bf16),
            pltpu.VMEM((half, width), bf16),
            pltpu.VMEM((half, width), bf16),
            pltpu.VMEM((count, width), bf16),
            pltpu.VMEM((count, width), bf16),
            pltpu.VMEM((half, width), bf16),
            pltpu.VMEM((half, width), bf16),
        ]
        + [pltpu.SemaphoreType.DMA((10,))] * 2,
        collective_id,
        parts,
    )


def batch_gather_kernel(count, *refs):
    kinds = (len(refs) - 2) // 2
    ins, outs, (send, recv) = refs[:kinds], refs[kinds : 2 * kinds], refs[2 * kinds :]
    me = lax.axis_index("batch")
    peers = [{"batch": lax.rem(me + step, count)} for step in range(1, count)]
    greet(peers)
    copies = []
    for index, peer in enumerate(peers):
        for kind in range(kinds):
            at = index * kinds + kind
            copies.append(remote(ins[kind], outs[kind].at[me], send.at[at], recv.at[at], peer))
            copies[-1].start()
    for kind in range(kinds):
        outs[kind][me] = ins[kind][...]
    for copy in copies:
        copy.wait()


def batch_gather(blocks, collective_id):
    count = lax.axis_size("batch")
    return comm_call(
        functools.partial(batch_gather_kernel, count),
        [jax.ShapeDtypeStruct((count,) + block.shape, block.dtype) for block in blocks],
        [pltpu.SemaphoreType.DMA(((count - 1) * len(blocks),))] * 2,
        collective_id,
        *blocks,
    )


def batch_trade_kernel(count, parts, out, send, recv):
    me = lax.axis_index("batch")
    peers = [lax.rem(me + step, count) for step in range(1, count)]
    greet([{"batch": peer} for peer in peers])
    copies = []
    for index, peer in enumerate(peers):
        copies.append(
            remote(parts.at[peer], out.at[me], send.at[index], recv.at[index], {"batch": peer})
        )
        copies[-1].start()
    out[me] = parts[me]
    for copy in copies:
        copy.wait()


def batch_trade(parts):
    count = parts.shape[0]
    return comm_call(
        functools.partial(batch_trade_kernel, count),
        jax.ShapeDtypeStruct(parts.shape, parts.dtype),
        [pltpu.SemaphoreType.DMA((count - 1,))] * 2,
        8,
        parts,
    )


def causal_mix(projected, taps):
    once = jnp.pad(projected, ((1, 0), (0, 0)))[:-1]
    twice = jnp.pad(projected, ((2, 0), (0, 0)))[:-2]
    return taps[0] * projected + taps[1] * once + taps[2] * twice


def causal_mix_back(grad, projected, taps):
    ahead_one = jnp.pad(grad, ((0, 1), (0, 0)))[1:]
    ahead_two = jnp.pad(grad, ((0, 2), (0, 0)))[2:]
    grad_in = taps[0] * grad + taps[1] * ahead_one + taps[2] * ahead_two
    once = jnp.pad(projected, ((1, 0), (0, 0)))[:-1]
    twice = jnp.pad(projected, ((2, 0), (0, 0)))[:-2]
    grad_taps = [
        jnp.sum(grad * projected, 0),
        jnp.sum(grad * once, 0),
        jnp.sum(grad * twice, 0),
    ]
    return (grad_in, grad_taps)


def allowed_keys(lead, reach, length):
    query_at = jnp.arange(lead, reach)[:, None]
    key_at = jnp.arange(reach)[None, :]
    return (key_at <= query_at) & (key_at < length)


def attend(queries, keys_all, values_all, length):
    total = queries.shape[0]
    block = min(512, total)
    factor = queries.shape[-1] ** (-0.5)
    outputs = []
    totals = []
    for index in range(total // block):
        lead = index * block
        reach = lead + block
        scores = (
            jnp.einsum("qhd,khd->hqk", queries[lead:reach], keys_all[:reach], preferred_element_type=f32)
            * factor
        )
        scores = jnp.where(allowed_keys(lead, reach, length)[None], scores, masked_score)
        peak = jnp.max(scores, axis=-1, keepdims=True)
        raised = jnp.exp(scores - peak)
        weight_sum = jnp.sum(raised, axis=-1, keepdims=True)
        probs = (raised / weight_sum).astype(bf16)
        result = jnp.einsum("hqk,khd->qhd", probs, values_all[:reach], preferred_element_type=f32)
        outputs.append(result.astype(bf16))
        totals.append((peak + jnp.log(weight_sum))[..., 0])
    return (jnp.concatenate(outputs, 0), jnp.concatenate(totals, 1))


def attend_back(grad_out, queries, keys_all, values_all, length, totals):
    total = queries.shape[0]
    block = min(512, total)
    factor = queries.shape[-1] ** (-0.5)
    grad_queries = []
    grad_keys = jnp.zeros(keys_all.shape, f32)
    grad_values = jnp.zeros(values_all.shape, f32)
    for index in range(total // block):
        lead = index * block
        reach = lead + block
        scores = (
            jnp.einsum("qhd,khd->hqk", queries[lead:reach], keys_all[:reach], preferred_element_type=f32)
            * factor
        )
        allowed = allowed_keys(lead, reach, length)[None]
        probs = jnp.where(allowed, jnp.exp(scores - totals[:, lead:reach, None]), 0.0)
        grad_block = grad_out[lead:reach]
        grad_probs = jnp.einsum(
            "qhd,khd->hqk", grad_block, values_all[:reach], preferred_element_type=f32
        )
        inner = jnp.sum(probs * grad_probs, axis=-1, keepdims=True)
        grad_scores = (probs * (grad_probs - inner)).astype(bf16)
        grad_queries.append(
            jnp.einsum("hqk,khd->qhd", grad_scores, keys_all[:reach], preferred_element_type=f32)
            * factor
        )
        grad_keys = grad_keys.at[:reach].add(
            jnp.einsum("hqk,qhd->khd", grad_scores, queries[lead:reach], preferred_element_type=f32)
            * factor
        )
        grad_values = grad_values.at[:reach].add(
            jnp.einsum("hqk,qhd->khd", probs.astype(bf16), grad_block, preferred_element_type=f32)
        )
    return (jnp.concatenate(grad_queries, 0), grad_keys, grad_values)


def attention_forward(gathered, length, weights):
    qkv_mat, taps, out_turned = weights
    local_width = out_turned.shape[1]
    heads_here = local_width // HEAD
    projected = mm(gathered, qkv_mat, 1, 0)
    mixed = causal_mix(projected, taps).astype(bf16)
    triple = mixed.reshape(-1, 3, heads_here, HEAD)
    context, totals = attend(triple[:, 0], triple[:, 1], triple[:, 2], length)
    context = context.reshape(-1, local_width)
    partial = mm(context, out_turned, 1, 1).astype(bf16).reshape(4, -1, D)
    return partial, (gathered, projected, mixed, context, totals)


def attention_backward(grad_rows, length, weights, kept):
    qkv_mat, taps, out_turned = weights
    gathered, projected, mixed, context, totals = kept
    local_width = out_turned.shape[1]
    heads_here = local_width // HEAD
    grad_context = mm(grad_rows, out_turned, 1, 0).astype(bf16).reshape(-1, heads_here, HEAD)
    triple = mixed.reshape(-1, 3, heads_here, HEAD)
    grad_queries, grad_keys, grad_values = attend_back(
        grad_context, triple[:, 0], triple[:, 1], triple[:, 2], length, totals
    )
    grad_mixed = jnp.stack([grad_queries, grad_keys, grad_values], 1).reshape(-1, 3 * local_width)
    grad_projected, grad_taps = causal_mix_back(grad_mixed, projected, taps)
    grad_projected = grad_projected.astype(bf16)
    partial = mm(grad_projected, qkv_mat, 1, 1).astype(bf16).reshape(4, -1, D)
    grad_qkv = mm(gathered, grad_projected, 0, 0)
    grad_outmat = mm(grad_rows, context, 0, 0)
    blob = jnp.concatenate([grad_qkv.astype(bf16), grad_outmat.astype(bf16)], 1)
    return partial, blob, grad_taps


def ffn_forward(gathered, weights):
    up_mat, down_turned = weights
    hidden = mm(gathered, up_mat, 1, 0)
    active = jnp.square(jnp.maximum(hidden, 0.0)).astype(bf16)
    partial = mm(active, down_turned, 1, 1).astype(bf16).reshape(4, -1, D)
    return partial, (gathered, hidden, active)


def ffn_backward(grad_rows, weights, kept):
    up_mat, down_turned = weights
    gathered, hidden, active = kept
    grad_active = mm(grad_rows, down_turned, 1, 0)
    grad_hidden = (grad_active * 2.0 * jnp.maximum(hidden, 0.0)).astype(bf16)
    partial = mm(grad_hidden, up_mat, 1, 1).astype(bf16).reshape(4, -1, D)
    grad_down = mm(grad_rows, active, 0, 0)
    grad_up = mm(gathered, grad_hidden, 0, 0)
    blob = jnp.concatenate([grad_up.astype(bf16), grad_down.astype(bf16)], 1)
    return partial, blob


LOOK = 512


def lookup_kernel(ids, table, out):
    total = jnp.zeros((table.shape[0], ids.shape[2]), f32)
    wanted = ids[0]
    row = lax.broadcasted_iota(jnp.int32, (LOOK, ids.shape[2]), 0)
    for lead in range(0, table.shape[1], LOOK):
        hit = jnp.where(row == wanted - lead, 1.0, 0.0).astype(bf16)
        total += jnp.dot(table[:, lead : lead + LOOK], hit, preferred_element_type=f32)
    out[0, 0] = total.astype(bf16)


def lookup(table, ids):
    batches, parts, _, slots = ids.shape
    depth, vocab_rows = table.shape
    return pl.pallas_call(
        lookup_kernel,
        grid=(batches * parts,),
        out_shape=jax.ShapeDtypeStruct((parts, batches, depth, slots), bf16),
        in_specs=[
            pl.BlockSpec((1, 1, slots), lambda at: (at, 0, 0)),
            pl.BlockSpec((depth, vocab_rows), lambda at: (0, 0)),
        ],
        out_specs=pl.BlockSpec((1, 1, depth, slots), lambda at: (at % parts, at // parts, 0, 0)),
        compiler_params=pltpu.CompilerParams(vmem_limit_bytes=40 << 20),
    )(ids.reshape(batches * parts, 1, slots), table)


def spread_kernel(batches, ids, grads, base, out):
    at = pl.program_id(0)
    columns = out.shape[1]
    slots = ids.shape[2]
    row = lax.broadcasted_iota(jnp.int32, (columns, slots), 0) + at * columns

    def step(index, total):
        for part in range(8):
            hit = jnp.where(row == ids[index * 8 + part], 1.0, 0.0).astype(bf16)
            total += mm(grads[part, index], hit, 1, 1)
        return total

    out[...] = lax.fori_loop(0, batches, step, base[...].astype(f32))


def spread(grads, ids, base):
    parts, batches, depth, slots = grads.shape
    vocab_rows = base.shape[1]
    columns = 512
    return pl.pallas_call(
        functools.partial(spread_kernel, batches),
        grid=(vocab_rows // columns,),
        out_shape=jax.ShapeDtypeStruct((depth, vocab_rows), f32),
        in_specs=[
            pl.BlockSpec((batches * parts, 1, slots), lambda at: (0, 0, 0)),
            pl.BlockSpec((parts, batches, depth, slots), lambda at: (0, 0, 0, 0)),
            pl.BlockSpec((depth, columns), lambda at: (0, at)),
        ],
        out_specs=pl.BlockSpec((depth, columns), lambda at: (0, at)),
        compiler_params=pltpu.CompilerParams(vmem_limit_bytes=40 << 20),
    )(ids.reshape(batches * parts, 1, slots), grads, base)


def summed(landed):
    one, two = landed
    return (one.astype(f32) + two.astype(f32)).astype(bf16)


def over_batch(block):
    return lax.psum_scatter(block, "batch", scatter_dimension=0, tiled=False)


def tie(*values):
    return lax.optimization_barrier(values)


def on_device(
    token_ids,
    seq_lengths,
    embed_table,
    norm_gains,
    final_gain,
    qkv_weight,
    qkv_conv,
    out_weight,
    up_weight,
    down_weight,
    logit_grad,
):
    section = lax.axis_index("section")
    first = section == 0
    core, seq_at, x_at, _ = place()
    quarter = 2 * core + x_at
    me = lax.axis_index("tensor")
    at_batch = lax.axis_index("batch")
    tensor_count = lax.axis_size("tensor")
    batch_count = lax.axis_size("batch")
    section_count = lax.axis_size("section")
    slot_length = token_ids.shape[1]
    shard_rows = slot_length // tensor_count
    local_width = out_weight.shape[1]
    heads_here = local_width // HEAD
    hidden_width = up_weight.shape[2]
    root_scale = math.sqrt(D)
    depth = D // batch_count
    length = seq_lengths[seq_at]
    sequences = token_ids.shape[0]

    table_own = embed_table.astype(bf16).T
    attn_own = jnp.concatenate(
        [
            qkv_weight[0].reshape(depth, 3 * local_width).astype(bf16),
            out_weight[0].astype(bf16).T,
        ],
        1,
    )
    ffn_own = jnp.concatenate([up_weight[0].astype(bf16), down_weight[0].astype(bf16).T], 1)
    attn_all = lax.all_gather(attn_own, "batch", axis=0, tiled=True)
    ffn_all = lax.all_gather(ffn_own, "batch", axis=0, tiled=True)
    table_turned = lax.all_gather(table_own, "batch", axis=0, tiled=True)

    gain_width = final_gain.shape[0]
    small = jnp.concatenate(
        [norm_gains.astype(f32).reshape(-1), final_gain.astype(f32), qkv_conv.astype(f32).reshape(-1)]
    )
    small_rows = -(-small.shape[0] // 1024) * 8
    small = jnp.pad(small, (0, small_rows * 128 - small.shape[0])).reshape(small_rows, 128)
    all_ids, small = batch_gather([token_ids.reshape(-1, 128), small], 5)
    small = plane_gather(small.reshape(batch_count * small_rows, 128), 6)
    small = small.reshape(2, 2, 2, batch_count, -1).transpose(1, 3, 0, 2, 4)
    small = small.reshape(section_count, batch_count, tensor_count, -1).astype(bf16).astype(f32)
    gains_all = small[..., : 5 * gain_width].reshape(-1, 5, gain_width)
    gains_all = gains_all.transpose(1, 0, 2).reshape(5, D)
    taps_size = qkv_conv.size
    taps_all = small[..., 5 * gain_width : 5 * gain_width + taps_size].reshape(
        section_count, batch_count, tensor_count, 3, 3, heads_here, -1
    )
    taps_here = lax.dynamic_index_in_dim(taps_all, quarter, 2, keepdims=False)
    taps_here = taps_here.transpose(0, 3, 2, 4, 1, 5).reshape(section_count, 3, 3 * local_width)
    final_scale = gains_all[4]

    vocab_rows = embed_table.shape[0]
    owner_start = (section * tensor_count + me) * vocab_rows
    local_ids = all_ids.reshape(batch_count, sequences * 4, 1, shard_rows) - owner_start
    picked = lookup(table_own, local_ids)
    total = plane_reduce(picked.reshape(8, D, shard_rows), 3).astype(bf16)
    embedded = batch_trade(total.reshape(batch_count, depth, shard_rows))
    embedded = embedded.reshape(D, shard_rows).T

    def attn_weights(block, layer):
        return block[:, : 3 * local_width], taps_here[layer], block[:, 3 * local_width :]

    def ffn_weights(block):
        return block[:, :hidden_width], block[:, hidden_width:]

    first_rows = embedded.astype(f32) * root_scale
    normed = (first_rows * norm_factor(first_rows) * gains_all[0]).astype(bf16)
    gathered, block = group_gather(normed, 1, cargo=("out", 0, attn_all))
    attn_first = attn_weights(block, 0)
    partial, attn_kept_first = attention_forward(gathered.reshape(-1, D), length, attn_first)
    gathered, first_middle, block = turn(
        partial, first_rows, gains_all[1], 20, False, cargo=("out", 0, ffn_all)
    )
    ffn_first = ffn_weights(block)
    partial, ffn_kept_first = ffn_forward(gathered.reshape(-1, D), ffn_first)
    gathered, second_rows, block = turn(
        partial, first_middle, gains_all[2], 21, True, cargo=("out", 1, attn_all)
    )
    attn_second = attn_weights(block, 1)
    partial, attn_kept_second = attention_forward(gathered.reshape(-1, D), length, attn_second)
    gathered, second_middle, block = turn(
        partial, second_rows, gains_all[3], 24, False, cargo=("out", 1, ffn_all)
    )
    ffn_second = ffn_weights(block)
    partial, ffn_kept_second = ffn_forward(gathered.reshape(-1, D), ffn_second)

    def halves(blob):
        return blob.reshape(batch_count, 2, depth // 2, blob.shape[1])

    grad_both = mm(logit_grad.reshape(-1, vocab_rows), table_turned, 1, 1).astype(bf16)
    grad_final = plane_reduce(grad_both.reshape(8, shard_rows, D), 4)
    own_at = quarter * shard_rows + jnp.arange(shard_rows)
    grad_final = jnp.where((own_at < length)[:, None], grad_final, 0.0)

    partial, grad_final = tie(partial, grad_final)
    final_rows = (second_middle + group_reduce(partial, 2)).astype(bf16).astype(f32)
    normed_final = (final_rows * norm_factor(final_rows) * final_scale).astype(bf16)
    final_both = plane_gather(normed_final, 7).reshape(-1, D)
    logits = mm(final_both, table_turned, 1, 0).astype(bf16).reshape(sequences, slot_length, -1)
    valid = (jnp.arange(slot_length)[None, :] < seq_lengths[:, None]).reshape(-1, 1)
    masked_final = jnp.where(valid, final_both, jnp.zeros((), bf16))
    head_table = mm(masked_final, logit_grad.reshape(-1, vocab_rows), 0, 0).astype(bf16)
    grad_final, head_table = tie(grad_final, head_table)
    head_done = lax.psum_scatter(head_table, "batch", scatter_dimension=0, tiled=True)

    grad_rows, grad_final_gain = norm_back(grad_final, final_rows, final_scale)
    gathered = group_gather(grad_rows.astype(bf16), 13).reshape(-1, D)
    partial, blob = ffn_backward(gathered, ffn_second, ffn_kept_second)
    gathered, grad_rows, gain_2f, *landed = turn(
        partial, second_middle, gains_all[3], 22, False, passed=grad_rows,
        cargo=("in", 1, halves(blob)),
    )
    ffn_second_sum = summed(landed)
    partial, blob, taps_second = attention_backward(
        gathered.reshape(-1, D), length, attn_second, attn_kept_second
    )
    gathered, grad_rows, gain_2a, *landed = turn(
        partial, second_rows, gains_all[2], 23, True, passed=grad_rows,
        cargo=("in", 1, halves(blob)),
    )
    attn_second_sum = summed(landed)
    partial, blob = ffn_backward(gathered.reshape(-1, D), ffn_first, ffn_kept_first)
    gathered, grad_rows, gain_1f, *landed = turn(
        partial, first_middle, gains_all[1], 25, False, passed=grad_rows,
        cargo=("in", 0, halves(blob)),
    )
    ffn_first_sum = summed(landed)
    partial, blob, taps_first = attention_backward(
        gathered.reshape(-1, D), length, attn_first, attn_kept_first
    )
    partial, head_done = tie(partial, head_done)
    ffn_second_done, attn_second_done = over_batch(ffn_second_sum), over_batch(attn_second_sum)
    grad_norm, *landed = group_reduce(partial, 14, cargo=("in", 0, halves(blob)))
    attn_first_sum = summed(landed)
    grad_norm, gain_1a = norm_back(grad_norm, first_rows, gains_all[0])
    grad_rows = grad_rows + grad_norm
    grad_rows, ffn_second_done, attn_second_done = tie(
        grad_rows, ffn_second_done, attn_second_done
    )
    ffn_first_done, attn_first_done = over_batch(ffn_first_sum), over_batch(attn_first_sum)

    def placed(first_part, second_part):
        keep = jnp.where(first, first_part, second_part)
        got = lax.ppermute(jnp.where(first, second_part, first_part), "section", [(0, 1), (1, 0)])
        return jnp.where(
            first, jnp.concatenate([keep, got], 0), jnp.concatenate([got, keep], 0)
        ).astype(f32)

    attn_done = placed(attn_first_done, attn_second_done)
    ffn_done = placed(ffn_first_done, ffn_second_done)
    qkv_done = attn_done[:, : 3 * local_width].reshape(1, depth, 3, local_width)
    out_done = attn_done[:, 3 * local_width :].T[None]
    up_done = ffn_done[:, :hidden_width][None]
    down_done = ffn_done[:, hidden_width:].T[None]

    embed_grad = (grad_rows * root_scale).astype(bf16).T
    traded = batch_trade(embed_grad.reshape(batch_count, depth, shard_rows))
    every = plane_gather(traded.reshape(D, shard_rows), 10)
    every = every.reshape(8, batch_count, depth, shard_rows)
    table_done = spread(every, local_ids, head_done).T

    def row_at(index, vector):
        padded = jnp.pad(vector, (0, D - vector.shape[0]))[None]
        return jnp.where(jnp.arange(16)[:, None] == index, padded, 0.0)

    vectors = [gain_1a, gain_1f[0], gain_2a[0], gain_2f[0], grad_final_gain, *taps_first, *taps_second]
    rows = sum(row_at(index, vector) for index, vector in enumerate(vectors))
    rows = plane_gather(rows, 11)
    gain_sums = jnp.sum(rows[:, :5], 0)
    holders = rows.reshape(2, 4, 16, D)[:, :, 5:11].reshape(2, 4, 2, 3, D)
    taps_sums = jnp.sum(lax.dynamic_index_in_dim(holders, me, 1, keepdims=False), 0)
    taps_sums = lax.dynamic_index_in_dim(taps_sums, section, 0, keepdims=False)
    sums = jnp.pad(jnp.concatenate([gain_sums, taps_sums]), ((0, 0), (0, 0)))
    sums = batch_gather([sums], 12)
    sums = jnp.sum(sums, 0)
    whole_at = (section * batch_count + at_batch) * tensor_count + me
    gain_part = lax.dynamic_slice_in_dim(sums[:5], whole_at * gain_width, gain_width, 1)
    gains_done = gain_part[:4].reshape(2, 2, gain_width)
    final_done = gain_part[4]
    conv_part = sums[5:8, : 3 * local_width].reshape(3, 3, heads_here, HEAD).transpose(1, 0, 2, 3)
    conv_done = lax.dynamic_slice_in_dim(
        conv_part, at_batch * qkv_conv.shape[4], qkv_conv.shape[4], 3
    )[None]
    return (
        logits,
        table_done,
        gains_done,
        final_done,
        qkv_done,
        conv_done,
        out_done,
        up_done,
        down_done,
    )


def solution(mesh):
    in_specs = (
        P("batch", None),
        P("batch"),
        P(("section", "tensor"), "batch"),
        P(None, None, ("section", "batch", "tensor")),
        P(("section", "batch", "tensor")),
        P("section", "batch", None, "tensor"),
        P("section", None, None, "tensor", "batch"),
        P("section", "tensor", "batch"),
        P("section", "batch", "tensor"),
        P("section", "tensor", "batch"),
        P("batch", None, ("section", "tensor")),
    )
    out_specs = (
        P("batch", None, ("section", "tensor")),
        P(("section", "tensor"), "batch"),
        P(None, None, ("section", "batch", "tensor")),
        P(("section", "batch", "tensor")),
        P("section", "batch", None, "tensor"),
        P("section", None, None, "tensor", "batch"),
        P("section", "tensor", "batch"),
        P("section", "batch", "tensor"),
        P("section", "tensor", "batch"),
    )
    return jax.shard_map(
        on_device, mesh=mesh, in_specs=in_specs, out_specs=out_specs, check_vma=False
    )
```

```python
import functools
import math

import jax
import jax.numpy as jnp
from jax import lax
from jax.experimental import pallas as pl
from jax.experimental.pallas import tpu as pltpu
from jax.sharding import PartitionSpec as P

D = 768
HEAD = 64

norm_eps = 1e-06
masked_score = -1e30
bf16 = jnp.bfloat16
f32 = jnp.float32


def mm(left, right, left_dim, right_dim):
    return lax.dot_general(
        left, right, (((left_dim,), (right_dim,)), ((), ())), preferred_element_type=f32
    )


def norm_factor(rows):
    return lax.rsqrt(jnp.mean(rows * rows, axis=-1, keepdims=True) + norm_eps)


def norm_back(grad, rows, gain):
    factor = norm_factor(rows)
    scaled = grad * gain
    inner = jnp.mean(scaled * rows, axis=-1, keepdims=True)
    grad_rows = factor * scaled - rows * (factor * factor * factor * inner)
    return grad_rows, jnp.sum(grad * rows * factor, axis=0)


MESH = pl.DeviceIdType.MESH


def place():
    core = lax.axis_index("section")
    tensor = lax.axis_index("tensor")
    return core, tensor // 2, tensor % 2, tensor


def remote(src, dst, send, recv, device):
    return pltpu.make_async_remote_copy(
        src_ref=src,
        dst_ref=dst,
        send_sem=send,
        recv_sem=recv,
        device_id=device,
        device_id_type=MESH,
    )


def greet(devices):
    barrier = pltpu.get_barrier_semaphore()
    for device in devices:
        pl.semaphore_signal(barrier, inc=1, device_id=device, device_id_type=MESH)
    pl.semaphore_wait(barrier, len(devices))


def comm_call(body, out_shape, scratch, collective_id, *operands, cargo=None):
    shapes = list(out_shape) if isinstance(out_shape, (list, tuple)) else [out_shape]
    in_specs = [pl.BlockSpec(memory_space=pltpu.VMEM)] * len(operands)
    out_specs = [pl.BlockSpec(memory_space=pltpu.VMEM)] * len(shapes)
    scratch = list(scratch)
    count_in, count_out = len(operands), len(shapes)
    loads = 0
    if cargo is not None:
        kind, layer, arrays = cargo
        loads = len(arrays)
        operands = operands + tuple(arrays)
        in_specs += [pl.BlockSpec(memory_space=pl.ANY)] * loads
        landing = []
        for array in arrays:
            if kind == "out":
                landing.append(jax.ShapeDtypeStruct(array.shape, array.dtype))
            else:
                batches, _, rows, width = array.shape
                landing += [jax.ShapeDtypeStruct((batches, rows, width), array.dtype)] * 2
        shapes += landing
        out_specs += [pl.BlockSpec(memory_space=pl.ANY)] * len(landing)
        scratch += [pltpu.SemaphoreType.DMA((loads, 3))] * 2

    def kernel(*refs):
        ins, rest = refs[: len(operands)], refs[len(operands) :]
        outs, rest = rest[: len(shapes)], rest[len(shapes) :]
        if cargo is None:
            body(*ins, *outs, *rest)
            return
        send, recv = rest[-2:]
        made = Outward if kind == "out" else Inward
        lands = len(landing) // loads

        def load():
            return [
                made(
                    layer,
                    ins[count_in + at],
                    outs[count_out + lands * at : count_out + lands * (at + 1)],
                    send.at[at],
                    recv.at[at],
                )
                for at in range(loads)
            ]

        body(*ins[:count_in], *outs[:count_out], *rest[:-2], load=load)

    results = pl.pallas_call(
        kernel,
        out_shape=shapes,
        in_specs=in_specs,
        out_specs=out_specs,
        scratch_shapes=scratch,
        compiler_params=pltpu.CompilerParams(
            collective_id=collective_id, has_side_effects=True, vmem_limit_bytes=40 << 20
        ),
    )(*operands)
    return results if len(shapes) > 1 else results[0]


class Outward:
    def __init__(self, layer, source, landing, send, recv):
        core, y, _, tensor = place()
        target = landing[0]
        self.layer, self.core, self.y = layer, core, y
        self.near = remote(source, target, send.at[0], recv.at[0], {"section": 1 - core})
        self.far = remote(
            source, target, send.at[1], recv.at[0], {"section": y, "tensor": tensor + 2 - 4 * y}
        )
        self.local = pltpu.make_async_copy(source, target, recv.at[1])

    def start(self):
        @pl.when(self.core == self.layer)
        def _():
            self.far.start()

            @pl.when(self.y == self.layer)
            def _():
                self.local.start()

            @pl.when(self.y != self.layer)
            def _():
                self.near.start()

    def wait(self):
        stays = (self.core == self.layer) & (self.y == self.layer)

        @pl.when(stays)
        def _():
            self.local.wait()

        @pl.when(jnp.logical_not(stays))
        def _():
            self.far.wait_recv()

        @pl.when(self.core == self.layer)
        def _():
            self.far.wait_send()

            @pl.when(self.y != self.layer)
            def _():
                self.near.wait_send()


class Inward:
    def __init__(self, layer, source, landing, send, recv):
        core, y, _, tensor = place()
        above = tensor + 2 - 4 * y
        self.near = core == y
        self.to_core = remote(
            source.at[:, 1 - y], landing[0], send.at[0], recv.at[0], {"section": 1 - core}
        )
        self.to_same = remote(
            source.at[:, 1 - y], landing[0], send.at[0], recv.at[0], {"tensor": above}
        )
        self.to_both = remote(
            source.at[:, y],
            landing[1],
            send.at[1],
            recv.at[1],
            {"section": 1 - core, "tensor": above},
        )
        self.fill = pltpu.make_async_copy(source.at[:, y], landing[1], recv.at[2])

    def start(self):
        @pl.when(self.near)
        def _():
            self.to_core.start()
            self.fill.start()

        @pl.when(jnp.logical_not(self.near))
        def _():
            self.to_same.start()
            self.to_both.start()

    def wait(self):
        @pl.when(self.near)
        def _():
            self.to_same.wait_recv()
            self.fill.wait()
            self.to_core.wait_send()

        @pl.when(jnp.logical_not(self.near))
        def _():
            self.to_core.wait_recv()
            self.to_both.wait_recv()
            self.to_same.wait_send()
            self.to_both.wait_send()


def greet_group(other, beside, load):
    if load is None:
        greet([other, beside])
        return []
    _, y, _, tensor = place()
    above = tensor + 2 - 4 * y
    greet([other, beside, {"section": 0, "tensor": above}, {"section": 1, "tensor": above}])
    made = load()
    for one in made:
        one.start()
    return made


PIECES = 4


def group_gather_kernel(own, out, send, recv, load=None):
    core, _, x, tensor = place()
    other = {"section": 1 - core}
    beside = {"tensor": tensor + 1 - 2 * x}
    here = 2 * core + x
    there = 2 * core + 1 - x
    cargo = greet_group(other, beside, load)
    piece = own.shape[0] // PIECES
    cuts = [pl.ds(at * piece, piece) for at in range(PIECES)]
    across = []
    for at, cut in enumerate(cuts):
        copy = remote(own.at[cut], out.at[here, cut], send.at[at], recv.at[at], beside)
        copy.start()
        across.append(copy)
    last = 2 * PIECES
    direct = remote(own, out.at[here], send.at[last], recv.at[last], other)
    direct.start()
    out[here] = own[...]
    passed = []
    for at, cut in enumerate(cuts):
        across[at].wait_recv()
        copy = remote(
            out.at[there, cut],
            out.at[there, cut],
            send.at[PIECES + at],
            recv.at[PIECES + at],
            other,
        )
        copy.start()
        passed.append(copy)
    for copy in across:
        copy.wait_send()
    direct.wait()
    for copy in passed:
        copy.wait()
    for one in cargo:
        one.wait()


def group_gather(rows, collective_id, cargo=None):
    count, width = rows.shape
    return comm_call(
        group_gather_kernel,
        jax.ShapeDtypeStruct((4, count, width), rows.dtype),
        [pltpu.SemaphoreType.DMA((2 * PIECES + 1,))] * 2,
        collective_id,
        rows,
        cargo=cargo,
    )


def group_reduce_kernel(parts, out, near, far, mixed, send, recv, load=None):
    core, _, x, tensor = place()
    other = {"section": 1 - core}
    beside = {"tensor": tensor + 1 - 2 * x}
    here = 2 * core + x
    there = 2 * core + 1 - x
    over_here = 2 * (1 - core) + x
    over_there = 2 * (1 - core) + 1 - x
    cargo = greet_group(other, beside, load)
    piece = out.shape[0] // PIECES
    cuts = [pl.ds(at * piece, piece) for at in range(PIECES)]
    first = []
    for at, cut in enumerate(cuts):
        copy = remote(
            parts.at[over_there, cut], near.at[1, cut], send.at[at], recv.at[at], other
        )
        copy.start()
        first.append(copy)
    last = 2 * PIECES
    direct = remote(parts.at[over_here], near.at[0], send.at[last], recv.at[last], other)
    direct.start()
    across = []
    for at, cut in enumerate(cuts):
        first[at].wait_recv()
        mixed[cut] = (parts[there, cut].astype(f32) + near[1, cut].astype(f32)).astype(bf16)
        copy = remote(
            mixed.at[cut], far.at[cut], send.at[PIECES + at], recv.at[PIECES + at], beside
        )
        copy.start()
        across.append(copy)
    direct.wait()
    for at, cut in enumerate(cuts):
        across[at].wait_recv()
        out[cut] = (
            parts[here, cut].astype(f32) + near[0, cut].astype(f32) + far[cut].astype(f32)
        )
    for copy in first + across:
        copy.wait_send()
    for one in cargo:
        one.wait()


def group_reduce(parts, collective_id, cargo=None):
    parts = parts.reshape(4, -1, D)
    _, count, width = parts.shape
    return comm_call(
        group_reduce_kernel,
        jax.ShapeDtypeStruct((count, width), f32),
        [
            pltpu.VMEM((2, count, width), bf16),
            pltpu.VMEM((count, width), bf16),
            pltpu.VMEM((count, width), bf16),
        ]
        + [pltpu.SemaphoreType.DMA((2 * PIECES + 1,))] * 2,
        collective_id,
        parts,
        cargo=cargo,
    )


def turn_kernel(backward, rounded, *refs, load=None):
    if backward:
        parts, rows, gain, passed, gathered, fresh, gain_grad, near, far, mixed, send, recv = refs
    else:
        parts, rows, gain, gathered, fresh, near, far, mixed, send, recv = refs
    core, _, x, tensor = place()
    other = {"section": 1 - core}
    beside = {"tensor": tensor + 1 - 2 * x}
    here = 2 * core + x
    there = 2 * core + 1 - x
    over_here = 2 * (1 - core) + x
    over_there = 2 * (1 - core) + 1 - x
    cargo = greet_group(other, beside, load)
    piece = fresh.shape[0] // PIECES
    cuts = [pl.ds(at * piece, piece) for at in range(PIECES)]

    def start(src, dst, kind, at, device):
        index = kind * PIECES + at
        made = remote(src, dst, send.at[index], recv.at[index], device)
        made.start()
        return made

    handed, direct = [], []
    for at, cut in enumerate(cuts):
        handed.append(start(parts.at[over_there, cut], near.at[1, cut], 0, at, other))
        direct.append(start(parts.at[over_here, cut], near.at[0, cut], 1, at, other))
    across = []
    for at, cut in enumerate(cuts):
        handed[at].wait_recv()
        mixed[cut] = (parts[there, cut].astype(f32) + near[1, cut].astype(f32)).astype(bf16)
        across.append(start(mixed.at[cut], far.at[cut], 2, at, beside))
    out_across, out_direct, onward = [], [], []
    gains = gain[...]
    for at in range(PIECES + 1):
        if at < PIECES:
            cut = cuts[at]
            direct[at].wait_recv()
            across[at].wait_recv()
            total = (
                parts[here, cut].astype(f32) + near[0, cut].astype(f32) + far[cut].astype(f32)
            )
            held = rows[cut]
            if backward:
                factor = norm_factor(held)
                scaled = total * gains
                inner = jnp.mean(scaled * held, axis=-1, keepdims=True)
                new = passed[cut] + factor * scaled - held * (factor * factor * factor * inner)
                gain_part = jnp.sum(total * held * factor, axis=0, keepdims=True)
                gain_grad[...] = gain_part if at == 0 else gain_grad[...] + gain_part
                if rounded:
                    new = new.astype(bf16).astype(f32)
                shown = new.astype(bf16)
            else:
                new = held + total
                if rounded:
                    new = new.astype(bf16).astype(f32)
                shown = (new * norm_factor(new) * gains).astype(bf16)
            fresh[cut] = new
            gathered[here, cut] = shown
            out_across.append(start(gathered.at[here, cut], gathered.at[here, cut], 3, at, beside))
            out_direct.append(start(gathered.at[here, cut], gathered.at[here, cut], 4, at, other))
        if at >= 1:
            cut = cuts[at - 1]
            out_across[at - 1].wait_recv()
            onward.append(start(gathered.at[there, cut], gathered.at[there, cut], 5, at - 1, other))
    for made in handed + direct + across + out_across:
        made.wait_send()
    for made in out_direct + onward:
        made.wait()
    for one in cargo:
        one.wait()


def turn(parts, rows, gain, collective_id, rounded, passed=None, cargo=None):
    parts = parts.reshape(4, -1, D)
    _, count, width = parts.shape
    backward = passed is not None
    shapes = [
        jax.ShapeDtypeStruct((4, count, width), bf16),
        jax.ShapeDtypeStruct((count, width), f32),
    ]
    operands = [parts, rows, gain.reshape(1, width)]
    if backward:
        shapes.append(jax.ShapeDtypeStruct((1, width), f32))
        operands.append(passed)
    return comm_call(
        functools.partial(turn_kernel, backward, rounded),
        shapes,
        [
            pltpu.VMEM((2, count, width), bf16),
            pltpu.VMEM((count, width), bf16),
            pltpu.VMEM((count, width), bf16),
        ]
        + [pltpu.SemaphoreType.DMA((6 * PIECES,))] * 2,
        collective_id,
        *operands,
        cargo=cargo,
    )


def plane_peers():
    core, y, x, tensor = place()
    return [
        {"section": 1 - core},
        {"tensor": tensor + 1 - 2 * x},
        {"tensor": tensor + 2 - 4 * y},
    ]


def plane_gather_kernel(own, out, send, recv):
    greet(plane_peers())
    plane_exchange(own, out, send, recv)


def plane_exchange(own, out, send, recv):
    core, y, x, _ = place()
    other, beside, above = plane_peers()
    half = own.shape[0] // 2
    cut = [pl.ds(0, half), pl.ds(half, half)]

    def slot(along_y, along_x):
        return 4 * along_y + 2 * core + along_x

    me = slot(y, x)
    at_x, at_y, at_both = slot(y, 1 - x), slot(1 - y, x), slot(1 - y, 1 - x)

    def copy(src, where, index, device):
        made = remote(src, out.at[where], send.at[index], recv.at[index], device)
        made.start()
        return made

    to_x = [remote(own.at[cut[h]], out.at[me, cut[h]], send.at[h], recv.at[h], beside) for h in (0, 1)]
    to_y = [remote(own.at[cut[h]], out.at[me, cut[h]], send.at[2 + h], recv.at[2 + h], above) for h in (0, 1)]
    to_x[0].start()
    to_y[1].start()
    to_x[1].start()
    to_y[0].start()
    pending = [copy(own, me, 4, other)]
    out[me] = own[...]

    def onward(where, h, index, device):
        made = remote(
            out.at[where, cut[h]], out.at[where, cut[h]], send.at[index], recv.at[index], device
        )
        made.start()
        return made

    to_x[0].wait_recv()
    diag_y = onward(at_x, 0, 5, above)
    pending.append(onward(at_x, 0, 6, other))
    to_y[1].wait_recv()
    diag_x = onward(at_y, 1, 7, beside)
    pending.append(onward(at_y, 1, 8, other))
    to_x[1].wait_recv()
    pending.append(onward(at_x, 1, 9, other))
    to_y[0].wait_recv()
    pending.append(onward(at_y, 0, 10, other))
    diag_y.wait_recv()
    pending.append(onward(at_both, 0, 11, other))
    diag_x.wait_recv()
    pending.append(onward(at_both, 1, 12, other))
    for made in to_x + to_y + [diag_x, diag_y]:
        made.wait_send()
    for made in pending:
        made.wait()


def plane_gather(block, collective_id):
    count, width = block.shape
    return comm_call(
        plane_gather_kernel,
        jax.ShapeDtypeStruct((8, count, width), block.dtype),
        [pltpu.SemaphoreType.DMA((13,))] * 2,
        collective_id,
        block,
    )


def plane_reduce_kernel(parts, out, near, mixed, via_x, via_y, from_x, from_y, hop_x, hop_y, send, recv):
    core, y, x, tensor = place()
    other = {"section": 1 - core}
    beside = {"tensor": tensor + 1 - 2 * x}
    above = {"tensor": tensor + 2 - 4 * y}
    greet([other, beside, above])
    half = out.shape[0] // 2
    cut = [pl.ds(0, half), pl.ds(half, half)]

    def slot(at_core, along_y, along_x):
        return 4 * along_y + 2 * at_core + along_x

    targets = [(1 - y, 1 - x), (y, 1 - x), (1 - y, x), (y, x)]
    handed = []
    for index, (along_y, along_x) in enumerate(targets):
        made = remote(
            parts.at[slot(1 - core, along_y, along_x)],
            near.at[index],
            send.at[index],
            recv.at[index],
            other,
        )
        made.start()
        handed.append(made)

    def joined(index, where=slice(None)):
        along_y, along_x = targets[index]
        mine = parts[slot(core, along_y, along_x), where]
        return mine.astype(f32) + near[index, where].astype(f32)

    def start(src, dst, index, device):
        made = remote(src, dst, send.at[index], recv.at[index], device)
        made.start()
        return made

    handed[0].wait_recv()
    mixed[0] = joined(0).astype(bf16)
    diag_x = start(mixed.at[0, cut[0]], via_x, 4, beside)
    diag_y = start(mixed.at[0, cut[1]], via_y, 5, above)
    handed[1].wait_recv()
    mixed[1] = joined(1).astype(bf16)
    straight_x = start(mixed.at[1, cut[0]], from_x.at[cut[0]], 6, beside)
    handed[2].wait_recv()
    mixed[2] = joined(2).astype(bf16)
    straight_y = start(mixed.at[2, cut[1]], from_y.at[cut[1]], 7, above)
    diag_x.wait_recv()
    hop_y[...] = (mixed[2, cut[0]].astype(f32) + via_x[...].astype(f32)).astype(bf16)
    turned_y = start(hop_y, from_y.at[cut[0]], 8, above)
    diag_y.wait_recv()
    hop_x[...] = (mixed[1, cut[1]].astype(f32) + via_y[...].astype(f32)).astype(bf16)
    turned_x = start(hop_x, from_x.at[cut[1]], 9, beside)
    handed[3].wait_recv()
    straight_x.wait_recv()
    turned_y.wait_recv()
    out[cut[0]] = joined(3, cut[0]) + from_x[cut[0]].astype(f32) + from_y[cut[0]].astype(f32)
    straight_y.wait_recv()
    turned_x.wait_recv()
    out[cut[1]] = joined(3, cut[1]) + from_x[cut[1]].astype(f32) + from_y[cut[1]].astype(f32)
    for made in handed + [diag_x, diag_y, straight_x, straight_y, turned_x, turned_y]:
        made.wait_send()


def plane_reduce(parts, collective_id):
    _, count, width = parts.shape
    half = count // 2
    return comm_call(
        plane_reduce_kernel,
        jax.ShapeDtypeStruct((count, width), f32),
        [
            pltpu.VMEM((4, count, width), bf16),
            pltpu.VMEM((3, count, width), bf16),
            pltpu.VMEM((half, width), bf16),
            pltpu.VMEM((half, width), bf16),
            pltpu.VMEM((count, width), bf16),
            pltpu.VMEM((count, width), bf16),
            pltpu.VMEM((half, width), bf16),
            pltpu.VMEM((half, width), bf16),
        ]
        + [pltpu.SemaphoreType.DMA((10,))] * 2,
        collective_id,
        parts,
    )


def batch_peers(count):
    me = lax.axis_index("batch")
    return [{"batch": lax.rem(me + step, count)} for step in range(1, count)]


def batch_exchange(count, ins, outs, send, recv):
    me = lax.axis_index("batch")
    copies = []
    for index, peer in enumerate(batch_peers(count)):
        for kind in range(len(ins)):
            at = index * len(ins) + kind
            copies.append(remote(ins[kind], outs[kind].at[me], send.at[at], recv.at[at], peer))
            copies[-1].start()
    for kind in range(len(ins)):
        outs[kind][me] = ins[kind][...]
    return copies


def batch_gather_kernel(count, *refs):
    kinds = (len(refs) - 2) // 2
    greet(batch_peers(count))
    for copy in batch_exchange(count, refs[:kinds], refs[kinds : 2 * kinds], *refs[2 * kinds :]):
        copy.wait()


def batch_gather(blocks, collective_id):
    count = lax.axis_size("batch")
    return comm_call(
        functools.partial(batch_gather_kernel, count),
        [jax.ShapeDtypeStruct((count,) + block.shape, block.dtype) for block in blocks],
        [pltpu.SemaphoreType.DMA(((count - 1) * len(blocks),))] * 2,
        collective_id,
        *blocks,
    )


def plane_and_batch_kernel(count, own, few, out, few_out, send, recv, few_send, few_recv):
    greet(plane_peers() + batch_peers(count))
    copies = batch_exchange(count, [few], [few_out], few_send, few_recv)
    plane_exchange(own, out, send, recv)
    for copy in copies:
        copy.wait()


def plane_and_batch_gather(block, few, collective_id):
    count = lax.axis_size("batch")
    return comm_call(
        functools.partial(plane_and_batch_kernel, count),
        [
            jax.ShapeDtypeStruct((8,) + block.shape, block.dtype),
            jax.ShapeDtypeStruct((count,) + few.shape, few.dtype),
        ],
        [pltpu.SemaphoreType.DMA((13,))] * 2 + [pltpu.SemaphoreType.DMA((count - 1,))] * 2,
        collective_id,
        block,
        few,
    )


def batch_trade_kernel(count, parts, few, out, few_out, send, recv, few_send, few_recv):
    me = lax.axis_index("batch")
    greet(plane_peers() + batch_peers(count))
    copies = []
    for index, peer in enumerate(batch_peers(count)):
        copies.append(
            remote(parts.at[peer["batch"]], out.at[me], send.at[index], recv.at[index], peer)
        )
        copies[-1].start()
    out[me] = parts[me]
    plane_exchange(few, few_out, few_send, few_recv)
    for copy in copies:
        copy.wait()


def batch_trade(parts, few, collective_id):
    count = parts.shape[0]
    return comm_call(
        functools.partial(batch_trade_kernel, count),
        [
            jax.ShapeDtypeStruct(parts.shape, parts.dtype),
            jax.ShapeDtypeStruct((8,) + few.shape, few.dtype),
        ],
        [pltpu.SemaphoreType.DMA((count - 1,))] * 2 + [pltpu.SemaphoreType.DMA((13,))] * 2,
        collective_id,
        parts,
        few,
    )


ROWS = 256


PACKED = ((0, 0), (0, 1), (1, 0), (1, 1), (2, 0), (2, 1), (0, 2), (1, 2), (2, 2))


def packed(blocks, out):
    cuts = [blocks[:, kind, HEAD * head : HEAD * head + HEAD] for kind, head in PACKED]
    return jnp.concatenate(cuts + [out[:, 2 * HEAD :], out[:, : 2 * HEAD]], 1)


def unpacked(block):
    place_of = {pair: at * HEAD for at, pair in enumerate(PACKED)}
    kinds = []
    for kind in range(3):
        cuts = [
            block[:, place_of[kind, head] : place_of[kind, head] + HEAD] for head in range(3)
        ]
        kinds.append(jnp.concatenate(cuts, 1))
    return jnp.stack(kinds, 1)


def attention_heads(mixed, queries, keys, values):
    low = lax.broadcasted_iota(jnp.int32, (mixed.shape[0], 128), 1) < HEAD
    tile = [mixed[:, 128 * at : 128 * at + 128] for at in range(5)]
    scaled = tile[0] * (HEAD**-0.5)
    queries[0] = jnp.where(low, scaled, 0.0).astype(bf16)
    queries[1] = jnp.where(low, 0.0, scaled).astype(bf16)
    queries[2] = jnp.where(low, tile[3] * (HEAD**-0.5), 0.0).astype(bf16)
    keys[0] = tile[1].astype(bf16)
    keys[1] = pltpu.roll(tile[3], HEAD, 1).astype(bf16)
    values[0] = tile[2].astype(bf16)
    values[1] = tile[4].astype(bf16)


def key_bias(length, total):
    at = lax.broadcasted_iota(jnp.int32, (1, total), 1)
    return jnp.where(at < length, 0.0, masked_score)


def masked(scores, bias, lead):
    scores = scores + bias
    row = lax.broadcasted_iota(jnp.int32, (ROWS, ROWS), 0)
    column = lax.broadcasted_iota(jnp.int32, (ROWS, ROWS), 1)
    last = jnp.where(column <= row, scores[:, lead:], masked_score)
    return last if lead == 0 else jnp.concatenate([scores[:, :lead], last], 1)


def attention_forward_kernel(
    length, x, weight, taps, partial, mixed_out, projected_out, context, totals, projected, queries, keys, values
):
    total = x.shape[0]
    width = 5 * 128
    projected[:8] = jnp.zeros((8, width), f32)
    for lead in range(0, total, ROWS):
        block = jnp.dot(x[lead : lead + ROWS], weight[:, :width], preferred_element_type=f32)
        projected[lead + 8 : lead + 8 + ROWS] = block
        projected_out[lead : lead + ROWS] = block.astype(bf16)
    for lead in range(0, total, ROWS):
        mixed = taps[0:1] * projected[lead + 8 : lead + 8 + ROWS]
        mixed += taps[1:2] * projected[lead + 7 : lead + 7 + ROWS]
        mixed += taps[2:3] * projected[lead + 6 : lead + 6 + ROWS]
        mixed = mixed.astype(bf16)
        mixed_out[lead : lead + ROWS] = mixed
        rows = pl.ds(lead, ROWS)
        attention_heads(
            mixed.astype(f32), queries.at[:, rows], keys.at[:, rows], values.at[:, rows]
        )
    bias = key_bias(length[0], total)
    lane = lax.broadcasted_iota(jnp.int32, (ROWS, 128), 1)
    low = lane < HEAD
    for lead in range(0, total, ROWS):
        reach = lead + ROWS
        found = []
        log_sums = jnp.zeros((ROWS, 128), f32)
        for head in range(3):
            scores = mm(queries[head, lead:reach], keys[head // 2, :reach], 1, 1)
            scores = masked(scores, bias[:, :reach], lead)
            peak = jnp.max(scores, axis=1, keepdims=True)
            raised = jnp.exp(scores - peak)
            weight_sum = jnp.sum(raised, axis=1, keepdims=True)
            probs = (raised * (1.0 / weight_sum)).astype(bf16)
            found.append(
                jnp.dot(probs, values[head // 2, :reach], preferred_element_type=f32)
            )
            log_sums = jnp.where(lane == head, peak + jnp.log(weight_sum), log_sums)
        totals[lead:reach] = log_sums
        joined = jnp.concatenate(
            [
                jnp.where(low, 0.0, pltpu.roll(found[2], HEAD, 1)),
                jnp.where(low, found[0], found[1]),
            ],
            1,
        ).astype(bf16)
        context[lead:reach] = joined
        partial[lead:reach] = mm(joined, weight[:, 512:768], 1, 1).astype(bf16)


def attention_call(body, out_shape, scratch, length, *operands):
    whole = pl.BlockSpec(memory_space=pltpu.VMEM)
    return pl.pallas_call(
        body,
        out_shape=out_shape,
        in_specs=[pl.BlockSpec(memory_space=pltpu.SMEM)] + [whole] * len(operands),
        out_specs=[whole] * len(out_shape),
        scratch_shapes=scratch,
        compiler_params=pltpu.CompilerParams(vmem_limit_bytes=50 << 20),
    )(length.reshape(1), *operands)


def attention_forward(x, length, weight, taps):
    total = x.shape[0]
    partial, *kept = attention_call(
        attention_forward_kernel,
        [
            jax.ShapeDtypeStruct((total, D), bf16),
            jax.ShapeDtypeStruct((total, 640), bf16),
            jax.ShapeDtypeStruct((total, 640), bf16),
            jax.ShapeDtypeStruct((total, 256), bf16),
            jax.ShapeDtypeStruct((total, 128), f32),
        ],
        [
            pltpu.VMEM((total + 8, 640), f32),
            pltpu.VMEM((3, total, 128), bf16),
            pltpu.VMEM((2, total, 128), bf16),
            pltpu.VMEM((2, total, 128), bf16),
        ],
        length,
        x,
        weight,
        taps,
    )
    return partial, (x, *kept)


def attention_backward_kernel(
    length,
    grads,
    x,
    weight,
    taps,
    mixed,
    projected,
    context,
    totals,
    partial,
    weight_grad,
    taps_grad,
    queries,
    keys,
    values,
    outer,
    key_grad,
    value_grad,
    mixed_grad,
    projected_grad,
    turned,
):
    total = x.shape[0]
    width = 5 * 128
    low = lax.broadcasted_iota(jnp.int32, (ROWS, 128), 1) < HEAD
    for lead in range(0, total, ROWS):
        rows = pl.ds(lead, ROWS)
        attention_heads(
            mixed[lead : lead + ROWS].astype(f32),
            queries.at[:, rows],
            keys.at[:, rows],
            values.at[:, rows],
        )
        block = jnp.dot(grads[lead : lead + ROWS], weight[:, 512:768], preferred_element_type=f32)
        third, pair = block[:, :128], block[:, 128:]
        outer[0, lead : lead + ROWS] = jnp.where(low, pair, 0.0).astype(bf16)
        outer[1, lead : lead + ROWS] = jnp.where(low, 0.0, pair).astype(bf16)
        outer[2, lead : lead + ROWS] = jnp.where(low, pltpu.roll(third, HEAD, 1), 0.0).astype(bf16)
    mixed_grad[total:] = jnp.zeros((8, width), f32)
    bias = key_bias(length[0], total)
    for lead in reversed(range(0, total, ROWS)):
        reach = lead + ROWS
        query_grad = []
        for head in range(3):
            its_keys, its_values = keys[head // 2, :reach], values[head // 2, :reach]
            scores = mm(queries[head, lead:reach], its_keys, 1, 1)
            scores = masked(scores, bias[:, :reach], lead)
            probs = jnp.exp(scores - totals[lead:reach, head : head + 1])
            grad_probs = mm(outer[head, lead:reach], its_values, 1, 1)
            product = probs * grad_probs
            inner = jnp.sum(product, axis=1, keepdims=True)
            grad_scores = (product - probs * inner).astype(bf16)
            query_grad.append(jnp.dot(grad_scores, its_keys, preferred_element_type=f32))
            value_part = mm(probs.astype(bf16), outer[head, lead:reach], 0, 0)
            key_part = mm(grad_scores, queries[head, lead:reach], 0, 0)
            if lead + ROWS == total and head != 1:
                value_grad[head // 2] = value_part
                key_grad[head // 2] = key_part
            else:
                value_grad[head // 2, :reach] += value_part
                key_grad[head // 2, :reach] += key_part
        scale = HEAD**-0.5
        mixed_grad[lead:reach, 0:128] = jnp.where(low, query_grad[0], query_grad[1]) * scale
        mixed_grad[lead:reach, 384:512] = query_grad[2] * scale
    grown = jnp.zeros((8, width), f32)
    for lead in reversed(range(0, total, ROWS)):
        reach = lead + ROWS
        mixed_grad[lead:reach, 128:256] = key_grad[0, lead:reach]
        mixed_grad[lead:reach, 256:384] = value_grad[0, lead:reach]
        mixed_grad[lead:reach, 384:512] = jnp.where(
            low, mixed_grad[lead:reach, 384:512], pltpu.roll(key_grad[1, lead:reach], HEAD, 1)
        )
        mixed_grad[lead:reach, 512:640] = value_grad[1, lead:reach]
        here = projected[lead:reach].astype(f32)
        back = jnp.zeros((ROWS, width), f32)
        parts = []
        for tap in range(3):
            ahead = mixed_grad[lead + tap : reach + tap]
            back += taps[tap : tap + 1] * ahead
            parts.append(jnp.sum(ahead * here, axis=0, keepdims=True))
        grown += jnp.concatenate(parts + [jnp.zeros((5, width), f32)], 0)
        back = back.astype(bf16)
        partial[lead:reach] = mm(back, weight[:, :width], 1, 1).astype(bf16)
        projected_grad[lead:reach] = back
    taps_grad[...] = grown
    turned[0] = x[...].T
    turned[1] = grads[...].T
    for lead in range(0, D, ROWS):
        reach = lead + ROWS
        across = jnp.dot(turned[0, lead:reach], projected_grad[...], preferred_element_type=f32)
        outward = jnp.dot(turned[1, lead:reach], context[...], preferred_element_type=f32)
        weight_grad[lead:reach, :512] = across[:, :512].astype(bf16)
        weight_grad[lead:reach, 512:640] = (across[:, 512:] + outward[:, :128]).astype(bf16)
        weight_grad[lead:reach, 640:] = outward[:, 128:].astype(bf16)


def attention_backward(grads, length, weight, taps, kept):
    x, mixed, projected, context, totals = kept
    total = x.shape[0]
    return attention_call(
        attention_backward_kernel,
        [
            jax.ShapeDtypeStruct((total, D), bf16),
            jax.ShapeDtypeStruct((D, 768), bf16),
            jax.ShapeDtypeStruct((8, 640), f32),
        ],
        [
            pltpu.VMEM((3, total, 128), bf16),
            pltpu.VMEM((2, total, 128), bf16),
            pltpu.VMEM((2, total, 128), bf16),
            pltpu.VMEM((3, total, 128), bf16),
            pltpu.VMEM((2, total, 128), f32),
            pltpu.VMEM((2, total, 128), f32),
            pltpu.VMEM((total + 8, 640), f32),
            pltpu.VMEM((total, 640), bf16),
            pltpu.VMEM((2, D, total), bf16),
        ],
        length,
        grads,
        x,
        weight,
        taps,
        mixed,
        projected,
        context,
        totals,
    )


def ffn_forward(gathered, weights):
    up_mat, down_turned = weights
    hidden = mm(gathered, up_mat, 1, 0)
    active = jnp.square(jnp.maximum(hidden, 0.0)).astype(bf16)
    partial = mm(active, down_turned, 1, 1).astype(bf16).reshape(4, -1, D)
    return partial, (gathered, hidden, active)


def ffn_backward(grad_rows, weights, kept):
    up_mat, down_turned = weights
    gathered, hidden, active = kept
    grad_active = mm(grad_rows, down_turned, 1, 0)
    grad_hidden = (grad_active * 2.0 * jnp.maximum(hidden, 0.0)).astype(bf16)
    partial = mm(grad_hidden, up_mat, 1, 1).astype(bf16).reshape(4, -1, D)
    grad_down = mm(grad_rows, active, 0, 0)
    grad_up = mm(gathered, grad_hidden, 0, 0)
    return partial, [grad_up.astype(bf16), grad_down.astype(bf16)]


LOOK = 512


def lookup_kernel(ids, table, out):
    for part in range(ids.shape[0]):
        total = jnp.zeros((table.shape[0], ids.shape[2]), f32)
        wanted = ids[part]
        row = lax.broadcasted_iota(jnp.int32, (LOOK, ids.shape[2]), 0)
        for lead in range(0, table.shape[1], LOOK):
            hit = jnp.where(row == wanted - lead, 1.0, 0.0).astype(bf16)
            total += jnp.dot(table[:, lead : lead + LOOK], hit, preferred_element_type=f32)
        out[part, 0] = total.astype(bf16)


def lookup(table, ids):
    batches, parts, _, slots = ids.shape
    depth, vocab_rows = table.shape
    return pl.pallas_call(
        lookup_kernel,
        grid=(batches,),
        out_shape=jax.ShapeDtypeStruct((parts, batches, depth, slots), bf16),
        in_specs=[
            pl.BlockSpec((parts, 1, slots), lambda at: (at, 0, 0)),
            pl.BlockSpec((depth, vocab_rows), lambda at: (0, 0)),
        ],
        out_specs=pl.BlockSpec((parts, 1, depth, slots), lambda at: (0, at, 0, 0)),
        compiler_params=pltpu.CompilerParams(vmem_limit_bytes=40 << 20),
    )(ids.reshape(batches * parts, 1, slots), table)


def spread_kernel(ids, grads, base, out, wanted):
    at = pl.program_id(0)
    columns = out.shape[1]
    parts, batches, _, slots = grads.shape

    @pl.when(at == 0)
    def _():
        def turned(group, carry):
            across = ids[pl.ds(pl.multiple_of(group * 8, 8), 8)].T
            for part in range(8):
                wanted[group * 8 + part] = jnp.broadcast_to(
                    across[:, part : part + 1], (slots, 128)
                ).astype(jnp.int16)
            return carry

        lax.fori_loop(0, batches * parts // 8, turned, 0)

    lane = lax.broadcasted_iota(jnp.int16, (slots, 128), 1) + (at * columns).astype(jnp.int16)
    together = min(batches, 4)

    def step(index, total):
        for inner in range(together):
            batch = index * together + inner
            for part in range(parts):
                here = wanted[batch * parts + part]
                hit = jnp.concatenate(
                    [
                        jnp.where(here == lane + jnp.int16(lead), bf16(1), bf16(0))
                        for lead in range(0, columns, 128)
                    ],
                    1,
                )
                total += jnp.dot(grads[part, batch], hit, preferred_element_type=f32)
        return total

    out[...] = lax.fori_loop(0, batches // together, step, base[...].astype(f32))


def spread(grads, ids, base):
    parts, batches, depth, slots = grads.shape
    vocab_rows = base.shape[1]
    columns = 256
    return pl.pallas_call(
        spread_kernel,
        grid=(vocab_rows // columns,),
        out_shape=jax.ShapeDtypeStruct((depth, vocab_rows), f32),
        in_specs=[
            pl.BlockSpec((batches * parts, slots), lambda at: (0, 0)),
            pl.BlockSpec((parts, batches, depth, slots), lambda at: (0, 0, 0, 0)),
            pl.BlockSpec((depth, columns), lambda at: (0, at)),
        ],
        out_specs=pl.BlockSpec((depth, columns), lambda at: (0, at)),
        scratch_shapes=[pltpu.VMEM((batches * parts, slots, 128), jnp.int16)],
        compiler_params=pltpu.CompilerParams(vmem_limit_bytes=56 << 20),
    )(ids.reshape(batches * parts, slots), grads, base)


def summed(landed):
    sums = [
        (one.astype(f32) + two.astype(f32)).astype(bf16)
        for one, two in zip(landed[::2], landed[1::2])
    ]
    return jnp.concatenate(sums, -1)


def over_batch(block):
    return lax.psum_scatter(block, "batch", scatter_dimension=0, tiled=False)


def tie(*values):
    return lax.optimization_barrier(values)


def on_device(
    token_ids,
    seq_lengths,
    embed_table,
    norm_gains,
    final_gain,
    qkv_weight,
    qkv_conv,
    out_weight,
    up_weight,
    down_weight,
    logit_grad,
):
    section = lax.axis_index("section")
    first = section == 0
    core, seq_at, x_at, _ = place()
    quarter = 2 * core + x_at
    me = lax.axis_index("tensor")
    at_batch = lax.axis_index("batch")
    tensor_count = lax.axis_size("tensor")
    batch_count = lax.axis_size("batch")
    section_count = lax.axis_size("section")
    slot_length = token_ids.shape[1]
    shard_rows = slot_length // tensor_count
    local_width = out_weight.shape[1]
    heads_here = local_width // HEAD
    hidden_width = up_weight.shape[2]
    root_scale = math.sqrt(D)
    depth = D // batch_count
    length = seq_lengths[seq_at]
    sequences = token_ids.shape[0]

    table_own = embed_table.astype(bf16).T
    attn_own = packed(qkv_weight[0].astype(bf16), out_weight[0].astype(bf16).T)
    ffn_own = jnp.concatenate([up_weight[0].astype(bf16), down_weight[0].astype(bf16).T], 1)
    attn_all = lax.all_gather(attn_own, "batch", axis=0, tiled=True)
    ffn_all = lax.all_gather(ffn_own, "batch", axis=0, tiled=True)
    table_turned = lax.all_gather(table_own, "batch", axis=0, tiled=True)

    gain_width = final_gain.shape[0]
    whole_at = (section * batch_count + at_batch) * tensor_count + me
    gains_own = jnp.concatenate([norm_gains.reshape(4, gain_width), final_gain[None]])
    gains_own = lax.dynamic_update_slice_in_dim(
        jnp.zeros((5, D), f32), gains_own.astype(bf16).astype(f32), whole_at * gain_width, 1
    )
    taps_own = qkv_conv[0].astype(bf16).astype(f32).transpose(1, 0, 2, 3)
    taps_own = lax.dynamic_update_slice_in_dim(
        jnp.zeros((3, 3, heads_here, HEAD), f32), taps_own, at_batch * qkv_conv.shape[4], 3
    ).reshape(3, 3, local_width)
    small = jnp.concatenate([gains_own, packed(taps_own, jnp.zeros((3, local_width), f32))])
    all_ids, small = batch_gather([token_ids.reshape(-1, 128), small], 5)
    small = jnp.sum(small, 0)

    vocab_rows = embed_table.shape[0]
    owner_start = (section * tensor_count + me) * vocab_rows
    local_ids = all_ids.reshape(batch_count, sequences * 4, 1, shard_rows) - owner_start
    picked = lookup(table_own, local_ids)
    total = plane_reduce(picked.reshape(8, D, shard_rows), 3).astype(bf16)
    embedded, small = batch_trade(total.reshape(batch_count, depth, shard_rows), small, 8)
    gains_all = jnp.sum(small[:, :5], 0)
    final_scale = gains_all[4]
    taps_here = [
        lax.dynamic_index_in_dim(
            small, 4 * (quarter // 2) + 2 * layer + quarter % 2, 0, keepdims=False
        )[5:, :640]
        for layer in range(section_count)
    ]
    embedded = embedded.reshape(D, shard_rows).T

    def ffn_weights(block):
        return block[:, :hidden_width], block[:, hidden_width:]

    first_rows = embedded.astype(f32) * root_scale
    normed = (first_rows * norm_factor(first_rows) * gains_all[0]).astype(bf16)
    gathered, attn_first = group_gather(normed, 1, cargo=("out", 0, [attn_all]))
    partial, attn_kept_first = attention_forward(
        gathered.reshape(-1, D), length, attn_first, taps_here[0]
    )
    gathered, first_middle, block = turn(
        partial, first_rows, gains_all[1], 20, False, cargo=("out", 0, [ffn_all])
    )
    ffn_first = ffn_weights(block)
    partial, ffn_kept_first = ffn_forward(gathered.reshape(-1, D), ffn_first)
    gathered, second_rows, attn_second = turn(
        partial, first_middle, gains_all[2], 21, True, cargo=("out", 1, [attn_all])
    )
    partial, attn_kept_second = attention_forward(
        gathered.reshape(-1, D), length, attn_second, taps_here[1]
    )
    gathered, second_middle, block = turn(
        partial, second_rows, gains_all[3], 24, False, cargo=("out", 1, [ffn_all])
    )
    ffn_second = ffn_weights(block)
    partial, ffn_kept_second = ffn_forward(gathered.reshape(-1, D), ffn_second)

    def halves(blob):
        blob = blob if isinstance(blob, list) else [blob]
        return [one.reshape(batch_count, 2, depth // 2, one.shape[1]) for one in blob]

    grad_both = mm(logit_grad.reshape(-1, vocab_rows), table_turned, 1, 1).astype(bf16)
    grad_final = plane_reduce(grad_both.reshape(8, shard_rows, D), 4)
    own_at = quarter * shard_rows + jnp.arange(shard_rows)
    grad_final = jnp.where((own_at < length)[:, None], grad_final, 0.0)

    partial, grad_final = tie(partial, grad_final)
    final_rows = (second_middle + group_reduce(partial, 2)).astype(bf16).astype(f32)
    normed_final = (final_rows * norm_factor(final_rows) * final_scale).astype(bf16)
    final_both = plane_gather(normed_final, 7).reshape(-1, D)
    logits = mm(final_both, table_turned, 1, 0).astype(bf16).reshape(sequences, slot_length, -1)
    valid = (jnp.arange(slot_length)[None, :] < seq_lengths[:, None]).reshape(-1, 1)
    masked_final = jnp.where(valid, final_both, jnp.zeros((), bf16))
    head_table = mm(masked_final, logit_grad.reshape(-1, vocab_rows), 0, 0).astype(bf16)
    grad_final, head_table = tie(grad_final, head_table)
    head_done = lax.psum_scatter(head_table, "batch", scatter_dimension=0, tiled=True)

    grad_rows, grad_final_gain = norm_back(grad_final, final_rows, final_scale)
    gathered = group_gather(grad_rows.astype(bf16), 13).reshape(-1, D)
    partial, blob = ffn_backward(gathered, ffn_second, ffn_kept_second)
    gathered, grad_rows, gain_2f, *landed = turn(
        partial, second_middle, gains_all[3], 22, False, passed=grad_rows,
        cargo=("in", 1, halves(blob)),
    )
    ffn_second_sum = summed(landed)
    partial, blob, taps_second = attention_backward(
        gathered.reshape(-1, D), length, attn_second, taps_here[1], attn_kept_second
    )
    gathered, grad_rows, gain_2a, *landed = turn(
        partial, second_rows, gains_all[2], 23, True, passed=grad_rows,
        cargo=("in", 1, halves(blob)),
    )
    attn_second_sum = summed(landed)
    partial, blob = ffn_backward(gathered.reshape(-1, D), ffn_first, ffn_kept_first)
    partial, head_done = tie(partial, head_done)
    gathered, grad_rows, gain_1f, *landed = turn(
        partial, first_middle, gains_all[1], 25, False, passed=grad_rows,
        cargo=("in", 0, halves(blob)),
    )
    ffn_first_sum = summed(landed)
    partial, blob, taps_first = attention_backward(
        gathered.reshape(-1, D), length, attn_first, taps_here[0], attn_kept_first
    )
    ffn_second_done = over_batch(ffn_second_sum)
    partial, ffn_second_done = tie(partial, ffn_second_done)
    attn_second_done, ffn_first_done = over_batch(attn_second_sum), over_batch(ffn_first_sum)
    grad_norm, *landed = group_reduce(partial, 14, cargo=("in", 0, halves(blob)))
    attn_first_sum = summed(landed)
    grad_norm, gain_1a = norm_back(grad_norm, first_rows, gains_all[0])
    grad_rows = grad_rows + grad_norm
    grad_rows, attn_second_done, ffn_first_done = tie(
        grad_rows, attn_second_done, ffn_first_done
    )
    attn_first_done = over_batch(attn_first_sum)

    embed_grad = (grad_rows * root_scale).astype(bf16).T
    def row_at(index, vector):
        padded = jnp.pad(vector, (0, D - vector.shape[0]))[None]
        return jnp.where(jnp.arange(16)[:, None] == index, padded, 0.0)

    vectors = [gain_1a, gain_1f[0], gain_2a[0], gain_2f[0], grad_final_gain, *taps_first[:3], *taps_second[:3]]
    rows = sum(row_at(index, vector) for index, vector in enumerate(vectors))
    traded, rows = batch_trade(embed_grad.reshape(batch_count, depth, shard_rows), rows, 9)
    gain_sums = jnp.sum(rows[:, :5], 0)
    holders = rows.reshape(2, 4, 16, D)[:, :, 5:11].reshape(2, 4, 2, 3, D)
    taps_sums = jnp.sum(lax.dynamic_index_in_dim(holders, me, 1, keepdims=False), 0)
    taps_sums = lax.dynamic_index_in_dim(taps_sums, section, 0, keepdims=False)
    sums = jnp.concatenate([gain_sums, taps_sums])
    every, sums = plane_and_batch_gather(traded.reshape(D, shard_rows), sums, 10)
    sums, attn_first_done = tie(sums, attn_first_done)
    every = every.reshape(8, batch_count, depth, shard_rows)
    table_done = spread(every, local_ids, head_done).T
    sums = jnp.sum(sums, 0)
    gain_part = lax.dynamic_slice_in_dim(sums[:5], whole_at * gain_width, gain_width, 1)
    gains_done = gain_part[:4].reshape(2, 2, gain_width)
    final_done = gain_part[4]
    conv_part = unpacked(sums[5:8]).reshape(3, 3, heads_here, HEAD).transpose(1, 0, 2, 3)
    conv_done = lax.dynamic_slice_in_dim(
        conv_part, at_batch * qkv_conv.shape[4], qkv_conv.shape[4], 3
    )[None]
    def placed(first_part, second_part):
        keep = jnp.where(first, first_part, second_part)
        got = lax.ppermute(jnp.where(first, second_part, first_part), "section", [(0, 1), (1, 0)])
        return jnp.where(
            first, jnp.concatenate([keep, got], 0), jnp.concatenate([got, keep], 0)
        ).astype(f32)

    attn_done = placed(attn_first_done, attn_second_done)
    ffn_done = placed(ffn_first_done, ffn_second_done)
    qkv_done = unpacked(attn_done)[None]
    out_done = jnp.concatenate([attn_done[:, 640:], attn_done[:, 576:640]], 1).T[None]
    up_done = ffn_done[:, :hidden_width][None]
    down_done = ffn_done[:, hidden_width:].T[None]
    return (
        logits,
        table_done,
        gains_done,
        final_done,
        qkv_done,
        conv_done,
        out_done,
        up_done,
        down_done,
    )


def solution(mesh):
    in_specs = (
        P("batch", None),
        P("batch"),
        P(("section", "tensor"), "batch"),
        P(None, None, ("section", "batch", "tensor")),
        P(("section", "batch", "tensor")),
        P("section", "batch", None, "tensor"),
        P("section", None, None, "tensor", "batch"),
        P("section", "tensor", "batch"),
        P("section", "batch", "tensor"),
        P("section", "tensor", "batch"),
        P("batch", None, ("section", "tensor")),
    )
    out_specs = (
        P("batch", None, ("section", "tensor")),
        P(("section", "tensor"), "batch"),
        P(None, None, ("section", "batch", "tensor")),
        P(("section", "batch", "tensor")),
        P("section", "batch", None, "tensor"),
        P("section", None, None, "tensor", "batch"),
        P("section", "tensor", "batch"),
        P("section", "batch", "tensor"),
        P("section", "tensor", "batch"),
    )
    return jax.shard_map(
        on_device, mesh=mesh, in_specs=in_specs, out_specs=out_specs, check_vma=False
    )
```

```python
import functools
import math

import jax
import jax.numpy as jnp
from jax import lax
from jax.experimental import pallas as pl
from jax.experimental.pallas import tpu as pltpu
from jax.sharding import PartitionSpec as P

D = 768
HEAD = 64

norm_eps = 1e-06
masked_score = -1e30
bf16 = jnp.bfloat16
f32 = jnp.float32


def mm(left, right, left_dim, right_dim):
    return lax.dot_general(
        left, right, (((left_dim,), (right_dim,)), ((), ())), preferred_element_type=f32
    )


def norm_factor(rows):
    return lax.rsqrt(jnp.mean(rows * rows, axis=-1, keepdims=True) + norm_eps)


def norm_back(grad, rows, gain):
    factor = norm_factor(rows)
    scaled = grad * gain
    inner = jnp.mean(scaled * rows, axis=-1, keepdims=True)
    grad_rows = factor * scaled - rows * (factor * factor * factor * inner)
    return grad_rows, jnp.sum(grad * rows * factor, axis=0)


MESH = pl.DeviceIdType.MESH


def place():
    core = lax.axis_index("section")
    tensor = lax.axis_index("tensor")
    return core, tensor // 2, tensor % 2, tensor


def remote(src, dst, send, recv, device):
    return pltpu.make_async_remote_copy(
        src_ref=src,
        dst_ref=dst,
        send_sem=send,
        recv_sem=recv,
        device_id=device,
        device_id_type=MESH,
    )


def greet(devices):
    barrier = pltpu.get_barrier_semaphore()
    for device in devices:
        pl.semaphore_signal(barrier, inc=1, device_id=device, device_id_type=MESH)
    pl.semaphore_wait(barrier, len(devices))


def comm_call(
    body, out_shape, scratch, collective_id, *operands, cargo=None, streamed=(), room=16
):
    shapes = list(out_shape) if isinstance(out_shape, (list, tuple)) else [out_shape]
    in_specs = [pl.BlockSpec(memory_space=pltpu.VMEM)] * len(operands)
    out_specs = [pl.BlockSpec(memory_space=pltpu.VMEM)] * len(shapes)
    scratch = list(scratch)
    operands = operands + tuple(streamed)
    in_specs += [pl.BlockSpec(memory_space=pl.ANY)] * len(streamed)
    count_in, count_out = len(operands), len(shapes)
    loads = 0
    if cargo is not None:
        kind, layer, arrays = cargo
        loads = len(arrays)
        operands = operands + tuple(arrays)
        in_specs += [pl.BlockSpec(memory_space=pl.ANY)] * loads
        landing = []
        for array in arrays:
            if kind == "out":
                landing.append(jax.ShapeDtypeStruct(array.shape, array.dtype))
            else:
                batches, _, rows, width = array.shape
                landing += [jax.ShapeDtypeStruct((batches, rows, width), array.dtype)] * 2
        shapes += landing
        out_specs += [pl.BlockSpec(memory_space=pl.ANY)] * len(landing)
        scratch += [pltpu.SemaphoreType.DMA((loads, 3))] * 2

    def kernel(*refs):
        ins, rest = refs[: len(operands)], refs[len(operands) :]
        outs, rest = rest[: len(shapes)], rest[len(shapes) :]
        if cargo is None:
            body(*ins, *outs, *rest)
            return
        send, recv = rest[-2:]
        made = Outward if kind == "out" else Inward
        lands = len(landing) // loads

        def load():
            return [
                made(
                    layer,
                    ins[count_in + at],
                    outs[count_out + lands * at : count_out + lands * (at + 1)],
                    send.at[at],
                    recv.at[at],
                )
                for at in range(loads)
            ]

        body(*ins[:count_in], *outs[:count_out], *rest[:-2], load=load)

    results = pl.pallas_call(
        kernel,
        out_shape=shapes,
        in_specs=in_specs,
        out_specs=out_specs,
        scratch_shapes=scratch,
        compiler_params=pltpu.CompilerParams(
            collective_id=collective_id, has_side_effects=True, vmem_limit_bytes=room << 20
        ),
    )(*operands)
    return results if len(shapes) > 1 else results[0]


class Outward:
    def __init__(self, layer, source, landing, send, recv):
        core, y, _, tensor = place()
        target = landing[0]
        self.layer, self.core, self.y = layer, core, y
        self.near = remote(source, target, send.at[0], recv.at[0], {"section": 1 - core})
        self.far = remote(
            source, target, send.at[1], recv.at[0], {"section": y, "tensor": tensor + 2 - 4 * y}
        )
        self.local = pltpu.make_async_copy(source, target, recv.at[1])

    def start(self):
        @pl.when(self.core == self.layer)
        def _():
            self.far.start()

            @pl.when(self.y == self.layer)
            def _():
                self.local.start()

            @pl.when(self.y != self.layer)
            def _():
                self.near.start()

    def wait(self):
        stays = (self.core == self.layer) & (self.y == self.layer)

        @pl.when(stays)
        def _():
            self.local.wait()

        @pl.when(jnp.logical_not(stays))
        def _():
            self.far.wait_recv()

        @pl.when(self.core == self.layer)
        def _():
            self.far.wait_send()

            @pl.when(self.y != self.layer)
            def _():
                self.near.wait_send()


class Inward:
    def __init__(self, layer, source, landing, send, recv):
        core, y, _, tensor = place()
        above = tensor + 2 - 4 * y
        self.near = core == y
        self.to_core = remote(
            source.at[:, 1 - y], landing[0], send.at[0], recv.at[0], {"section": 1 - core}
        )
        self.to_same = remote(
            source.at[:, 1 - y], landing[0], send.at[0], recv.at[0], {"tensor": above}
        )
        self.to_both = remote(
            source.at[:, y],
            landing[1],
            send.at[1],
            recv.at[1],
            {"section": 1 - core, "tensor": above},
        )
        self.fill = pltpu.make_async_copy(source.at[:, y], landing[1], recv.at[2])

    def start(self):
        @pl.when(self.near)
        def _():
            self.to_core.start()
            self.fill.start()

        @pl.when(jnp.logical_not(self.near))
        def _():
            self.to_same.start()
            self.to_both.start()

    def wait(self):
        @pl.when(self.near)
        def _():
            self.to_same.wait_recv()
            self.fill.wait()
            self.to_core.wait_send()

        @pl.when(jnp.logical_not(self.near))
        def _():
            self.to_core.wait_recv()
            self.to_both.wait_recv()
            self.to_same.wait_send()
            self.to_both.wait_send()


def greet_group(other, beside, load):
    if load is None:
        greet([other, beside])
        return []
    _, y, _, tensor = place()
    above = tensor + 2 - 4 * y
    greet([other, beside, {"section": 0, "tensor": above}, {"section": 1, "tensor": above}])
    made = load()
    for one in made:
        one.start()
    return made


PIECES = 4


def group_gather_kernel(own, out, send, recv, load=None):
    core, _, x, tensor = place()
    other = {"section": 1 - core}
    beside = {"tensor": tensor + 1 - 2 * x}
    here = 2 * core + x
    there = 2 * core + 1 - x
    cargo = greet_group(other, beside, load)
    piece = own.shape[0] // PIECES
    cuts = [pl.ds(at * piece, piece) for at in range(PIECES)]
    across = []
    for at, cut in enumerate(cuts):
        copy = remote(own.at[cut], out.at[here, cut], send.at[at], recv.at[at], beside)
        copy.start()
        across.append(copy)
    last = 2 * PIECES
    direct = remote(own, out.at[here], send.at[last], recv.at[last], other)
    direct.start()
    out[here] = own[...]
    passed = []
    for at, cut in enumerate(cuts):
        across[at].wait_recv()
        copy = remote(
            out.at[there, cut],
            out.at[there, cut],
            send.at[PIECES + at],
            recv.at[PIECES + at],
            other,
        )
        copy.start()
        passed.append(copy)
    for copy in across:
        copy.wait_send()
    direct.wait()
    for copy in passed:
        copy.wait()
    for one in cargo:
        one.wait()


def group_gather(rows, collective_id, cargo=None):
    count, width = rows.shape
    return comm_call(
        group_gather_kernel,
        jax.ShapeDtypeStruct((4, count, width), rows.dtype),
        [pltpu.SemaphoreType.DMA((2 * PIECES + 1,))] * 2,
        collective_id,
        rows,
        cargo=cargo,
    )


def group_reduce_kernel(parts, out, near, far, mixed, send, recv, load=None):
    core, _, x, tensor = place()
    other = {"section": 1 - core}
    beside = {"tensor": tensor + 1 - 2 * x}
    here = 2 * core + x
    there = 2 * core + 1 - x
    over_here = 2 * (1 - core) + x
    over_there = 2 * (1 - core) + 1 - x
    cargo = greet_group(other, beside, load)
    piece = out.shape[0] // PIECES
    cuts = [pl.ds(at * piece, piece) for at in range(PIECES)]
    first = []
    for at, cut in enumerate(cuts):
        copy = remote(
            parts.at[over_there, cut], near.at[1, cut], send.at[at], recv.at[at], other
        )
        copy.start()
        first.append(copy)
    last = 2 * PIECES
    direct = remote(parts.at[over_here], near.at[0], send.at[last], recv.at[last], other)
    direct.start()
    across = []
    for at, cut in enumerate(cuts):
        first[at].wait_recv()
        mixed[cut] = (parts[there, cut].astype(f32) + near[1, cut].astype(f32)).astype(bf16)
        copy = remote(
            mixed.at[cut], far.at[cut], send.at[PIECES + at], recv.at[PIECES + at], beside
        )
        copy.start()
        across.append(copy)
    direct.wait()
    for at, cut in enumerate(cuts):
        across[at].wait_recv()
        out[cut] = (
            parts[here, cut].astype(f32) + near[0, cut].astype(f32) + far[cut].astype(f32)
        )
    for copy in first + across:
        copy.wait_send()
    for one in cargo:
        one.wait()


def group_reduce(parts, collective_id, cargo=None):
    parts = parts.reshape(4, -1, D)
    _, count, width = parts.shape
    return comm_call(
        group_reduce_kernel,
        jax.ShapeDtypeStruct((count, width), f32),
        [
            pltpu.VMEM((2, count, width), bf16),
            pltpu.VMEM((count, width), bf16),
            pltpu.VMEM((count, width), bf16),
        ]
        + [pltpu.SemaphoreType.DMA((2 * PIECES + 1,))] * 2,
        collective_id,
        parts,
        cargo=cargo,
    )


def turn_kernel(backward, rounded, *refs, load=None):
    if backward:
        parts, rows, gain, passed, gathered, fresh, gain_grad, near, far, mixed, send, recv = refs
    else:
        parts, rows, gain, gathered, fresh, near, far, mixed, send, recv = refs
    core, _, x, tensor = place()
    other = {"section": 1 - core}
    beside = {"tensor": tensor + 1 - 2 * x}
    here = 2 * core + x
    there = 2 * core + 1 - x
    over_here = 2 * (1 - core) + x
    over_there = 2 * (1 - core) + 1 - x
    cargo = greet_group(other, beside, load)
    piece = fresh.shape[0] // PIECES
    cuts = [pl.ds(at * piece, piece) for at in range(PIECES)]

    def start(src, dst, kind, at, device):
        index = kind * PIECES + at
        made = remote(src, dst, send.at[index], recv.at[index], device)
        made.start()
        return made

    handed, direct = [], []
    for at, cut in enumerate(cuts):
        handed.append(start(parts.at[over_there, cut], near.at[1, cut], 0, at, other))
        direct.append(start(parts.at[over_here, cut], near.at[0, cut], 1, at, other))
    across = []
    for at, cut in enumerate(cuts):
        handed[at].wait_recv()
        mixed[cut] = (parts[there, cut].astype(f32) + near[1, cut].astype(f32)).astype(bf16)
        across.append(start(mixed.at[cut], far.at[cut], 2, at, beside))
    out_across, out_direct, onward = [], [], []
    gains = gain[...]
    for at in range(PIECES + 1):
        if at < PIECES:
            cut = cuts[at]
            direct[at].wait_recv()
            across[at].wait_recv()
            total = (
                parts[here, cut].astype(f32) + near[0, cut].astype(f32) + far[cut].astype(f32)
            )
            held = rows[cut]
            if backward:
                factor = norm_factor(held)
                scaled = total * gains
                inner = jnp.mean(scaled * held, axis=-1, keepdims=True)
                new = passed[cut] + factor * scaled - held * (factor * factor * factor * inner)
                gain_part = jnp.sum(total * held * factor, axis=0, keepdims=True)
                gain_grad[...] = gain_part if at == 0 else gain_grad[...] + gain_part
                if rounded:
                    new = new.astype(bf16).astype(f32)
                shown = new.astype(bf16)
            else:
                new = held + total
                if rounded:
                    new = new.astype(bf16).astype(f32)
                shown = (new * norm_factor(new) * gains).astype(bf16)
            fresh[cut] = new
            gathered[here, cut] = shown
            out_across.append(start(gathered.at[here, cut], gathered.at[here, cut], 3, at, beside))
            out_direct.append(start(gathered.at[here, cut], gathered.at[here, cut], 4, at, other))
        if at >= 1:
            cut = cuts[at - 1]
            out_across[at - 1].wait_recv()
            onward.append(start(gathered.at[there, cut], gathered.at[there, cut], 5, at - 1, other))
    for made in handed + direct + across + out_across:
        made.wait_send()
    for made in out_direct + onward:
        made.wait()
    for one in cargo:
        one.wait()


def turn(parts, rows, gain, collective_id, rounded, passed=None, cargo=None):
    parts = parts.reshape(4, -1, D)
    _, count, width = parts.shape
    backward = passed is not None
    shapes = [
        jax.ShapeDtypeStruct((4, count, width), bf16),
        jax.ShapeDtypeStruct((count, width), f32),
    ]
    operands = [parts, rows, gain.reshape(1, width)]
    if backward:
        shapes.append(jax.ShapeDtypeStruct((1, width), f32))
        operands.append(passed)
    return comm_call(
        functools.partial(turn_kernel, backward, rounded),
        shapes,
        [
            pltpu.VMEM((2, count, width), bf16),
            pltpu.VMEM((count, width), bf16),
            pltpu.VMEM((count, width), bf16),
        ]
        + [pltpu.SemaphoreType.DMA((6 * PIECES,))] * 2,
        collective_id,
        *operands,
        cargo=cargo,
    )


def plane_peers():
    core, y, x, tensor = place()
    return [
        {"section": 1 - core},
        {"tensor": tensor + 1 - 2 * x},
        {"tensor": tensor + 2 - 4 * y},
    ]


def plane_gather_kernel(own, out, send, recv):
    greet(plane_peers())
    plane_exchange(own, out, send, recv)


class Chores:
    def __init__(self, units=()):
        self.units = list(units)

    def some(self, count):
        for _ in range(min(count, len(self.units))):
            self.units.pop(0)()

    def rest(self):
        self.some(len(self.units))


def stream(count, source_at, buffers, sems, work):
    def fetch(at):
        return pltpu.make_async_copy(source_at(at), buffers.at[at % 2], sems.at[at % 2])

    def unit(at):
        fetch(at).wait()
        work(at, buffers.at[at % 2])
        if at + 2 < count:
            fetch(at + 2).start()

    for at in range(min(2, count)):
        fetch(at).start()
    return [functools.partial(unit, at) for at in range(count)]


def plane_exchange(own, out, send, recv, chores=Chores()):
    core, y, x, _ = place()
    other, beside, above = plane_peers()
    half = own.shape[0] // 2
    cut = [pl.ds(0, half), pl.ds(half, half)]

    def slot(along_y, along_x):
        return 4 * along_y + 2 * core + along_x

    me = slot(y, x)
    at_x, at_y, at_both = slot(y, 1 - x), slot(1 - y, x), slot(1 - y, 1 - x)

    def copy(src, where, index, device):
        made = remote(src, out.at[where], send.at[index], recv.at[index], device)
        made.start()
        return made

    to_x = [remote(own.at[cut[h]], out.at[me, cut[h]], send.at[h], recv.at[h], beside) for h in (0, 1)]
    to_y = [remote(own.at[cut[h]], out.at[me, cut[h]], send.at[2 + h], recv.at[2 + h], above) for h in (0, 1)]
    to_x[0].start()
    to_y[1].start()
    to_x[1].start()
    to_y[0].start()
    pending = [copy(own, me, 4, other)]
    out[me] = own[...]

    def onward(where, h, index, device):
        made = remote(
            out.at[where, cut[h]], out.at[where, cut[h]], send.at[index], recv.at[index], device
        )
        made.start()
        return made

    chores.some(2)
    to_x[0].wait_recv()
    diag_y = onward(at_x, 0, 5, above)
    pending.append(onward(at_x, 0, 6, other))
    to_y[1].wait_recv()
    diag_x = onward(at_y, 1, 7, beside)
    pending.append(onward(at_y, 1, 8, other))
    chores.some(2)
    to_x[1].wait_recv()
    pending.append(onward(at_x, 1, 9, other))
    to_y[0].wait_recv()
    pending.append(onward(at_y, 0, 10, other))
    chores.some(2)
    diag_y.wait_recv()
    pending.append(onward(at_both, 0, 11, other))
    diag_x.wait_recv()
    pending.append(onward(at_both, 1, 12, other))
    chores.rest()
    for made in to_x + to_y + [diag_x, diag_y]:
        made.wait_send()
    for made in pending:
        made.wait()


def head_gather_kernel(own, table, grads, out, parts, buffers, sems, send, recv):
    greet(plane_peers())
    rows = own.shape[0]

    def work(at, block):
        parts[at] = mm(block[...], table[...], 1, 1).astype(bf16)

    chores = Chores(
        stream(8, lambda at: grads.at[pl.ds(rows * at, rows)], buffers, sems, work)
    )
    plane_exchange(own, out, send, recv, chores)


def head_gather(rows, table, grads):
    count, width = rows.shape
    return comm_call(
        head_gather_kernel,
        [jax.ShapeDtypeStruct((8, count, width), bf16)] * 2,
        [
            pltpu.VMEM((2, count, grads.shape[1]), bf16),
            pltpu.SemaphoreType.DMA((2,)),
        ]
        + [pltpu.SemaphoreType.DMA((13,))] * 2,
        7,
        rows,
        table,
        streamed=[grads],
        room=28,
    )


def plane_reduce_kernel(parts, out, *scratch):
    greet(plane_peers())
    plane_sum(parts, out, *scratch)


def plane_sum(
    parts, out, near, mixed, via_x, via_y, from_x, from_y, hop_x, hop_y, send, recv, chores=Chores()
):
    core, y, x, _ = place()
    other, beside, above = plane_peers()
    half = out.shape[0] // 2
    cut = [pl.ds(0, half), pl.ds(half, half)]

    def slot(at_core, along_y, along_x):
        return 4 * along_y + 2 * at_core + along_x

    targets = [(1 - y, 1 - x), (y, 1 - x), (1 - y, x), (y, x)]
    handed = []
    for index, (along_y, along_x) in enumerate(targets):
        made = remote(
            parts.at[slot(1 - core, along_y, along_x)],
            near.at[index],
            send.at[index],
            recv.at[index],
            other,
        )
        made.start()
        handed.append(made)

    def joined(index, where=slice(None)):
        along_y, along_x = targets[index]
        mine = parts[slot(core, along_y, along_x), where]
        return mine.astype(f32) + near[index, where].astype(f32)

    def start(src, dst, index, device):
        made = remote(src, dst, send.at[index], recv.at[index], device)
        made.start()
        return made

    handed[0].wait_recv()
    mixed[0] = joined(0).astype(bf16)
    diag_x = start(mixed.at[0, cut[0]], via_x, 4, beside)
    diag_y = start(mixed.at[0, cut[1]], via_y, 5, above)
    handed[1].wait_recv()
    mixed[1] = joined(1).astype(bf16)
    straight_x = start(mixed.at[1, cut[0]], from_x.at[cut[0]], 6, beside)
    handed[2].wait_recv()
    mixed[2] = joined(2).astype(bf16)
    straight_y = start(mixed.at[2, cut[1]], from_y.at[cut[1]], 7, above)
    chores.some(2)
    diag_x.wait_recv()
    hop_y[...] = (mixed[2, cut[0]].astype(f32) + via_x[...].astype(f32)).astype(bf16)
    turned_y = start(hop_y, from_y.at[cut[0]], 8, above)
    diag_y.wait_recv()
    hop_x[...] = (mixed[1, cut[1]].astype(f32) + via_y[...].astype(f32)).astype(bf16)
    turned_x = start(hop_x, from_x.at[cut[1]], 9, beside)
    chores.rest()
    handed[3].wait_recv()
    straight_x.wait_recv()
    turned_y.wait_recv()
    out[cut[0]] = joined(3, cut[0]) + from_x[cut[0]].astype(f32) + from_y[cut[0]].astype(f32)
    straight_y.wait_recv()
    turned_x.wait_recv()
    out[cut[1]] = joined(3, cut[1]) + from_x[cut[1]].astype(f32) + from_y[cut[1]].astype(f32)
    for made in handed + [diag_x, diag_y, straight_x, straight_y, turned_x, turned_y]:
        made.wait_send()


def plane_scratch(count, width):
    half = count // 2
    return [
        pltpu.VMEM((4, count, width), bf16),
        pltpu.VMEM((3, count, width), bf16),
        pltpu.VMEM((half, width), bf16),
        pltpu.VMEM((half, width), bf16),
        pltpu.VMEM((count, width), bf16),
        pltpu.VMEM((count, width), bf16),
        pltpu.VMEM((half, width), bf16),
        pltpu.VMEM((half, width), bf16),
    ] + [pltpu.SemaphoreType.DMA((10,))] * 2


def plane_reduce(parts, collective_id):
    _, count, width = parts.shape
    return comm_call(
        plane_reduce_kernel,
        jax.ShapeDtypeStruct((count, width), f32),
        plane_scratch(count, width),
        collective_id,
        parts,
    )


def head_reduce_kernel(parts, rows, valid, grads, out, table_grad, held, buffers, sems, *scratch):
    greet(plane_peers())
    width = buffers.shape[2]
    for lead in range(0, rows.shape[1], 128):
        held[:, lead : lead + 128] = rows[:, lead : lead + 128] * valid[...]

    def work(at, block):
        table_grad[:, width * at : width * at + width] = mm(held[...], block[...], 0, 0).astype(bf16)

    steps = grads.shape[1] // width
    chores = Chores(
        stream(steps, lambda at: grads.at[:, pl.ds(width * at, width)], buffers, sems, work)
    )
    plane_sum(parts, out, *scratch, chores=chores)


def head_reduce(parts, rows, valid, grads):
    _, count, width = parts.shape
    step = 512
    return comm_call(
        head_reduce_kernel,
        [
            jax.ShapeDtypeStruct((count, width), f32),
            jax.ShapeDtypeStruct((width, grads.shape[1]), bf16),
        ],
        [
            pltpu.VMEM(rows.shape, bf16),
            pltpu.VMEM((2, rows.shape[0], step), bf16),
            pltpu.SemaphoreType.DMA((2,)),
        ]
        + plane_scratch(count, width),
        4,
        parts,
        rows,
        valid,
        streamed=[grads],
        room=40,
    )


def batch_peers(count):
    me = lax.axis_index("batch")
    return [{"batch": lax.rem(me + step, count)} for step in range(1, count)]


def batch_exchange(count, ins, outs, send, recv):
    me = lax.axis_index("batch")
    copies = []
    for index, peer in enumerate(batch_peers(count)):
        for kind in range(len(ins)):
            at = index * len(ins) + kind
            copies.append(remote(ins[kind], outs[kind].at[me], send.at[at], recv.at[at], peer))
            copies[-1].start()
    for kind in range(len(ins)):
        outs[kind][me] = ins[kind][...]
    return copies


def batch_gather_kernel(count, *refs):
    kinds = (len(refs) - 2) // 2
    greet(batch_peers(count))
    for copy in batch_exchange(count, refs[:kinds], refs[kinds : 2 * kinds], *refs[2 * kinds :]):
        copy.wait()


def batch_gather(blocks, collective_id):
    count = lax.axis_size("batch")
    return comm_call(
        functools.partial(batch_gather_kernel, count),
        [jax.ShapeDtypeStruct((count,) + block.shape, block.dtype) for block in blocks],
        [pltpu.SemaphoreType.DMA(((count - 1) * len(blocks),))] * 2,
        collective_id,
        *blocks,
    )


def plane_and_batch_kernel(count, own, few, out, few_out, send, recv, few_send, few_recv):
    greet(plane_peers() + batch_peers(count))
    copies = batch_exchange(count, [few], [few_out], few_send, few_recv)
    plane_exchange(own, out, send, recv)
    for copy in copies:
        copy.wait()


def plane_and_batch_gather(block, few, collective_id):
    count = lax.axis_size("batch")
    return comm_call(
        functools.partial(plane_and_batch_kernel, count),
        [
            jax.ShapeDtypeStruct((8,) + block.shape, block.dtype),
            jax.ShapeDtypeStruct((count,) + few.shape, few.dtype),
        ],
        [pltpu.SemaphoreType.DMA((13,))] * 2 + [pltpu.SemaphoreType.DMA((count - 1,))] * 2,
        collective_id,
        block,
        few,
    )


def batch_trade_kernel(count, parts, few, out, few_out, send, recv, few_send, few_recv):
    me = lax.axis_index("batch")
    greet(plane_peers() + batch_peers(count))
    copies = []
    for index, peer in enumerate(batch_peers(count)):
        copies.append(
            remote(parts.at[peer["batch"]], out.at[me], send.at[index], recv.at[index], peer)
        )
        copies[-1].start()
    out[me] = parts[me]
    plane_exchange(few, few_out, few_send, few_recv)
    for copy in copies:
        copy.wait()


def batch_trade(parts, few, collective_id):
    count = parts.shape[0]
    return comm_call(
        functools.partial(batch_trade_kernel, count),
        [
            jax.ShapeDtypeStruct(parts.shape, parts.dtype),
            jax.ShapeDtypeStruct((8,) + few.shape, few.dtype),
        ],
        [pltpu.SemaphoreType.DMA((count - 1,))] * 2 + [pltpu.SemaphoreType.DMA((13,))] * 2,
        collective_id,
        parts,
        few,
    )


ROWS = 256


PACKED = ((0, 0), (0, 1), (1, 0), (1, 1), (2, 0), (2, 1), (0, 2), (1, 2), (2, 2))


def packed(blocks, out):
    cuts = [blocks[:, kind, HEAD * head : HEAD * head + HEAD] for kind, head in PACKED]
    return jnp.concatenate(cuts + [out[:, 2 * HEAD :], out[:, : 2 * HEAD]], 1)


def unpacked(block):
    place_of = {pair: at * HEAD for at, pair in enumerate(PACKED)}
    kinds = []
    for kind in range(3):
        cuts = [
            block[:, place_of[kind, head] : place_of[kind, head] + HEAD] for head in range(3)
        ]
        kinds.append(jnp.concatenate(cuts, 1))
    return jnp.stack(kinds, 1)


def attention_heads(mixed, queries, keys, values):
    low = lax.broadcasted_iota(jnp.int32, (mixed.shape[0], 128), 1) < HEAD
    tile = [mixed[:, 128 * at : 128 * at + 128] for at in range(5)]
    scaled = tile[0] * (HEAD**-0.5)
    queries[0] = jnp.where(low, scaled, 0.0).astype(bf16)
    queries[1] = jnp.where(low, 0.0, scaled).astype(bf16)
    queries[2] = jnp.where(low, tile[3] * (HEAD**-0.5), 0.0).astype(bf16)
    keys[0] = tile[1].astype(bf16)
    keys[1] = pltpu.roll(tile[3], HEAD, 1).astype(bf16)
    values[0] = tile[2].astype(bf16)
    values[1] = tile[4].astype(bf16)


def key_bias(length, total):
    at = lax.broadcasted_iota(jnp.int32, (1, total), 1)
    return jnp.where(at < length, 0.0, masked_score)


def masked(scores, bias, lead):
    scores = scores + bias
    row = lax.broadcasted_iota(jnp.int32, (ROWS, ROWS), 0)
    column = lax.broadcasted_iota(jnp.int32, (ROWS, ROWS), 1)
    last = jnp.where(column <= row, scores[:, lead:], masked_score)
    return last if lead == 0 else jnp.concatenate([scores[:, :lead], last], 1)


def attention_forward_kernel(
    length, x, weight, taps, partial, mixed_out, projected_out, context, totals, projected, queries, keys, values
):
    total = x.shape[0]
    width = 5 * 128
    projected[:8] = jnp.zeros((8, width), f32)
    for lead in range(0, total, ROWS):
        block = jnp.dot(x[lead : lead + ROWS], weight[:, :width], preferred_element_type=f32)
        projected[lead + 8 : lead + 8 + ROWS] = block
        projected_out[lead : lead + ROWS] = block.astype(bf16)
    for lead in range(0, total, ROWS):
        mixed = taps[0:1] * projected[lead + 8 : lead + 8 + ROWS]
        mixed += taps[1:2] * projected[lead + 7 : lead + 7 + ROWS]
        mixed += taps[2:3] * projected[lead + 6 : lead + 6 + ROWS]
        mixed = mixed.astype(bf16)
        mixed_out[lead : lead + ROWS] = mixed
        rows = pl.ds(lead, ROWS)
        attention_heads(
            mixed.astype(f32), queries.at[:, rows], keys.at[:, rows], values.at[:, rows]
        )
    bias = key_bias(length[0], total)
    lane = lax.broadcasted_iota(jnp.int32, (ROWS, 128), 1)
    low = lane < HEAD
    for lead in range(0, total, ROWS):
        reach = lead + ROWS
        found = []
        log_sums = jnp.zeros((ROWS, 128), f32)
        for head in range(3):
            scores = mm(queries[head, lead:reach], keys[head // 2, :reach], 1, 1)
            scores = masked(scores, bias[:, :reach], lead)
            peak = jnp.max(scores, axis=1, keepdims=True)
            raised = jnp.exp(scores - peak)
            weight_sum = jnp.sum(raised, axis=1, keepdims=True)
            probs = (raised * (1.0 / weight_sum)).astype(bf16)
            found.append(
                jnp.dot(probs, values[head // 2, :reach], preferred_element_type=f32)
            )
            log_sums = jnp.where(lane == head, peak + jnp.log(weight_sum), log_sums)
        totals[lead:reach] = log_sums
        joined = jnp.concatenate(
            [
                jnp.where(low, 0.0, pltpu.roll(found[2], HEAD, 1)),
                jnp.where(low, found[0], found[1]),
            ],
            1,
        ).astype(bf16)
        context[lead:reach] = joined
        partial[lead:reach] = mm(joined, weight[:, 512:768], 1, 1).astype(bf16)


def attention_call(body, out_shape, scratch, length, *operands):
    whole = pl.BlockSpec(memory_space=pltpu.VMEM)
    return pl.pallas_call(
        body,
        out_shape=out_shape,
        in_specs=[pl.BlockSpec(memory_space=pltpu.SMEM)] + [whole] * len(operands),
        out_specs=[whole] * len(out_shape),
        scratch_shapes=scratch,
        compiler_params=pltpu.CompilerParams(vmem_limit_bytes=32 << 20),
    )(length.reshape(1), *operands)


def attention_forward(x, length, weight, taps):
    total = x.shape[0]
    partial, *kept = attention_call(
        attention_forward_kernel,
        [
            jax.ShapeDtypeStruct((total, D), bf16),
            jax.ShapeDtypeStruct((total, 640), bf16),
            jax.ShapeDtypeStruct((total, 640), bf16),
            jax.ShapeDtypeStruct((total, 256), bf16),
            jax.ShapeDtypeStruct((total, 128), f32),
        ],
        [
            pltpu.VMEM((total + 8, 640), f32),
            pltpu.VMEM((3, total, 128), bf16),
            pltpu.VMEM((2, total, 128), bf16),
            pltpu.VMEM((2, total, 128), bf16),
        ],
        length,
        x,
        weight,
        taps,
    )
    return partial, (x, *kept)


def attention_backward_kernel(
    length,
    grads,
    x,
    weight,
    taps,
    mixed,
    projected,
    context,
    totals,
    partial,
    weight_grad,
    taps_grad,
    queries,
    keys,
    values,
    outer,
    key_grad,
    value_grad,
    mixed_grad,
    projected_grad,
    turned,
):
    total = x.shape[0]
    width = 5 * 128
    low = lax.broadcasted_iota(jnp.int32, (ROWS, 128), 1) < HEAD
    for lead in range(0, total, ROWS):
        rows = pl.ds(lead, ROWS)
        attention_heads(
            mixed[lead : lead + ROWS].astype(f32),
            queries.at[:, rows],
            keys.at[:, rows],
            values.at[:, rows],
        )
        block = jnp.dot(grads[lead : lead + ROWS], weight[:, 512:768], preferred_element_type=f32)
        third, pair = block[:, :128], block[:, 128:]
        outer[0, lead : lead + ROWS] = jnp.where(low, pair, 0.0).astype(bf16)
        outer[1, lead : lead + ROWS] = jnp.where(low, 0.0, pair).astype(bf16)
        outer[2, lead : lead + ROWS] = jnp.where(low, pltpu.roll(third, HEAD, 1), 0.0).astype(bf16)
    mixed_grad[total:] = jnp.zeros((8, width), f32)
    bias = key_bias(length[0], total)
    for lead in reversed(range(0, total, ROWS)):
        reach = lead + ROWS
        query_grad = []
        for head in range(3):
            its_keys, its_values = keys[head // 2, :reach], values[head // 2, :reach]
            scores = mm(queries[head, lead:reach], its_keys, 1, 1)
            scores = masked(scores, bias[:, :reach], lead)
            probs = jnp.exp(scores - totals[lead:reach, head : head + 1])
            grad_probs = mm(outer[head, lead:reach], its_values, 1, 1)
            product = probs * grad_probs
            inner = jnp.sum(product, axis=1, keepdims=True)
            grad_scores = (product - probs * inner).astype(bf16)
            query_grad.append(jnp.dot(grad_scores, its_keys, preferred_element_type=f32))
            value_part = mm(probs.astype(bf16), outer[head, lead:reach], 0, 0)
            key_part = mm(grad_scores, queries[head, lead:reach], 0, 0)
            if lead + ROWS == total and head != 1:
                value_grad[head // 2] = value_part
                key_grad[head // 2] = key_part
            else:
                value_grad[head // 2, :reach] += value_part
                key_grad[head // 2, :reach] += key_part
        scale = HEAD**-0.5
        mixed_grad[lead:reach, 0:128] = jnp.where(low, query_grad[0], query_grad[1]) * scale
        mixed_grad[lead:reach, 384:512] = query_grad[2] * scale
    grown = jnp.zeros((8, width), f32)
    for lead in reversed(range(0, total, ROWS)):
        reach = lead + ROWS
        mixed_grad[lead:reach, 128:256] = key_grad[0, lead:reach]
        mixed_grad[lead:reach, 256:384] = value_grad[0, lead:reach]
        mixed_grad[lead:reach, 384:512] = jnp.where(
            low, mixed_grad[lead:reach, 384:512], pltpu.roll(key_grad[1, lead:reach], HEAD, 1)
        )
        mixed_grad[lead:reach, 512:640] = value_grad[1, lead:reach]
        here = projected[lead:reach].astype(f32)
        back = jnp.zeros((ROWS, width), f32)
        parts = []
        for tap in range(3):
            ahead = mixed_grad[lead + tap : reach + tap]
            back += taps[tap : tap + 1] * ahead
            parts.append(jnp.sum(ahead * here, axis=0, keepdims=True))
        grown += jnp.concatenate(parts + [jnp.zeros((5, width), f32)], 0)
        back = back.astype(bf16)
        partial[lead:reach] = mm(back, weight[:, :width], 1, 1).astype(bf16)
        projected_grad[lead:reach] = back
    taps_grad[...] = grown
    turned[0] = x[...].T
    turned[1] = grads[...].T
    for lead in range(0, D, ROWS):
        reach = lead + ROWS
        across = jnp.dot(turned[0, lead:reach], projected_grad[...], preferred_element_type=f32)
        outward = jnp.dot(turned[1, lead:reach], context[...], preferred_element_type=f32)
        weight_grad[lead:reach, :512] = across[:, :512].astype(bf16)
        weight_grad[lead:reach, 512:640] = (across[:, 512:] + outward[:, :128]).astype(bf16)
        weight_grad[lead:reach, 640:] = outward[:, 128:].astype(bf16)


def attention_backward(grads, length, weight, taps, kept):
    x, mixed, projected, context, totals = kept
    total = x.shape[0]
    return attention_call(
        attention_backward_kernel,
        [
            jax.ShapeDtypeStruct((total, D), bf16),
            jax.ShapeDtypeStruct((D, 768), bf16),
            jax.ShapeDtypeStruct((8, 640), f32),
        ],
        [
            pltpu.VMEM((3, total, 128), bf16),
            pltpu.VMEM((2, total, 128), bf16),
            pltpu.VMEM((2, total, 128), bf16),
            pltpu.VMEM((3, total, 128), bf16),
            pltpu.VMEM((2, total, 128), f32),
            pltpu.VMEM((2, total, 128), f32),
            pltpu.VMEM((total + 8, 640), f32),
            pltpu.VMEM((total, 640), bf16),
            pltpu.VMEM((2, D, total), bf16),
        ],
        length,
        grads,
        x,
        weight,
        taps,
        mixed,
        projected,
        context,
        totals,
    )


def ffn_forward(gathered, weights):
    up_mat, down_turned = weights
    hidden = mm(gathered, up_mat, 1, 0)
    active = jnp.square(jnp.maximum(hidden, 0.0)).astype(bf16)
    partial = mm(active, down_turned, 1, 1).astype(bf16).reshape(4, -1, D)
    return partial, (gathered, hidden, active)


def ffn_backward(grad_rows, weights, kept):
    up_mat, down_turned = weights
    gathered, hidden, active = kept
    grad_active = mm(grad_rows, down_turned, 1, 0)
    grad_hidden = (grad_active * 2.0 * jnp.maximum(hidden, 0.0)).astype(bf16)
    partial = mm(grad_hidden, up_mat, 1, 1).astype(bf16).reshape(4, -1, D)
    grad_down = mm(grad_rows, active, 0, 0)
    grad_up = mm(gathered, grad_hidden, 0, 0)
    return partial, [grad_up.astype(bf16), grad_down.astype(bf16)]


LOOK = 512


def lookup_kernel(ids, table, out):
    for part in range(ids.shape[0]):
        total = jnp.zeros((table.shape[0], ids.shape[2]), f32)
        wanted = ids[part]
        row = lax.broadcasted_iota(jnp.int32, (LOOK, ids.shape[2]), 0)
        for lead in range(0, table.shape[1], LOOK):
            hit = jnp.where(row == wanted - lead, 1.0, 0.0).astype(bf16)
            total += jnp.dot(table[:, lead : lead + LOOK], hit, preferred_element_type=f32)
        out[part, 0] = total.astype(bf16)


def lookup(table, ids):
    batches, parts, _, slots = ids.shape
    depth, vocab_rows = table.shape
    return pl.pallas_call(
        lookup_kernel,
        grid=(batches,),
        out_shape=jax.ShapeDtypeStruct((parts, batches, depth, slots), bf16),
        in_specs=[
            pl.BlockSpec((parts, 1, slots), lambda at: (at, 0, 0)),
            pl.BlockSpec((depth, vocab_rows), lambda at: (0, 0)),
        ],
        out_specs=pl.BlockSpec((parts, 1, depth, slots), lambda at: (0, at, 0, 0)),
        compiler_params=pltpu.CompilerParams(vmem_limit_bytes=40 << 20),
    )(ids.reshape(batches * parts, 1, slots), table)


def spread_kernel(ids, grads, base, out, wanted):
    at = pl.program_id(0)
    columns = out.shape[1]
    parts, batches, _, slots = grads.shape

    @pl.when(at == 0)
    def _():
        def turned(group, carry):
            across = ids[pl.ds(pl.multiple_of(group * 8, 8), 8)].T
            for part in range(8):
                wanted[group * 8 + part] = jnp.broadcast_to(
                    across[:, part : part + 1], (slots, 128)
                ).astype(jnp.int16)
            return carry

        lax.fori_loop(0, batches * parts // 8, turned, 0)

    lane = lax.broadcasted_iota(jnp.int16, (slots, 128), 1) + (at * columns).astype(jnp.int16)
    together = min(batches, 4)

    def step(index, total):
        for inner in range(together):
            batch = index * together + inner
            for part in range(parts):
                here = wanted[batch * parts + part]
                hit = jnp.concatenate(
                    [
                        jnp.where(here == lane + jnp.int16(lead), bf16(1), bf16(0))
                        for lead in range(0, columns, 128)
                    ],
                    1,
                )
                total += jnp.dot(grads[part, batch], hit, preferred_element_type=f32)
        return total

    out[...] = lax.fori_loop(0, batches // together, step, base[...].astype(f32))


def spread(grads, ids, base):
    parts, batches, depth, slots = grads.shape
    vocab_rows = base.shape[1]
    columns = 256
    return pl.pallas_call(
        spread_kernel,
        grid=(vocab_rows // columns,),
        out_shape=jax.ShapeDtypeStruct((depth, vocab_rows), f32),
        in_specs=[
            pl.BlockSpec((batches * parts, slots), lambda at: (0, 0)),
            pl.BlockSpec((parts, batches, depth, slots), lambda at: (0, 0, 0, 0)),
            pl.BlockSpec((depth, columns), lambda at: (0, at)),
        ],
        out_specs=pl.BlockSpec((depth, columns), lambda at: (0, at)),
        scratch_shapes=[pltpu.VMEM((batches * parts, slots, 128), jnp.int16)],
        compiler_params=pltpu.CompilerParams(vmem_limit_bytes=32 << 20),
    )(ids.reshape(batches * parts, slots), grads, base)


def summed(landed):
    sums = [
        (one.astype(f32) + two.astype(f32)).astype(bf16)
        for one, two in zip(landed[::2], landed[1::2])
    ]
    return jnp.concatenate(sums, -1)


def over_batch(block):
    return lax.psum_scatter(block, "batch", scatter_dimension=0, tiled=False)


def tie(*values):
    return lax.optimization_barrier(values)


def on_device(
    token_ids,
    seq_lengths,
    embed_table,
    norm_gains,
    final_gain,
    qkv_weight,
    qkv_conv,
    out_weight,
    up_weight,
    down_weight,
    logit_grad,
):
    section = lax.axis_index("section")
    first = section == 0
    core, seq_at, x_at, _ = place()
    quarter = 2 * core + x_at
    me = lax.axis_index("tensor")
    at_batch = lax.axis_index("batch")
    tensor_count = lax.axis_size("tensor")
    batch_count = lax.axis_size("batch")
    section_count = lax.axis_size("section")
    slot_length = token_ids.shape[1]
    shard_rows = slot_length // tensor_count
    local_width = out_weight.shape[1]
    heads_here = local_width // HEAD
    hidden_width = up_weight.shape[2]
    root_scale = math.sqrt(D)
    depth = D // batch_count
    length = seq_lengths[seq_at]
    sequences = token_ids.shape[0]

    table_own = embed_table.astype(bf16).T
    attn_own = packed(qkv_weight[0].astype(bf16), out_weight[0].astype(bf16).T)
    ffn_own = jnp.concatenate([up_weight[0].astype(bf16), down_weight[0].astype(bf16).T], 1)
    attn_all = lax.all_gather(attn_own, "batch", axis=0, tiled=True)
    ffn_all = lax.all_gather(ffn_own, "batch", axis=0, tiled=True)
    table_turned = lax.all_gather(table_own, "batch", axis=0, tiled=True)

    gain_width = final_gain.shape[0]
    whole_at = (section * batch_count + at_batch) * tensor_count + me
    gains_own = jnp.concatenate([norm_gains.reshape(4, gain_width), final_gain[None]])
    gains_own = lax.dynamic_update_slice_in_dim(
        jnp.zeros((5, D), f32), gains_own.astype(bf16).astype(f32), whole_at * gain_width, 1
    )
    taps_own = qkv_conv[0].astype(bf16).astype(f32).transpose(1, 0, 2, 3)
    taps_own = lax.dynamic_update_slice_in_dim(
        jnp.zeros((3, 3, heads_here, HEAD), f32), taps_own, at_batch * qkv_conv.shape[4], 3
    ).reshape(3, 3, local_width)
    small = jnp.concatenate([gains_own, packed(taps_own, jnp.zeros((3, local_width), f32))])
    all_ids, small = batch_gather([token_ids.reshape(-1, 128), small], 5)
    small = jnp.sum(small, 0)

    vocab_rows = embed_table.shape[0]
    owner_start = (section * tensor_count + me) * vocab_rows
    local_ids = all_ids.reshape(batch_count, sequences * 4, 1, shard_rows) - owner_start
    picked = lookup(table_own, local_ids)
    total = plane_reduce(picked.reshape(8, D, shard_rows), 3).astype(bf16)
    embedded, small = batch_trade(total.reshape(batch_count, depth, shard_rows), small, 8)
    gains_all = jnp.sum(small[:, :5], 0)
    final_scale = gains_all[4]
    taps_here = [
        lax.dynamic_index_in_dim(
            small, 4 * (quarter // 2) + 2 * layer + quarter % 2, 0, keepdims=False
        )[5:, :640]
        for layer in range(section_count)
    ]
    embedded = embedded.reshape(D, shard_rows).T

    def ffn_weights(block):
        return block[:, :hidden_width], block[:, hidden_width:]

    first_rows = embedded.astype(f32) * root_scale
    normed = (first_rows * norm_factor(first_rows) * gains_all[0]).astype(bf16)
    gathered, attn_first = group_gather(normed, 1, cargo=("out", 0, [attn_all]))
    partial, attn_kept_first = attention_forward(
        gathered.reshape(-1, D), length, attn_first, taps_here[0]
    )
    gathered, first_middle, block = turn(
        partial, first_rows, gains_all[1], 20, False, cargo=("out", 0, [ffn_all])
    )
    ffn_first = ffn_weights(block)
    partial, ffn_kept_first = ffn_forward(gathered.reshape(-1, D), ffn_first)
    gathered, second_rows, attn_second = turn(
        partial, first_middle, gains_all[2], 21, True, cargo=("out", 1, [attn_all])
    )
    partial, attn_kept_second = attention_forward(
        gathered.reshape(-1, D), length, attn_second, taps_here[1]
    )
    gathered, second_middle, block = turn(
        partial, second_rows, gains_all[3], 24, False, cargo=("out", 1, [ffn_all])
    )
    ffn_second = ffn_weights(block)
    partial, ffn_kept_second = ffn_forward(gathered.reshape(-1, D), ffn_second)

    def halves(blob):
        blob = blob if isinstance(blob, list) else [blob]
        return [one.reshape(batch_count, 2, depth // 2, one.shape[1]) for one in blob]

    final_rows = (second_middle + group_reduce(partial, 2)).astype(bf16).astype(f32)
    normed_final = (final_rows * norm_factor(final_rows) * final_scale).astype(bf16)
    grads_flat = logit_grad.reshape(-1, vocab_rows)
    final_both, grad_parts = head_gather(normed_final, table_turned, grads_flat)
    final_both = final_both.reshape(-1, D)
    valid = (jnp.arange(slot_length)[None, :] < seq_lengths[:, None]).reshape(-1, 1)
    valid = jnp.broadcast_to(valid, (valid.shape[0], 128)).astype(bf16)
    grad_final, head_table = head_reduce(grad_parts, final_both, valid, grads_flat)
    own_at = quarter * shard_rows + jnp.arange(shard_rows)
    grad_final = jnp.where((own_at < length)[:, None], grad_final, 0.0)
    logits = mm(final_both, table_turned, 1, 0).astype(bf16).reshape(sequences, slot_length, -1)
    head_done = lax.psum_scatter(head_table, "batch", scatter_dimension=0, tiled=True)

    grad_rows, grad_final_gain = norm_back(grad_final, final_rows, final_scale)
    gathered = group_gather(grad_rows.astype(bf16), 13).reshape(-1, D)
    partial, blob = ffn_backward(gathered, ffn_second, ffn_kept_second)
    gathered, grad_rows, gain_2f, *landed = turn(
        partial, second_middle, gains_all[3], 22, False, passed=grad_rows,
        cargo=("in", 1, halves(blob)),
    )
    ffn_second_sum = summed(landed)
    partial, blob, taps_second = attention_backward(
        gathered.reshape(-1, D), length, attn_second, taps_here[1], attn_kept_second
    )
    gathered, grad_rows, gain_2a, *landed = turn(
        partial, second_rows, gains_all[2], 23, True, passed=grad_rows,
        cargo=("in", 1, halves(blob)),
    )
    attn_second_sum = summed(landed)
    partial, blob = ffn_backward(gathered.reshape(-1, D), ffn_first, ffn_kept_first)
    partial, head_done = tie(partial, head_done)
    gathered, grad_rows, gain_1f, *landed = turn(
        partial, first_middle, gains_all[1], 25, False, passed=grad_rows,
        cargo=("in", 0, halves(blob)),
    )
    ffn_first_sum = summed(landed)
    partial, blob, taps_first = attention_backward(
        gathered.reshape(-1, D), length, attn_first, taps_here[0], attn_kept_first
    )
    ffn_second_done = over_batch(ffn_second_sum)
    partial, ffn_second_done = tie(partial, ffn_second_done)
    attn_second_done, ffn_first_done = over_batch(attn_second_sum), over_batch(ffn_first_sum)
    grad_norm, *landed = group_reduce(partial, 14, cargo=("in", 0, halves(blob)))
    attn_first_sum = summed(landed)
    grad_norm, gain_1a = norm_back(grad_norm, first_rows, gains_all[0])
    grad_rows = grad_rows + grad_norm
    grad_rows, attn_second_done, ffn_first_done = tie(
        grad_rows, attn_second_done, ffn_first_done
    )

    embed_grad = (grad_rows * root_scale).astype(bf16).T
    def row_at(index, vector):
        padded = jnp.pad(vector, (0, D - vector.shape[0]))[None]
        return jnp.where(jnp.arange(16)[:, None] == index, padded, 0.0)

    vectors = [gain_1a, gain_1f[0], gain_2a[0], gain_2f[0], grad_final_gain, *taps_first[:3], *taps_second[:3]]
    rows = sum(row_at(index, vector) for index, vector in enumerate(vectors))
    traded, rows = batch_trade(embed_grad.reshape(batch_count, depth, shard_rows), rows, 9)
    traded, attn_first_sum = tie(traded, attn_first_sum)
    attn_first_done = over_batch(attn_first_sum)
    gain_sums = jnp.sum(rows[:, :5], 0)
    holders = rows.reshape(2, 4, 16, D)[:, :, 5:11].reshape(2, 4, 2, 3, D)
    taps_sums = jnp.sum(lax.dynamic_index_in_dim(holders, me, 1, keepdims=False), 0)
    taps_sums = lax.dynamic_index_in_dim(taps_sums, section, 0, keepdims=False)
    sums = jnp.concatenate([gain_sums, taps_sums])
    every, sums = plane_and_batch_gather(traded.reshape(D, shard_rows), sums, 10)
    sums, attn_first_done = tie(sums, attn_first_done)
    every = every.reshape(8, batch_count, depth, shard_rows)
    table_done = spread(every, local_ids, head_done).T
    sums = jnp.sum(sums, 0)
    gain_part = lax.dynamic_slice_in_dim(sums[:5], whole_at * gain_width, gain_width, 1)
    gains_done = gain_part[:4].reshape(2, 2, gain_width)
    final_done = gain_part[4]
    conv_part = unpacked(sums[5:8]).reshape(3, 3, heads_here, HEAD).transpose(1, 0, 2, 3)
    conv_done = lax.dynamic_slice_in_dim(
        conv_part, at_batch * qkv_conv.shape[4], qkv_conv.shape[4], 3
    )[None]
    def placed(first_part, second_part):
        keep = jnp.where(first, first_part, second_part)
        got = lax.ppermute(jnp.where(first, second_part, first_part), "section", [(0, 1), (1, 0)])
        return jnp.where(
            first, jnp.concatenate([keep, got], 0), jnp.concatenate([got, keep], 0)
        ).astype(f32)

    attn_done = placed(attn_first_done, attn_second_done)
    ffn_done = placed(ffn_first_done, ffn_second_done)
    qkv_done = unpacked(attn_done)[None]
    out_done = jnp.concatenate([attn_done[:, 640:], attn_done[:, 576:640]], 1).T[None]
    up_done = ffn_done[:, :hidden_width][None]
    down_done = ffn_done[:, hidden_width:].T[None]
    return (
        logits,
        table_done,
        gains_done,
        final_done,
        qkv_done,
        conv_done,
        out_done,
        up_done,
        down_done,
    )


def solution(mesh):
    in_specs = (
        P("batch", None),
        P("batch"),
        P(("section", "tensor"), "batch"),
        P(None, None, ("section", "batch", "tensor")),
        P(("section", "batch", "tensor")),
        P("section", "batch", None, "tensor"),
        P("section", None, None, "tensor", "batch"),
        P("section", "tensor", "batch"),
        P("section", "batch", "tensor"),
        P("section", "tensor", "batch"),
        P("batch", None, ("section", "tensor")),
    )
    out_specs = (
        P("batch", None, ("section", "tensor")),
        P(("section", "tensor"), "batch"),
        P(None, None, ("section", "batch", "tensor")),
        P(("section", "batch", "tensor")),
        P("section", "batch", None, "tensor"),
        P("section", None, None, "tensor", "batch"),
        P("section", "tensor", "batch"),
        P("section", "batch", "tensor"),
        P("section", "tensor", "batch"),
    )
    return jax.shard_map(
        on_device, mesh=mesh, in_specs=in_specs, out_specs=out_specs, check_vma=False
    )
```

```python
import functools
import math

import jax
import jax.numpy as jnp
from jax import lax
from jax.experimental import pallas as pl
from jax.experimental.pallas import tpu as pltpu
from jax.sharding import PartitionSpec as P

D = 768
HEAD = 64

norm_eps = 1e-06
masked_score = -1e30
bf16 = jnp.bfloat16
f32 = jnp.float32


def mm(left, right, left_dim, right_dim):
    return lax.dot_general(
        left, right, (((left_dim,), (right_dim,)), ((), ())), preferred_element_type=f32
    )


def norm_factor(rows):
    return lax.rsqrt(jnp.mean(rows * rows, axis=-1, keepdims=True) + norm_eps)


def norm_back(grad, rows, gain):
    factor = norm_factor(rows)
    scaled = grad * gain
    inner = jnp.mean(scaled * rows, axis=-1, keepdims=True)
    grad_rows = factor * scaled - rows * (factor * factor * factor * inner)
    return grad_rows, jnp.sum(grad * rows * factor, axis=0, keepdims=True)


MESH = pl.DeviceIdType.MESH


def place():
    core = lax.axis_index("section")
    tensor = lax.axis_index("tensor")
    return core, tensor // 2, tensor % 2, tensor


def remote(src, dst, send, recv, device):
    return pltpu.make_async_remote_copy(
        src_ref=src,
        dst_ref=dst,
        send_sem=send,
        recv_sem=recv,
        device_id=device,
        device_id_type=MESH,
    )


def greet(devices):
    barrier = pltpu.get_barrier_semaphore()
    for device in devices:
        pl.semaphore_signal(barrier, inc=1, device_id=device, device_id_type=MESH)
    pl.semaphore_wait(barrier, len(devices))


def comm_call(
    body, out_shape, scratch, collective_id, *operands, cargo=None, streamed=(), room=6
):
    shapes = list(out_shape) if isinstance(out_shape, (list, tuple)) else [out_shape]
    in_specs = [pl.BlockSpec(memory_space=pltpu.VMEM)] * len(operands)
    out_specs = [pl.BlockSpec(memory_space=pltpu.VMEM)] * len(shapes)
    scratch = list(scratch)
    operands = operands + tuple(streamed)
    in_specs += [pl.BlockSpec(memory_space=pl.ANY)] * len(streamed)
    count_in, count_out = len(operands), len(shapes)
    loads = 0
    if cargo is not None:
        kind, items = cargo
        loads = len(items)
        arrays = []
        landing = []
        for layer, array, lead, width in items:
            if not any(array is one for one in arrays):
                arrays.append(array)
            if kind == "out":
                landing.append(jax.ShapeDtypeStruct((array.shape[0], width), array.dtype))
            else:
                batches, _, rows, _ = array.shape
                landing += [jax.ShapeDtypeStruct((batches, rows, width), array.dtype)] * 2
        operands = operands + tuple(arrays)
        in_specs += [pl.BlockSpec(memory_space=pl.ANY)] * len(arrays)
        shapes += landing
        out_specs += [pl.BlockSpec(memory_space=pl.ANY)] * len(landing)
        scratch += [pltpu.SemaphoreType.DMA((loads, 3))] * 2

    def kernel(*refs):
        ins, rest = refs[: len(operands)], refs[len(operands) :]
        outs, rest = rest[: len(shapes)], rest[len(shapes) :]
        if cargo is None:
            body(*ins, *outs, *rest)
            return
        send, recv = rest[-2:]
        made = Outward if kind == "out" else Inward
        lands_each = len(landing) // loads

        def load():
            loaded = []
            for at, (layer, array, lead, width) in enumerate(items):
                source = ins[count_in + [array is one for one in arrays].index(True)]
                if width < array.shape[-1]:
                    cut = (slice(None),) * (len(array.shape) - 1) + (pl.ds(lead, width),)
                    source = source.at[cut]
                lands = outs[count_out + lands_each * at : count_out + lands_each * (at + 1)]
                loaded.append(made(layer, source, lands, send.at[at], recv.at[at]))
            return loaded

        body(*ins[:count_in], *outs[:count_out], *rest[:-2], load=load)

    results = pl.pallas_call(
        kernel,
        out_shape=shapes,
        in_specs=in_specs,
        out_specs=out_specs,
        scratch_shapes=scratch,
        compiler_params=pltpu.CompilerParams(
            collective_id=collective_id, has_side_effects=True, vmem_limit_bytes=room << 20
        ),
    )(*operands)
    return results if len(shapes) > 1 else results[0]


class Outward:
    def __init__(self, layer, source, landing, send, recv):
        core, y, _, tensor = place()
        target = landing[0]
        self.layer, self.core, self.y = layer, core, y
        self.near = remote(source, target, send.at[0], recv.at[0], {"section": 1 - core})
        self.far = remote(
            source, target, send.at[1], recv.at[0], {"section": y, "tensor": tensor + 2 - 4 * y}
        )
        self.local = pltpu.make_async_copy(source, target, recv.at[1])

    def start(self):
        @pl.when(self.core == self.layer)
        def _():
            self.far.start()

            @pl.when(self.y == self.layer)
            def _():
                self.local.start()

            @pl.when(self.y != self.layer)
            def _():
                self.near.start()

    def wait(self):
        stays = (self.core == self.layer) & (self.y == self.layer)

        @pl.when(stays)
        def _():
            self.local.wait()

        @pl.when(jnp.logical_not(stays))
        def _():
            self.far.wait_recv()

        @pl.when(self.core == self.layer)
        def _():
            self.far.wait_send()

            @pl.when(self.y != self.layer)
            def _():
                self.near.wait_send()


class Inward:
    def __init__(self, layer, source, landing, send, recv):
        core, y, _, tensor = place()
        above = tensor + 2 - 4 * y
        self.near = core == y
        self.to_core = remote(
            source.at[:, 1 - y], landing[0], send.at[0], recv.at[0], {"section": 1 - core}
        )
        self.to_same = remote(
            source.at[:, 1 - y], landing[0], send.at[0], recv.at[0], {"tensor": above}
        )
        self.to_both = remote(
            source.at[:, y],
            landing[1],
            send.at[1],
            recv.at[1],
            {"section": 1 - core, "tensor": above},
        )
        self.fill = pltpu.make_async_copy(source.at[:, y], landing[1], recv.at[2])

    def start(self):
        @pl.when(self.near)
        def _():
            self.to_core.start()
            self.fill.start()

        @pl.when(jnp.logical_not(self.near))
        def _():
            self.to_same.start()
            self.to_both.start()

    def wait(self):
        @pl.when(self.near)
        def _():
            self.to_same.wait_recv()
            self.fill.wait()
            self.to_core.wait_send()

        @pl.when(jnp.logical_not(self.near))
        def _():
            self.to_core.wait_recv()
            self.to_both.wait_recv()
            self.to_same.wait_send()
            self.to_both.wait_send()


def greet_group(other, beside, load):
    if load is None:
        greet([other, beside])
        return []
    _, y, _, tensor = place()
    above = tensor + 2 - 4 * y
    greet([other, beside, {"section": 0, "tensor": above}, {"section": 1, "tensor": above}])
    made = load()
    for one in made:
        one.start()
    return made


PIECES = 4


def group_gather_kernel(own, out, send, recv, load=None):
    core, _, x, tensor = place()
    other = {"section": 1 - core}
    beside = {"tensor": tensor + 1 - 2 * x}
    here = 2 * core + x
    there = 2 * core + 1 - x
    cargo = greet_group(other, beside, load)
    piece = own.shape[0] // PIECES
    cuts = [pl.ds(at * piece, piece) for at in range(PIECES)]
    across = []
    for at, cut in enumerate(cuts):
        copy = remote(own.at[cut], out.at[here, cut], send.at[at], recv.at[at], beside)
        copy.start()
        across.append(copy)
    last = 2 * PIECES
    direct = remote(own, out.at[here], send.at[last], recv.at[last], other)
    direct.start()
    out[here] = own[...]
    passed = []
    for at, cut in enumerate(cuts):
        across[at].wait_recv()
        copy = remote(
            out.at[there, cut],
            out.at[there, cut],
            send.at[PIECES + at],
            recv.at[PIECES + at],
            other,
        )
        copy.start()
        passed.append(copy)
    for copy in across:
        copy.wait_send()
    direct.wait()
    for copy in passed:
        copy.wait()
    for one in cargo:
        one.wait()


def group_gather(rows, collective_id, cargo=None):
    count, width = rows.shape
    return comm_call(
        group_gather_kernel,
        jax.ShapeDtypeStruct((4, count, width), rows.dtype),
        [pltpu.SemaphoreType.DMA((2 * PIECES + 1,))] * 2,
        collective_id,
        rows,
        cargo=cargo,
    )


def group_reduce_kernel(parts, out, near, far, mixed, send, recv, load=None):
    core, _, x, tensor = place()
    other = {"section": 1 - core}
    beside = {"tensor": tensor + 1 - 2 * x}
    here = 2 * core + x
    there = 2 * core + 1 - x
    over_here = 2 * (1 - core) + x
    over_there = 2 * (1 - core) + 1 - x
    cargo = greet_group(other, beside, load)
    piece = out.shape[0] // PIECES
    cuts = [pl.ds(at * piece, piece) for at in range(PIECES)]
    first = []
    for at, cut in enumerate(cuts):
        copy = remote(
            parts.at[over_there, cut], near.at[1, cut], send.at[at], recv.at[at], other
        )
        copy.start()
        first.append(copy)
    last = 2 * PIECES
    direct = remote(parts.at[over_here], near.at[0], send.at[last], recv.at[last], other)
    direct.start()
    across = []
    for at, cut in enumerate(cuts):
        first[at].wait_recv()
        mixed[cut] = (parts[there, cut].astype(f32) + near[1, cut].astype(f32)).astype(bf16)
        copy = remote(
            mixed.at[cut], far.at[cut], send.at[PIECES + at], recv.at[PIECES + at], beside
        )
        copy.start()
        across.append(copy)
    direct.wait()
    for at, cut in enumerate(cuts):
        across[at].wait_recv()
        out[cut] = (
            parts[here, cut].astype(f32) + near[0, cut].astype(f32) + far[cut].astype(f32)
        )
    for copy in first + across:
        copy.wait_send()
    for one in cargo:
        one.wait()


def group_reduce(parts, collective_id, cargo=None):
    parts = parts.reshape(4, -1, D)
    _, count, width = parts.shape
    return comm_call(
        group_reduce_kernel,
        jax.ShapeDtypeStruct((count, width), f32),
        [
            pltpu.VMEM((2, count, width), bf16),
            pltpu.VMEM((count, width), bf16),
            pltpu.VMEM((count, width), bf16),
        ]
        + [pltpu.SemaphoreType.DMA((2 * PIECES + 1,))] * 2,
        collective_id,
        parts,
        cargo=cargo,
    )


def turn_kernel(backward, rounded, *refs, load=None):
    if backward:
        parts, rows, gain, passed, gathered, fresh, gain_grad, near, far, mixed, send, recv = refs
    else:
        parts, rows, gain, gathered, fresh, near, far, mixed, send, recv = refs
    core, _, x, tensor = place()
    other = {"section": 1 - core}
    beside = {"tensor": tensor + 1 - 2 * x}
    here = 2 * core + x
    there = 2 * core + 1 - x
    over_here = 2 * (1 - core) + x
    over_there = 2 * (1 - core) + 1 - x
    cargo = greet_group(other, beside, load)
    piece = fresh.shape[0] // PIECES
    cuts = [pl.ds(at * piece, piece) for at in range(PIECES)]

    def start(src, dst, kind, at, device):
        index = kind * PIECES + at
        made = remote(src, dst, send.at[index], recv.at[index], device)
        made.start()
        return made

    handed, direct = [], []
    for at, cut in enumerate(cuts):
        handed.append(start(parts.at[over_there, cut], near.at[1, cut], 0, at, other))
        direct.append(start(parts.at[over_here, cut], near.at[0, cut], 1, at, other))
    across = []
    for at, cut in enumerate(cuts):
        handed[at].wait_recv()
        mixed[cut] = (parts[there, cut].astype(f32) + near[1, cut].astype(f32)).astype(bf16)
        across.append(start(mixed.at[cut], far.at[cut], 2, at, beside))
    out_across, out_direct, onward = [], [], []
    gains = gain[...]
    for at in range(PIECES + 1):
        if at < PIECES:
            cut = cuts[at]
            direct[at].wait_recv()
            across[at].wait_recv()
            total = (
                parts[here, cut].astype(f32) + near[0, cut].astype(f32) + far[cut].astype(f32)
            )
            held = rows[cut]
            if backward:
                factor = norm_factor(held)
                scaled = total * gains
                inner = jnp.mean(scaled * held, axis=-1, keepdims=True)
                new = passed[cut] + factor * scaled - held * (factor * factor * factor * inner)
                gain_part = jnp.sum(total * held * factor, axis=0, keepdims=True)
                gain_grad[...] = gain_part if at == 0 else gain_grad[...] + gain_part
                if rounded:
                    new = new.astype(bf16).astype(f32)
                shown = new.astype(bf16)
            else:
                new = held + total
                if rounded:
                    new = new.astype(bf16).astype(f32)
                shown = (new * norm_factor(new) * gains).astype(bf16)
            fresh[cut] = new
            gathered[here, cut] = shown
            out_across.append(start(gathered.at[here, cut], gathered.at[here, cut], 3, at, beside))
            out_direct.append(start(gathered.at[here, cut], gathered.at[here, cut], 4, at, other))
        if at >= 1:
            cut = cuts[at - 1]
            out_across[at - 1].wait_recv()
            onward.append(start(gathered.at[there, cut], gathered.at[there, cut], 5, at - 1, other))
    for made in handed + direct + across + out_across:
        made.wait_send()
    for made in out_direct + onward:
        made.wait()
    for one in cargo:
        one.wait()


def turn(parts, rows, gain, collective_id, rounded, passed=None, cargo=None):
    parts = parts.reshape(4, -1, D)
    _, count, width = parts.shape
    backward = passed is not None
    shapes = [
        jax.ShapeDtypeStruct((4, count, width), bf16),
        jax.ShapeDtypeStruct((count, width), f32),
    ]
    operands = [parts, rows, gain.reshape(1, width)]
    if backward:
        shapes.append(jax.ShapeDtypeStruct((1, width), f32))
        operands.append(passed)
    return comm_call(
        functools.partial(turn_kernel, backward, rounded),
        shapes,
        [
            pltpu.VMEM((2, count, width), bf16),
            pltpu.VMEM((count, width), bf16),
            pltpu.VMEM((count, width), bf16),
        ]
        + [pltpu.SemaphoreType.DMA((6 * PIECES,))] * 2,
        collective_id,
        *operands,
        cargo=cargo,
    )


def plane_peers():
    core, y, x, tensor = place()
    return [
        {"section": 1 - core},
        {"tensor": tensor + 1 - 2 * x},
        {"tensor": tensor + 2 - 4 * y},
    ]


def plane_gather_kernel(own, out, send, recv):
    greet(plane_peers())
    plane_exchange(own, out, send, recv)


class Chores:
    def __init__(self, units=()):
        self.units = list(units)

    def some(self, count):
        for _ in range(min(count, len(self.units))):
            self.units.pop(0)()

    def rest(self):
        self.some(len(self.units))


def stream(count, source_at, buffers, sems, work):
    def fetch(at):
        return pltpu.make_async_copy(source_at(at), buffers.at[at % 2], sems.at[at % 2])

    def unit(at):
        fetch(at).wait()
        work(at, buffers.at[at % 2])
        if at + 2 < count:
            fetch(at + 2).start()

    for at in range(min(2, count)):
        fetch(at).start()
    return [functools.partial(unit, at) for at in range(count)]


def plane_exchange(own, out, send, recv, chores=Chores()):
    core, y, x, _ = place()
    other, beside, above = plane_peers()
    half = own.shape[0] // 2
    cut = [pl.ds(0, half), pl.ds(half, half)]

    def slot(along_y, along_x):
        return 4 * along_y + 2 * core + along_x

    me = slot(y, x)
    at_x, at_y, at_both = slot(y, 1 - x), slot(1 - y, x), slot(1 - y, 1 - x)

    def copy(src, where, index, device):
        made = remote(src, out.at[where], send.at[index], recv.at[index], device)
        made.start()
        return made

    to_x = [remote(own.at[cut[h]], out.at[me, cut[h]], send.at[h], recv.at[h], beside) for h in (0, 1)]
    to_y = [remote(own.at[cut[h]], out.at[me, cut[h]], send.at[2 + h], recv.at[2 + h], above) for h in (0, 1)]
    to_x[0].start()
    to_y[1].start()
    to_x[1].start()
    to_y[0].start()
    pending = [copy(own, me, 4, other)]
    out[me] = own[...]

    def onward(where, h, index, device):
        made = remote(
            out.at[where, cut[h]], out.at[where, cut[h]], send.at[index], recv.at[index], device
        )
        made.start()
        return made

    chores.some(2)
    to_x[0].wait_recv()
    diag_y = onward(at_x, 0, 5, above)
    pending.append(onward(at_x, 0, 6, other))
    to_y[1].wait_recv()
    diag_x = onward(at_y, 1, 7, beside)
    pending.append(onward(at_y, 1, 8, other))
    chores.some(2)
    to_x[1].wait_recv()
    pending.append(onward(at_x, 1, 9, other))
    to_y[0].wait_recv()
    pending.append(onward(at_y, 0, 10, other))
    chores.some(2)
    diag_y.wait_recv()
    pending.append(onward(at_both, 0, 11, other))
    diag_x.wait_recv()
    pending.append(onward(at_both, 1, 12, other))
    chores.rest()
    for made in to_x + to_y + [diag_x, diag_y]:
        made.wait_send()
    for made in pending:
        made.wait()


def head_gather_kernel(own, table, grads, out, parts, buffers, sems, send, recv):
    greet(plane_peers())
    rows = own.shape[0]

    def work(at, block):
        parts[at] = mm(block[...], table[...], 1, 1).astype(bf16)

    chores = Chores(
        stream(8, lambda at: grads.at[pl.ds(rows * at, rows)], buffers, sems, work)
    )
    plane_exchange(own, out, send, recv, chores)


def head_gather(rows, table, grads):
    count, width = rows.shape
    return comm_call(
        head_gather_kernel,
        [jax.ShapeDtypeStruct((8, count, width), bf16)] * 2,
        [
            pltpu.VMEM((2, count, grads.shape[1]), bf16),
            pltpu.SemaphoreType.DMA((2,)),
        ]
        + [pltpu.SemaphoreType.DMA((13,))] * 2,
        7,
        rows,
        table,
        streamed=[grads],
        room=40,
    )


def plane_reduce_kernel(parts, out, *scratch):
    greet(plane_peers())
    plane_sum(parts, out, *scratch)


def plane_sum(
    parts, out, near, mixed, via_x, via_y, from_x, from_y, hop_x, hop_y, send, recv, chores=Chores()
):
    core, y, x, _ = place()
    other, beside, above = plane_peers()
    half = out.shape[0] // 2
    cut = [pl.ds(0, half), pl.ds(half, half)]

    def slot(at_core, along_y, along_x):
        return 4 * along_y + 2 * at_core + along_x

    targets = [(1 - y, 1 - x), (y, 1 - x), (1 - y, x), (y, x)]
    handed = []
    for index, (along_y, along_x) in enumerate(targets):
        made = remote(
            parts.at[slot(1 - core, along_y, along_x)],
            near.at[index],
            send.at[index],
            recv.at[index],
            other,
        )
        made.start()
        handed.append(made)

    def joined(index, where=slice(None)):
        along_y, along_x = targets[index]
        mine = parts[slot(core, along_y, along_x), where]
        return mine.astype(f32) + near[index, where].astype(f32)

    def start(src, dst, index, device):
        made = remote(src, dst, send.at[index], recv.at[index], device)
        made.start()
        return made

    handed[0].wait_recv()
    mixed[0] = joined(0).astype(bf16)
    diag_x = start(mixed.at[0, cut[0]], via_x, 4, beside)
    diag_y = start(mixed.at[0, cut[1]], via_y, 5, above)
    handed[1].wait_recv()
    mixed[1] = joined(1).astype(bf16)
    straight_x = start(mixed.at[1, cut[0]], from_x.at[cut[0]], 6, beside)
    handed[2].wait_recv()
    mixed[2] = joined(2).astype(bf16)
    straight_y = start(mixed.at[2, cut[1]], from_y.at[cut[1]], 7, above)
    chores.some(2)
    diag_x.wait_recv()
    hop_y[...] = (mixed[2, cut[0]].astype(f32) + via_x[...].astype(f32)).astype(bf16)
    turned_y = start(hop_y, from_y.at[cut[0]], 8, above)
    diag_y.wait_recv()
    hop_x[...] = (mixed[1, cut[1]].astype(f32) + via_y[...].astype(f32)).astype(bf16)
    turned_x = start(hop_x, from_x.at[cut[1]], 9, beside)
    chores.rest()
    handed[3].wait_recv()
    straight_x.wait_recv()
    turned_y.wait_recv()
    out[cut[0]] = joined(3, cut[0]) + from_x[cut[0]].astype(f32) + from_y[cut[0]].astype(f32)
    straight_y.wait_recv()
    turned_x.wait_recv()
    out[cut[1]] = joined(3, cut[1]) + from_x[cut[1]].astype(f32) + from_y[cut[1]].astype(f32)
    for made in handed + [diag_x, diag_y, straight_x, straight_y, turned_x, turned_y]:
        made.wait_send()


def plane_scratch(count, width):
    half = count // 2
    return [
        pltpu.VMEM((4, count, width), bf16),
        pltpu.VMEM((3, count, width), bf16),
        pltpu.VMEM((half, width), bf16),
        pltpu.VMEM((half, width), bf16),
        pltpu.VMEM((count, width), bf16),
        pltpu.VMEM((count, width), bf16),
        pltpu.VMEM((half, width), bf16),
        pltpu.VMEM((half, width), bf16),
    ] + [pltpu.SemaphoreType.DMA((10,))] * 2


def plane_reduce(parts, collective_id):
    _, count, width = parts.shape
    return comm_call(
        plane_reduce_kernel,
        jax.ShapeDtypeStruct((count, width), f32),
        plane_scratch(count, width),
        collective_id,
        parts,
    )


def head_reduce_kernel(parts, rows, valid, grads, out, table_grad, held, buffers, sems, *scratch):
    greet(plane_peers())
    width = buffers.shape[2]
    for lead in range(0, rows.shape[1], 128):
        held[:, lead : lead + 128] = rows[:, lead : lead + 128] * valid[...]

    def work(at, block):
        table_grad[:, width * at : width * at + width] = mm(held[...], block[...], 0, 0).astype(bf16)

    steps = grads.shape[1] // width
    chores = Chores(
        stream(steps, lambda at: grads.at[:, pl.ds(width * at, width)], buffers, sems, work)
    )
    plane_sum(parts, out, *scratch, chores=chores)


def head_reduce(parts, rows, valid, grads):
    _, count, width = parts.shape
    step = 512
    return comm_call(
        head_reduce_kernel,
        [
            jax.ShapeDtypeStruct((count, width), f32),
            jax.ShapeDtypeStruct((width, grads.shape[1]), bf16),
        ],
        [
            pltpu.VMEM(rows.shape, bf16),
            pltpu.VMEM((2, rows.shape[0], step), bf16),
            pltpu.SemaphoreType.DMA((2,)),
        ]
        + plane_scratch(count, width),
        4,
        parts,
        rows,
        valid,
        streamed=[grads],
        room=42,
    )


def batch_peers(count):
    me = lax.axis_index("batch")
    return [{"batch": lax.rem(me + step, count)} for step in range(1, count)]


def batch_exchange(count, ins, outs, send, recv):
    me = lax.axis_index("batch")
    copies = []
    for index, peer in enumerate(batch_peers(count)):
        for kind in range(len(ins)):
            at = index * len(ins) + kind
            copies.append(remote(ins[kind], outs[kind].at[me], send.at[at], recv.at[at], peer))
            copies[-1].start()
    for kind in range(len(ins)):
        outs[kind][me] = ins[kind][...]
    return copies


def batch_gather_kernel(count, *refs):
    kinds = (len(refs) - 2) // 2
    greet(batch_peers(count))
    for copy in batch_exchange(count, refs[:kinds], refs[kinds : 2 * kinds], *refs[2 * kinds :]):
        copy.wait()


def batch_gather(blocks, collective_id):
    count = lax.axis_size("batch")
    return comm_call(
        functools.partial(batch_gather_kernel, count),
        [jax.ShapeDtypeStruct((count,) + block.shape, block.dtype) for block in blocks],
        [pltpu.SemaphoreType.DMA(((count - 1) * len(blocks),))] * 2,
        collective_id,
        *blocks,
    )


def plane_and_batch_kernel(count, own, few, out, few_out, send, recv, few_send, few_recv):
    greet(plane_peers() + batch_peers(count))
    copies = batch_exchange(count, [few], [few_out], few_send, few_recv)
    plane_exchange(own, out, send, recv)
    for copy in copies:
        copy.wait()


def plane_and_batch_gather(block, few, collective_id):
    count = lax.axis_size("batch")
    return comm_call(
        functools.partial(plane_and_batch_kernel, count),
        [
            jax.ShapeDtypeStruct((8,) + block.shape, block.dtype),
            jax.ShapeDtypeStruct((count,) + few.shape, few.dtype),
        ],
        [pltpu.SemaphoreType.DMA((13,))] * 2 + [pltpu.SemaphoreType.DMA((count - 1,))] * 2,
        collective_id,
        block,
        few,
    )


def batch_trade_kernel(count, leads, parts, *refs, load=None):
    pieces, refs = refs[: len(leads)], refs[len(leads) :]
    out, few_out, few, send, recv, few_send, few_recv = refs
    few[...] = jnp.zeros(few.shape, few.dtype)
    for lead, piece in zip(leads, pieces):
        few[lead : lead + piece.shape[0], : piece.shape[1]] = piece[...]
    me = lax.axis_index("batch")
    core, y, _, tensor = place()
    peers = plane_peers() + batch_peers(count)
    if load is not None:
        peers.append({"section": 1 - core, "tensor": tensor + 2 - 4 * y})
    greet(peers)
    cargo = load() if load is not None else []
    for one in cargo:
        one.start()
    copies = []
    for index, peer in enumerate(batch_peers(count)):
        copies.append(
            remote(parts.at[peer["batch"]], out.at[me], send.at[index], recv.at[index], peer)
        )
        copies[-1].start()
    out[me] = parts[me]
    plane_exchange(few, few_out, few_send, few_recv)
    for copy in copies:
        copy.wait()
    for one in cargo:
        one.wait()


def batch_trade(parts, pieces, rows, collective_id, cargo=None):
    count = parts.shape[0]
    return comm_call(
        functools.partial(batch_trade_kernel, count, [lead for lead, _ in pieces]),
        [
            jax.ShapeDtypeStruct(parts.shape, parts.dtype),
            jax.ShapeDtypeStruct((8, rows, D), f32),
        ],
        [pltpu.VMEM((rows, D), f32)]
        + [pltpu.SemaphoreType.DMA((count - 1,))] * 2
        + [pltpu.SemaphoreType.DMA((13,))] * 2,
        collective_id,
        parts,
        *[piece for _, piece in pieces],
        cargo=cargo,
    )


ROWS = 256

PACKED = ((0, 0), (0, 1), (1, 0), (1, 1), (2, 0), (2, 1), (0, 2), (1, 2), (2, 2))


def packed(blocks, out):
    cuts = [blocks[:, kind, HEAD * head : HEAD * head + HEAD] for kind, head in PACKED]
    return jnp.concatenate(cuts + [out[:, 2 * HEAD :], out[:, : 2 * HEAD]], 1)


def unpacked(block):
    place_of = {pair: at * HEAD for at, pair in enumerate(PACKED)}
    kinds = []
    for kind in range(3):
        cuts = [
            block[:, place_of[kind, head] : place_of[kind, head] + HEAD] for head in range(3)
        ]
        kinds.append(jnp.concatenate(cuts, 1))
    return jnp.stack(kinds, 1)


def attention_heads(mixed, queries, keys, values):
    low = lax.broadcasted_iota(jnp.int32, (mixed.shape[0], 128), 1) < HEAD
    tile = [mixed[:, 128 * at : 128 * at + 128] for at in range(5)]
    scaled = tile[0] * (HEAD**-0.5)
    queries[0] = jnp.where(low, scaled, 0.0).astype(bf16)
    queries[1] = jnp.where(low, 0.0, scaled).astype(bf16)
    queries[2] = jnp.where(low, tile[3] * (HEAD**-0.5), 0.0).astype(bf16)
    keys[0] = tile[1].astype(bf16)
    keys[1] = pltpu.roll(tile[3], HEAD, 1).astype(bf16)
    values[0] = tile[2].astype(bf16)
    values[1] = tile[4].astype(bf16)


def key_bias(length, total):
    at = lax.broadcasted_iota(jnp.int32, (1, total), 1)
    return jnp.where(at < length, 0.0, masked_score)


def masked(scores, bias, lead):
    scores = scores + bias
    row = lax.broadcasted_iota(jnp.int32, (ROWS, ROWS), 0)
    column = lax.broadcasted_iota(jnp.int32, (ROWS, ROWS), 1)
    last = jnp.where(column <= row, scores[:, lead:], masked_score)
    return last if lead == 0 else jnp.concatenate([scores[:, :lead], last], 1)


def attention_forward_kernel(
    length, x, weight, taps, partial, mixed_out, projected_out, context, totals, projected, queries, keys, values
):
    total = x.shape[0]
    width = 5 * 128
    projected[:8] = jnp.zeros((8, width), f32)
    for lead in range(0, total, ROWS):
        block = jnp.dot(x[lead : lead + ROWS], weight[:, :width], preferred_element_type=f32)
        projected[lead + 8 : lead + 8 + ROWS] = block
        projected_out[lead : lead + ROWS] = block.astype(bf16)
    for lead in range(0, total, ROWS):
        mixed = taps[0:1] * projected[lead + 8 : lead + 8 + ROWS]
        mixed += taps[1:2] * projected[lead + 7 : lead + 7 + ROWS]
        mixed += taps[2:3] * projected[lead + 6 : lead + 6 + ROWS]
        mixed = mixed.astype(bf16)
        mixed_out[lead : lead + ROWS] = mixed
        rows = pl.ds(lead, ROWS)
        attention_heads(
            mixed.astype(f32), queries.at[:, rows], keys.at[:, rows], values.at[:, rows]
        )
    bias = key_bias(length[0], total)
    lane = lax.broadcasted_iota(jnp.int32, (ROWS, 128), 1)
    low = lane < HEAD
    for lead in range(0, total, ROWS):
        reach = lead + ROWS
        found = []
        log_sums = jnp.zeros((ROWS, 128), f32)
        for head in range(3):
            scores = mm(queries[head, lead:reach], keys[head // 2, :reach], 1, 1)
            scores = masked(scores, bias[:, :reach], lead)
            peak = jnp.max(scores, axis=1, keepdims=True)
            raised = jnp.exp(scores - peak)
            weight_sum = jnp.sum(raised, axis=1, keepdims=True)
            probs = (raised * (1.0 / weight_sum)).astype(bf16)
            found.append(
                jnp.dot(probs, values[head // 2, :reach], preferred_element_type=f32)
            )
            log_sums = jnp.where(lane == head, peak + jnp.log(weight_sum), log_sums)
        totals[lead:reach] = log_sums
        joined = jnp.concatenate(
            [
                jnp.where(low, 0.0, pltpu.roll(found[2], HEAD, 1)),
                jnp.where(low, found[0], found[1]),
            ],
            1,
        ).astype(bf16)
        context[lead:reach] = joined
        partial[lead:reach] = mm(joined, weight[:, 512:768], 1, 1).astype(bf16)


def attention_call(body, out_shape, scratch, room, length, *operands):
    whole = pl.BlockSpec(memory_space=pltpu.VMEM)
    return pl.pallas_call(
        body,
        out_shape=out_shape,
        in_specs=[pl.BlockSpec(memory_space=pltpu.SMEM)] + [whole] * len(operands),
        out_specs=[whole] * len(out_shape),
        scratch_shapes=scratch,
        compiler_params=pltpu.CompilerParams(vmem_limit_bytes=room << 20),
    )(length.reshape(1), *operands)


def attention_forward(x, length, weight, taps):
    total = x.shape[0]
    partial, *kept = attention_call(
        attention_forward_kernel,
        [
            jax.ShapeDtypeStruct((total, D), bf16),
            jax.ShapeDtypeStruct((total, 640), bf16),
            jax.ShapeDtypeStruct((total, 640), bf16),
            jax.ShapeDtypeStruct((total, 256), bf16),
            jax.ShapeDtypeStruct((total, 128), f32),
        ],
        [
            pltpu.VMEM((total + 8, 640), f32),
            pltpu.VMEM((3, total, 128), bf16),
            pltpu.VMEM((2, total, 128), bf16),
            pltpu.VMEM((2, total, 128), bf16),
        ],
        14,
        length,
        x,
        weight,
        taps,
    )
    return partial, (x, *kept)


def attention_backward_kernel(
    length,
    grads,
    x,
    weight,
    taps,
    mixed,
    projected,
    context,
    totals,
    partial,
    weight_grad,
    taps_grad,
    queries,
    keys,
    values,
    outer,
    key_grad,
    value_grad,
    mixed_grad,
    projected_grad,
    turned,
):
    total = x.shape[0]
    width = 5 * 128
    low = lax.broadcasted_iota(jnp.int32, (ROWS, 128), 1) < HEAD
    for lead in range(0, total, ROWS):
        rows = pl.ds(lead, ROWS)
        attention_heads(
            mixed[lead : lead + ROWS].astype(f32),
            queries.at[:, rows],
            keys.at[:, rows],
            values.at[:, rows],
        )
        block = jnp.dot(grads[lead : lead + ROWS], weight[:, 512:768], preferred_element_type=f32)
        third, pair = block[:, :128], block[:, 128:]
        outer[0, lead : lead + ROWS] = jnp.where(low, pair, 0.0).astype(bf16)
        outer[1, lead : lead + ROWS] = jnp.where(low, 0.0, pair).astype(bf16)
        outer[2, lead : lead + ROWS] = jnp.where(low, pltpu.roll(third, HEAD, 1), 0.0).astype(bf16)
    mixed_grad[total:] = jnp.zeros((8, width), f32)
    bias = key_bias(length[0], total)
    for lead in reversed(range(0, total, ROWS)):
        reach = lead + ROWS
        query_grad = []
        for head in range(3):
            its_keys, its_values = keys[head // 2, :reach], values[head // 2, :reach]
            scores = mm(queries[head, lead:reach], its_keys, 1, 1)
            scores = masked(scores, bias[:, :reach], lead)
            probs = jnp.exp(scores - totals[lead:reach, head : head + 1])
            grad_probs = mm(outer[head, lead:reach], its_values, 1, 1)
            product = probs * grad_probs
            inner = jnp.sum(product, axis=1, keepdims=True)
            grad_scores = (product - probs * inner).astype(bf16)
            query_grad.append(jnp.dot(grad_scores, its_keys, preferred_element_type=f32))
            value_part = mm(probs.astype(bf16), outer[head, lead:reach], 0, 0)
            key_part = mm(grad_scores, queries[head, lead:reach], 0, 0)
            if lead + ROWS == total and head != 1:
                value_grad[head // 2] = value_part
                key_grad[head // 2] = key_part
            else:
                value_grad[head // 2, :reach] += value_part
                key_grad[head // 2, :reach] += key_part
        scale = HEAD**-0.5
        mixed_grad[lead:reach, 0:128] = jnp.where(low, query_grad[0], query_grad[1]) * scale
        mixed_grad[lead:reach, 384:512] = query_grad[2] * scale
    grown = jnp.zeros((8, width), f32)
    for lead in reversed(range(0, total, ROWS)):
        reach = lead + ROWS
        mixed_grad[lead:reach, 128:256] = key_grad[0, lead:reach]
        mixed_grad[lead:reach, 256:384] = value_grad[0, lead:reach]
        mixed_grad[lead:reach, 384:512] = jnp.where(
            low, mixed_grad[lead:reach, 384:512], pltpu.roll(key_grad[1, lead:reach], HEAD, 1)
        )
        mixed_grad[lead:reach, 512:640] = value_grad[1, lead:reach]
        here = projected[lead:reach].astype(f32)
        back = jnp.zeros((ROWS, width), f32)
        parts = []
        for tap in range(3):
            ahead = mixed_grad[lead + tap : reach + tap]
            back += taps[tap : tap + 1] * ahead
            parts.append(jnp.sum(ahead * here, axis=0, keepdims=True))
        grown += jnp.concatenate(parts + [jnp.zeros((5, width), f32)], 0)
        back = back.astype(bf16)
        partial[lead:reach] = mm(back, weight[:, :width], 1, 1).astype(bf16)
        projected_grad[lead:reach] = back
    taps_grad[...] = grown
    turned[0] = x[...].T
    turned[1] = grads[...].T
    for lead in range(0, D, ROWS):
        reach = lead + ROWS
        across = jnp.dot(turned[0, lead:reach], projected_grad[...], preferred_element_type=f32)
        outward = jnp.dot(turned[1, lead:reach], context[...], preferred_element_type=f32)
        weight_grad[lead:reach, :512] = across[:, :512].astype(bf16)
        weight_grad[lead:reach, 512:640] = (across[:, 512:] + outward[:, :128]).astype(bf16)
        weight_grad[lead:reach, 640:] = outward[:, 128:].astype(bf16)


def attention_backward(grads, length, weight, taps, kept):
    x, mixed, projected, context, totals = kept
    total = x.shape[0]
    return attention_call(
        attention_backward_kernel,
        [
            jax.ShapeDtypeStruct((total, D), bf16),
            jax.ShapeDtypeStruct((D, 768), bf16),
            jax.ShapeDtypeStruct((8, 640), f32),
        ],
        [
            pltpu.VMEM((3, total, 128), bf16),
            pltpu.VMEM((2, total, 128), bf16),
            pltpu.VMEM((2, total, 128), bf16),
            pltpu.VMEM((3, total, 128), bf16),
            pltpu.VMEM((2, total, 128), f32),
            pltpu.VMEM((2, total, 128), f32),
            pltpu.VMEM((total + 8, 640), f32),
            pltpu.VMEM((total, 640), bf16),
            pltpu.VMEM((2, D, total), bf16),
        ],
        20,
        length,
        grads,
        x,
        weight,
        taps,
        mixed,
        projected,
        context,
        totals,
    )


def ffn_forward_kernel(x, up, *refs):
    downs, partial = refs[:-1], refs[-1]
    for lead in range(0, x.shape[0], ROWS):
        hidden = jnp.dot(x[lead : lead + ROWS], up[...], preferred_element_type=f32)
        active = jnp.square(jnp.maximum(hidden, 0.0)).astype(bf16)
        total, first = 0.0, 0
        for down in downs:
            width = down.shape[1]
            total += mm(active[:, first : first + width], down[...], 1, 1)
            first += width
        partial[lead : lead + ROWS] = total.astype(bf16)


def ffn_backward_kernel(grads, x, up, *refs):
    downs = refs[:-6]
    partial, up_grad, down_grad, hidden_grad, active, turned = refs[-6:]
    for lead in range(0, x.shape[0], ROWS):
        rows = pl.ds(lead, ROWS)
        hidden = jnp.dot(x[rows], up[...], preferred_element_type=f32)
        positive = jnp.maximum(hidden, 0.0)
        active[rows] = jnp.square(positive).astype(bf16)
        back = [jnp.dot(grads[rows], down[...], preferred_element_type=f32) for down in downs]
        back = back[0] if len(back) == 1 else jnp.concatenate(back, 1)
        back = (back * 2.0 * positive).astype(bf16)
        hidden_grad[rows] = back
        partial[rows] = mm(back, up[...], 1, 1).astype(bf16)
    turned[0] = x[...].T
    turned[1] = grads[...].T
    for lead in range(0, D, ROWS):
        rows = pl.ds(lead, ROWS)
        up_grad[rows] = jnp.dot(
            turned[0, rows], hidden_grad[...], preferred_element_type=f32
        ).astype(bf16)
        down_grad[rows] = jnp.dot(
            turned[1, rows], active[...], preferred_element_type=f32
        ).astype(bf16)


def local_call(body, out_shape, scratch, *operands):
    whole = pl.BlockSpec(memory_space=pltpu.VMEM)
    return pl.pallas_call(
        body,
        out_shape=out_shape,
        in_specs=[whole] * len(operands),
        out_specs=[whole] * len(out_shape),
        scratch_shapes=scratch,
        compiler_params=pltpu.CompilerParams(vmem_limit_bytes=14 << 20),
    )(*operands)


def ffn_forward(x, weights):
    up, downs = weights
    (partial,) = local_call(
        ffn_forward_kernel, [jax.ShapeDtypeStruct(x.shape, bf16)], [], x, up, *downs
    )
    return partial


def ffn_backward(grads, weights, x):
    up, downs = weights
    return local_call(
        ffn_backward_kernel,
        [
            jax.ShapeDtypeStruct(x.shape, bf16),
            jax.ShapeDtypeStruct(up.shape, bf16),
            jax.ShapeDtypeStruct(up.shape, bf16),
        ],
        [
            pltpu.VMEM((x.shape[0], up.shape[1]), bf16),
            pltpu.VMEM((x.shape[0], up.shape[1]), bf16),
            pltpu.VMEM((2, D, x.shape[0]), bf16),
        ],
        grads,
        x,
        up,
        *downs,
    )


LOOK = 512


def lookup_kernel(ids, table, out):
    for part in range(ids.shape[0]):
        total = jnp.zeros((table.shape[0], ids.shape[2]), f32)
        wanted = ids[part]
        row = lax.broadcasted_iota(jnp.int32, (LOOK, ids.shape[2]), 0)
        for lead in range(0, table.shape[1], LOOK):
            hit = jnp.where(row == wanted - lead, 1.0, 0.0).astype(bf16)
            total += jnp.dot(table[:, lead : lead + LOOK], hit, preferred_element_type=f32)
        out[part, 0] = total.astype(bf16)


def lookup(table, ids):
    batches, parts, _, slots = ids.shape
    depth, vocab_rows = table.shape
    return pl.pallas_call(
        lookup_kernel,
        grid=(batches,),
        out_shape=jax.ShapeDtypeStruct((parts, batches, depth, slots), bf16),
        in_specs=[
            pl.BlockSpec((parts, 1, slots), lambda at: (at, 0, 0)),
            pl.BlockSpec((depth, vocab_rows), lambda at: (0, 0)),
        ],
        out_specs=pl.BlockSpec((parts, 1, depth, slots), lambda at: (0, at, 0, 0)),
        compiler_params=pltpu.CompilerParams(vmem_limit_bytes=40 << 20),
    )(ids.reshape(batches * parts, 1, slots), table)


def spread_kernel(ids, grads, base, out, wanted):
    at = pl.program_id(0)
    columns = out.shape[1]
    parts, batches, _, slots = grads.shape

    @pl.when(at == 0)
    def _():
        def turned(group, carry):
            across = ids[pl.ds(pl.multiple_of(group * 8, 8), 8)].T
            for part in range(8):
                wanted[group * 8 + part] = jnp.broadcast_to(
                    across[:, part : part + 1], (slots, 128)
                ).astype(jnp.int16)
            return carry

        lax.fori_loop(0, batches * parts // 8, turned, 0)

    lane = lax.broadcasted_iota(jnp.int16, (slots, 128), 1) + (at * columns).astype(jnp.int16)
    together = min(batches, 4)

    def step(index, total):
        for inner in range(together):
            batch = index * together + inner
            for part in range(parts):
                here = wanted[batch * parts + part]
                hit = jnp.concatenate(
                    [
                        jnp.where(here == lane + jnp.int16(lead), bf16(1), bf16(0))
                        for lead in range(0, columns, 128)
                    ],
                    1,
                )
                total += jnp.dot(grads[part, batch], hit, preferred_element_type=f32)
        return total

    out[...] = lax.fori_loop(0, batches // together, step, base[...].astype(f32))


def spread(grads, ids, base):
    parts, batches, depth, slots = grads.shape
    vocab_rows = base.shape[1]
    columns = 256
    return pl.pallas_call(
        spread_kernel,
        grid=(vocab_rows // columns,),
        out_shape=jax.ShapeDtypeStruct((depth, vocab_rows), f32),
        in_specs=[
            pl.BlockSpec((batches * parts, slots), lambda at: (0, 0)),
            pl.BlockSpec((parts, batches, depth, slots), lambda at: (0, 0, 0, 0)),
            pl.BlockSpec((depth, columns), lambda at: (0, at)),
        ],
        out_specs=pl.BlockSpec((depth, columns), lambda at: (0, at)),
        scratch_shapes=[pltpu.VMEM((batches * parts, slots, 128), jnp.int16)],
        compiler_params=pltpu.CompilerParams(vmem_limit_bytes=32 << 20),
    )(ids.reshape(batches * parts, slots), grads, base)


def summed(landed):
    sums = [
        (one.astype(f32) + two.astype(f32)).astype(bf16)
        for one, two in zip(landed[::2], landed[1::2])
    ]
    return jnp.concatenate(sums, -1)


def over_batch(block):
    return lax.psum_scatter(block, "batch", scatter_dimension=0, tiled=False)


def tie(*values):
    return lax.optimization_barrier(values)


def on_device(
    token_ids,
    seq_lengths,
    embed_table,
    norm_gains,
    final_gain,
    qkv_weight,
    qkv_conv,
    out_weight,
    up_weight,
    down_weight,
    logit_grad,
):
    section = lax.axis_index("section")
    first = section == 0
    core, seq_at, x_at, _ = place()
    quarter = 2 * core + x_at
    me = lax.axis_index("tensor")
    at_batch = lax.axis_index("batch")
    tensor_count = lax.axis_size("tensor")
    batch_count = lax.axis_size("batch")
    section_count = lax.axis_size("section")
    slot_length = token_ids.shape[1]
    shard_rows = slot_length // tensor_count
    local_width = out_weight.shape[1]
    heads_here = local_width // HEAD
    hidden_width = up_weight.shape[2]
    root_scale = math.sqrt(D)
    depth = D // batch_count
    length = seq_lengths[seq_at]
    sequences = token_ids.shape[0]

    table_own = embed_table.astype(bf16).T
    attn_own = packed(qkv_weight[0].astype(bf16), out_weight[0].astype(bf16).T)
    ffn_own = jnp.concatenate([up_weight[0].astype(bf16), down_weight[0].astype(bf16).T], 1)
    attn_all = lax.all_gather(attn_own, "batch", axis=0, tiled=True)
    ffn_all = lax.all_gather(ffn_own, "batch", axis=0, tiled=True)
    table_turned = lax.all_gather(table_own, "batch", axis=0, tiled=True)

    gain_width = final_gain.shape[0]
    whole_at = (section * batch_count + at_batch) * tensor_count + me
    gains_own = jnp.concatenate([norm_gains.reshape(4, gain_width), final_gain[None]])
    gains_own = lax.dynamic_update_slice_in_dim(
        jnp.zeros((5, D), f32), gains_own.astype(bf16).astype(f32), whole_at * gain_width, 1
    )
    taps_own = qkv_conv[0].astype(bf16).astype(f32).transpose(1, 0, 2, 3)
    taps_own = lax.dynamic_update_slice_in_dim(
        jnp.zeros((3, 3, heads_here, HEAD), f32), taps_own, at_batch * qkv_conv.shape[4], 3
    ).reshape(3, 3, local_width)
    small = jnp.concatenate([gains_own, packed(taps_own, jnp.zeros((3, local_width), f32))])
    all_ids, small = batch_gather([token_ids.reshape(-1, 128), small], 5)
    small = jnp.sum(small, 0)

    vocab_rows = embed_table.shape[0]
    owner_start = (section * tensor_count + me) * vocab_rows
    local_ids = all_ids.reshape(batch_count, sequences * 4, 1, shard_rows) - owner_start
    picked = lookup(table_own, local_ids)
    total = plane_reduce(picked.reshape(8, D, shard_rows), 3).astype(bf16)
    embedded, small = batch_trade(
        total.reshape(batch_count, depth, shard_rows), [(0, small)], 16, 8
    )
    gains_all = jnp.sum(small[:, :5], 0)
    final_scale = gains_all[4]
    taps_here = [
        lax.dynamic_index_in_dim(
            small, 4 * (quarter // 2) + 2 * layer + quarter % 2, 0, keepdims=False
        )[5:8, :640]
        for layer in range(section_count)
    ]
    embedded = embedded.reshape(D, shard_rows).T

    part = hidden_width // 2
    first_rows = embedded.astype(f32) * root_scale
    normed = (first_rows * norm_factor(first_rows) * gains_all[0]).astype(bf16)
    gathered, attn_first = group_gather(normed, 1, cargo=("out", [(0, attn_all, 0, D)]))
    partial, attn_kept_first = attention_forward(gathered.reshape(-1, D), length, attn_first, taps_here[0])
    gathered, first_middle, up, down = turn(
        partial,
        first_rows,
        gains_all[1],
        20,
        False,
        cargo=("out", [(0, ffn_all, 0, hidden_width), (0, ffn_all, hidden_width, hidden_width)]),
    )
    ffn_first = (up, [down])
    ffn_kept_first = gathered.reshape(-1, D)
    partial = ffn_forward(ffn_kept_first, ffn_first)
    gathered, second_rows, attn_second, down_one = turn(
        partial,
        first_middle,
        gains_all[2],
        21,
        True,
        cargo=("out", [(1, attn_all, 0, D), (1, ffn_all, hidden_width, part)]),
    )
    partial, attn_kept_second = attention_forward(
        gathered.reshape(-1, D), length, attn_second, taps_here[1]
    )
    gathered, second_middle, up, down_two = turn(
        partial,
        second_rows,
        gains_all[3],
        24,
        False,
        cargo=("out", [(1, ffn_all, 0, hidden_width), (1, ffn_all, hidden_width + part, part)]),
    )
    ffn_second = (up, [down_one, down_two])
    ffn_kept_second = gathered.reshape(-1, D)
    partial = ffn_forward(ffn_kept_second, ffn_second)

    def halves(blob):
        return blob.reshape(batch_count, 2, depth // 2, blob.shape[1])

    final_rows = (second_middle + group_reduce(partial, 2)).astype(bf16).astype(f32)
    normed_final = (final_rows * norm_factor(final_rows) * final_scale).astype(bf16)
    grads_flat = logit_grad.reshape(-1, vocab_rows)
    final_both, grad_parts = head_gather(normed_final, table_turned, grads_flat)
    final_both = final_both.reshape(-1, D)
    valid = (jnp.arange(slot_length)[None, :] < seq_lengths[:, None]).reshape(-1, 1)
    valid = jnp.broadcast_to(valid, (valid.shape[0], 128)).astype(bf16)
    grad_final, head_table = head_reduce(grad_parts, final_both, valid, grads_flat)
    own_at = quarter * shard_rows + jnp.arange(shard_rows)
    grad_final = jnp.where((own_at < length)[:, None], grad_final, 0.0)
    logits = mm(final_both, table_turned, 1, 0).astype(bf16).reshape(sequences, slot_length, -1)
    head_done = lax.psum_scatter(head_table, "batch", scatter_dimension=0, tiled=True)

    grad_rows, grad_final_gain = norm_back(grad_final, final_rows, final_scale)
    gathered = group_gather(grad_rows.astype(bf16), 13).reshape(-1, D)
    partial, up, down = ffn_backward(gathered, ffn_second, ffn_kept_second)
    up, down = halves(up), halves(down)
    gathered, grad_rows, gain_2f, *landed_second = turn(
        partial,
        second_middle,
        gains_all[3],
        22,
        False,
        passed=grad_rows,
        cargo=("in", [(1, up, 0, hidden_width), (1, down, 0, part)]),
    )
    partial, blob, taps_second = attention_backward(
        gathered.reshape(-1, D), length, attn_second, taps_here[1], attn_kept_second
    )
    gathered, grad_rows, gain_2a, *landed = turn(
        partial,
        second_rows,
        gains_all[2],
        23,
        True,
        passed=grad_rows,
        cargo=("in", [(1, down, part, part), (1, halves(blob), 0, D)]),
    )
    second_sum = summed(landed_second + landed)
    partial, up, down = ffn_backward(gathered.reshape(-1, D), ffn_first, ffn_kept_first)
    up, down = halves(up), halves(down)
    gathered, grad_rows, gain_1f, *landed_first = turn(
        partial,
        first_middle,
        gains_all[1],
        25,
        False,
        passed=grad_rows,
        cargo=("in", [(0, up, 0, hidden_width), (0, down, 0, part)]),
    )
    taps_again, second_sum, head_done, gain_1f = tie(
        taps_here[0], second_sum, head_done, gain_1f
    )
    partial, blob, taps_first = attention_backward(
        gathered.reshape(-1, D), length, attn_first, taps_again, attn_kept_first
    )
    second_done = over_batch(second_sum)
    grad_norm, *landed = group_reduce(
        partial, 14, cargo=("in", [(0, down, part, part), (0, halves(blob), 0, D)])
    )
    first_sum = summed(landed_first + landed)
    grad_norm, gain_1a = norm_back(grad_norm, first_rows, gains_all[0])
    grad_rows = grad_rows + grad_norm

    embed_grad = (grad_rows * root_scale).astype(bf16).T
    pieces = [(0, gain_1a), (1, gain_1f), (2, gain_2a), (3, gain_2f), (4, grad_final_gain)]
    traded, rows = batch_trade(
        embed_grad.reshape(batch_count, depth, shard_rows),
        pieces + [(8, taps_first), (16, taps_second)],
        32,
        9,
    )
    rows, first_sum, second_done = tie(rows, first_sum, second_done)
    first_done = over_batch(first_sum)
    gain_sums = jnp.sum(rows[:, :5], 0)
    holders = rows.reshape(2, 4, 32, D)[:, :, 8:24].reshape(2, 4, 2, 8, D)
    taps_sums = jnp.sum(lax.dynamic_index_in_dim(holders, me, 1, keepdims=False), 0)
    taps_sums = lax.dynamic_index_in_dim(taps_sums, section, 0, keepdims=False)[:3]
    sums = jnp.concatenate([gain_sums, taps_sums])
    every, sums = plane_and_batch_gather(traded.reshape(D, shard_rows), sums, 10)
    sums, first_done = tie(sums, first_done)
    every = every.reshape(8, batch_count, depth, shard_rows)
    table_done = spread(every, local_ids, head_done).T
    sums = jnp.sum(sums, 0)
    gain_part = lax.dynamic_slice_in_dim(sums[:5], whole_at * gain_width, gain_width, 1)
    gains_done = gain_part[:4].reshape(2, 2, gain_width)
    final_done = gain_part[4]
    conv_part = unpacked(sums[5:8]).reshape(3, 3, heads_here, HEAD).transpose(1, 0, 2, 3)
    conv_done = lax.dynamic_slice_in_dim(
        conv_part, at_batch * qkv_conv.shape[4], qkv_conv.shape[4], 3
    )[None]
    def placed(first_part, second_part):
        keep = jnp.where(first, first_part, second_part)
        got = lax.ppermute(jnp.where(first, second_part, first_part), "section", [(0, 1), (1, 0)])
        return jnp.where(
            first, jnp.concatenate([keep, got], 0), jnp.concatenate([got, keep], 0)
        ).astype(f32)

    done = placed(first_done, second_done)
    up_done = done[:, :hidden_width][None]
    down_done = done[:, hidden_width : 2 * hidden_width].T[None]
    attn_done = done[:, 2 * hidden_width :]
    qkv_done = unpacked(attn_done)[None]
    out_done = jnp.concatenate([attn_done[:, 640:], attn_done[:, 576:640]], 1).T[None]
    return (
        logits,
        table_done,
        gains_done,
        final_done,
        qkv_done,
        conv_done,
        out_done,
        up_done,
        down_done,
    )


def solution(mesh):
    in_specs = (
        P("batch", None),
        P("batch"),
        P(("section", "tensor"), "batch"),
        P(None, None, ("section", "batch", "tensor")),
        P(("section", "batch", "tensor")),
        P("section", "batch", None, "tensor"),
        P("section", None, None, "tensor", "batch"),
        P("section", "tensor", "batch"),
        P("section", "batch", "tensor"),
        P("section", "tensor", "batch"),
        P("batch", None, ("section", "tensor")),
    )
    out_specs = (
        P("batch", None, ("section", "tensor")),
        P(("section", "tensor"), "batch"),
        P(None, None, ("section", "batch", "tensor")),
        P(("section", "batch", "tensor")),
        P("section", "batch", None, "tensor"),
        P("section", None, None, "tensor", "batch"),
        P("section", "tensor", "batch"),
        P("section", "batch", "tensor"),
        P("section", "tensor", "batch"),
    )
    return jax.shard_map(
        on_device, mesh=mesh, in_specs=in_specs, out_specs=out_specs, check_vma=False
    )
```

```python
import functools
import itertools
import math

import jax
import jax.numpy as jnp
from jax import lax
from jax.experimental import pallas as pl
from jax.experimental.pallas import tpu as pltpu
from jax.sharding import PartitionSpec as P

D = 768
HEAD = 64

norm_eps = 1e-06
masked_score = -1e30
bf16 = jnp.bfloat16
f32 = jnp.float32


def mm(left, right, left_dim, right_dim):
    return lax.dot_general(
        left, right, (((left_dim,), (right_dim,)), ((), ())), preferred_element_type=f32
    )


def norm_factor(rows):
    return lax.rsqrt(jnp.mean(rows * rows, axis=-1, keepdims=True) + norm_eps)


def norm_back(grad, rows, gain):
    factor = norm_factor(rows)
    scaled = grad * gain
    inner = jnp.mean(scaled * rows, axis=-1, keepdims=True)
    grad_rows = factor * scaled - rows * (factor * factor * factor * inner)
    return grad_rows, jnp.sum(grad * rows * factor, axis=0, keepdims=True)


MESH = pl.DeviceIdType.MESH


def place():
    core = lax.axis_index("section")
    tensor = lax.axis_index("tensor")
    return core, tensor // 2, tensor % 2, tensor


def remote(src, dst, send, recv, device):
    return pltpu.make_async_remote_copy(
        src_ref=src,
        dst_ref=dst,
        send_sem=send,
        recv_sem=recv,
        device_id=device,
        device_id_type=MESH,
    )


def greet(devices):
    barrier = pltpu.get_barrier_semaphore()
    for device in devices:
        pl.semaphore_signal(barrier, inc=1, device_id=device, device_id_type=MESH)
    pl.semaphore_wait(barrier, len(devices))


def comm_call(
    body, out_shape, scratch, collective_id, *operands, cargo=None, streamed=(), room=6
):
    shapes = list(out_shape) if isinstance(out_shape, (list, tuple)) else [out_shape]
    in_specs = [pl.BlockSpec(memory_space=pltpu.VMEM)] * len(operands)
    out_specs = [pl.BlockSpec(memory_space=pltpu.VMEM)] * len(shapes)
    scratch = list(scratch)
    operands = operands + tuple(streamed)
    in_specs += [pl.BlockSpec(memory_space=pl.ANY)] * len(streamed)
    count_in, count_out = len(operands), len(shapes)
    loads = 0
    if cargo is not None:
        kind, items = cargo
        loads = len(items)
        arrays = []
        landing = []
        for layer, array, lead, width in items:
            if not any(array is one for one in arrays):
                arrays.append(array)
            if kind == "out":
                landing.append(jax.ShapeDtypeStruct((array.shape[0], width), array.dtype))
            else:
                batches, _, rows, _ = array.shape
                landing += [jax.ShapeDtypeStruct((batches, rows, width), array.dtype)] * 2
        operands = operands + tuple(arrays)
        in_specs += [pl.BlockSpec(memory_space=pl.ANY)] * len(arrays)
        shapes += landing
        out_specs += [pl.BlockSpec(memory_space=pl.ANY)] * len(landing)
        scratch += [pltpu.SemaphoreType.DMA((loads, 3))] * 2

    def kernel(*refs):
        ins, rest = refs[: len(operands)], refs[len(operands) :]
        outs, rest = rest[: len(shapes)], rest[len(shapes) :]
        if cargo is None:
            body(*ins, *outs, *rest)
            return
        send, recv = rest[-2:]
        made = Outward if kind == "out" else Inward
        lands_each = len(landing) // loads

        def load():
            loaded = []
            for at, (layer, array, lead, width) in enumerate(items):
                source = ins[count_in + [array is one for one in arrays].index(True)]
                if width < array.shape[-1]:
                    cut = (slice(None),) * (len(array.shape) - 1) + (pl.ds(lead, width),)
                    source = source.at[cut]
                lands = outs[count_out + lands_each * at : count_out + lands_each * (at + 1)]
                loaded.append(made(layer, source, lands, send.at[at], recv.at[at]))
            return loaded

        body(*ins[:count_in], *outs[:count_out], *rest[:-2], load=load)

    results = pl.pallas_call(
        kernel,
        out_shape=shapes,
        in_specs=in_specs,
        out_specs=out_specs,
        scratch_shapes=scratch,
        compiler_params=pltpu.CompilerParams(
            collective_id=collective_id, has_side_effects=True, vmem_limit_bytes=room << 20
        ),
    )(*operands)
    return results if len(shapes) > 1 else results[0]


class Outward:
    def __init__(self, layer, source, landing, send, recv):
        core, y, _, tensor = place()
        target = landing[0]
        self.layer, self.core, self.y = layer, core, y
        self.near = remote(source, target, send.at[0], recv.at[0], {"section": 1 - core})
        self.far = remote(
            source, target, send.at[1], recv.at[0], {"section": y, "tensor": tensor + 2 - 4 * y}
        )
        self.local = pltpu.make_async_copy(source, target, recv.at[1])

    def start(self):
        @pl.when(self.core == self.layer)
        def _():
            self.far.start()

            @pl.when(self.y == self.layer)
            def _():
                self.local.start()

            @pl.when(self.y != self.layer)
            def _():
                self.near.start()

    def wait(self):
        stays = (self.core == self.layer) & (self.y == self.layer)

        @pl.when(stays)
        def _():
            self.local.wait()

        @pl.when(jnp.logical_not(stays))
        def _():
            self.far.wait_recv()

        @pl.when(self.core == self.layer)
        def _():
            self.far.wait_send()

            @pl.when(self.y != self.layer)
            def _():
                self.near.wait_send()


class Inward:
    def __init__(self, layer, source, landing, send, recv):
        core, y, _, tensor = place()
        above = tensor + 2 - 4 * y
        self.near = core == y
        self.to_core = remote(
            source.at[:, 1 - y], landing[0], send.at[0], recv.at[0], {"section": 1 - core}
        )
        self.to_same = remote(
            source.at[:, 1 - y], landing[0], send.at[0], recv.at[0], {"tensor": above}
        )
        self.to_both = remote(
            source.at[:, y],
            landing[1],
            send.at[1],
            recv.at[1],
            {"section": 1 - core, "tensor": above},
        )
        self.fill = pltpu.make_async_copy(source.at[:, y], landing[1], recv.at[2])

    def start(self):
        @pl.when(self.near)
        def _():
            self.to_core.start()
            self.fill.start()

        @pl.when(jnp.logical_not(self.near))
        def _():
            self.to_same.start()
            self.to_both.start()

    def wait(self):
        @pl.when(self.near)
        def _():
            self.to_same.wait_recv()
            self.fill.wait()
            self.to_core.wait_send()

        @pl.when(jnp.logical_not(self.near))
        def _():
            self.to_core.wait_recv()
            self.to_both.wait_recv()
            self.to_same.wait_send()
            self.to_both.wait_send()


def greet_group(other, beside, load):
    if load is None:
        greet([other, beside])
        return []
    _, y, _, tensor = place()
    above = tensor + 2 - 4 * y
    greet([other, beside, {"section": 0, "tensor": above}, {"section": 1, "tensor": above}])
    made = load()
    for one in made:
        one.start()
    return made


PIECES = 4


def group_gather_kernel(own, out, send, recv, load=None):
    core, _, x, tensor = place()
    other = {"section": 1 - core}
    beside = {"tensor": tensor + 1 - 2 * x}
    here = 2 * core + x
    there = 2 * core + 1 - x
    cargo = greet_group(other, beside, load)
    piece = own.shape[0] // PIECES
    cuts = [pl.ds(at * piece, piece) for at in range(PIECES)]
    across = []
    for at, cut in enumerate(cuts):
        copy = remote(own.at[cut], out.at[here, cut], send.at[at], recv.at[at], beside)
        copy.start()
        across.append(copy)
    last = 2 * PIECES
    direct = remote(own, out.at[here], send.at[last], recv.at[last], other)
    direct.start()
    out[here] = own[...]
    passed = []
    for at, cut in enumerate(cuts):
        across[at].wait_recv()
        copy = remote(
            out.at[there, cut],
            out.at[there, cut],
            send.at[PIECES + at],
            recv.at[PIECES + at],
            other,
        )
        copy.start()
        passed.append(copy)
    for copy in across:
        copy.wait_send()
    direct.wait()
    for copy in passed:
        copy.wait()
    for one in cargo:
        one.wait()


def group_gather(rows, collective_id, cargo=None):
    count, width = rows.shape
    return comm_call(
        group_gather_kernel,
        jax.ShapeDtypeStruct((4, count, width), rows.dtype),
        [pltpu.SemaphoreType.DMA((2 * PIECES + 1,))] * 2,
        collective_id,
        rows,
        cargo=cargo,
    )


def group_reduce_kernel(parts, out, near, far, mixed, send, recv, load=None):
    core, _, x, tensor = place()
    other = {"section": 1 - core}
    beside = {"tensor": tensor + 1 - 2 * x}
    here = 2 * core + x
    there = 2 * core + 1 - x
    over_here = 2 * (1 - core) + x
    over_there = 2 * (1 - core) + 1 - x
    cargo = greet_group(other, beside, load)
    piece = out.shape[0] // PIECES
    cuts = [pl.ds(at * piece, piece) for at in range(PIECES)]
    first = []
    for at, cut in enumerate(cuts):
        copy = remote(
            parts.at[over_there, cut], near.at[1, cut], send.at[at], recv.at[at], other
        )
        copy.start()
        first.append(copy)
    last = 2 * PIECES
    direct = remote(parts.at[over_here], near.at[0], send.at[last], recv.at[last], other)
    direct.start()
    across = []
    for at, cut in enumerate(cuts):
        first[at].wait_recv()
        mixed[cut] = (parts[there, cut].astype(f32) + near[1, cut].astype(f32)).astype(bf16)
        copy = remote(
            mixed.at[cut], far.at[cut], send.at[PIECES + at], recv.at[PIECES + at], beside
        )
        copy.start()
        across.append(copy)
    direct.wait()
    for at, cut in enumerate(cuts):
        across[at].wait_recv()
        out[cut] = (
            parts[here, cut].astype(f32) + near[0, cut].astype(f32) + far[cut].astype(f32)
        )
    for copy in first + across:
        copy.wait_send()
    for one in cargo:
        one.wait()


def group_reduce(parts, collective_id, cargo=None):
    parts = parts.reshape(4, -1, D)
    _, count, width = parts.shape
    return comm_call(
        group_reduce_kernel,
        jax.ShapeDtypeStruct((count, width), f32),
        [
            pltpu.VMEM((2, count, width), bf16),
            pltpu.VMEM((count, width), bf16),
            pltpu.VMEM((count, width), bf16),
        ]
        + [pltpu.SemaphoreType.DMA((2 * PIECES + 1,))] * 2,
        collective_id,
        parts,
        cargo=cargo,
    )


def turn_kernel(backward, rounded, *refs, load=None):
    if backward:
        parts, rows, gain, passed, gathered, fresh, gain_grad, near, far, mixed, send, recv = refs
    else:
        parts, rows, gain, gathered, fresh, near, far, mixed, send, recv = refs
    core, _, x, tensor = place()
    other = {"section": 1 - core}
    beside = {"tensor": tensor + 1 - 2 * x}
    here = 2 * core + x
    there = 2 * core + 1 - x
    over_here = 2 * (1 - core) + x
    over_there = 2 * (1 - core) + 1 - x
    cargo = greet_group(other, beside, load)
    piece = fresh.shape[0] // PIECES
    cuts = [pl.ds(at * piece, piece) for at in range(PIECES)]

    def start(src, dst, kind, at, device):
        index = kind * PIECES + at
        made = remote(src, dst, send.at[index], recv.at[index], device)
        made.start()
        return made

    handed, direct = [], []
    for at, cut in enumerate(cuts):
        handed.append(start(parts.at[over_there, cut], near.at[1, cut], 0, at, other))
        direct.append(start(parts.at[over_here, cut], near.at[0, cut], 1, at, other))
    across = []
    for at, cut in enumerate(cuts):
        handed[at].wait_recv()
        mixed[cut] = (parts[there, cut].astype(f32) + near[1, cut].astype(f32)).astype(bf16)
        across.append(start(mixed.at[cut], far.at[cut], 2, at, beside))
    out_across, out_direct, onward = [], [], []
    gains = gain[...]
    for at in range(PIECES + 1):
        if at < PIECES:
            cut = cuts[at]
            direct[at].wait_recv()
            across[at].wait_recv()
            total = (
                parts[here, cut].astype(f32) + near[0, cut].astype(f32) + far[cut].astype(f32)
            )
            held = rows[cut]
            if backward:
                factor = norm_factor(held)
                scaled = total * gains
                inner = jnp.mean(scaled * held, axis=-1, keepdims=True)
                new = passed[cut] + factor * scaled - held * (factor * factor * factor * inner)
                gain_part = jnp.sum(total * held * factor, axis=0, keepdims=True)
                gain_grad[...] = gain_part if at == 0 else gain_grad[...] + gain_part
                if rounded:
                    new = new.astype(bf16).astype(f32)
                shown = new.astype(bf16)
            else:
                new = held + total
                if rounded:
                    new = new.astype(bf16).astype(f32)
                shown = (new * norm_factor(new) * gains).astype(bf16)
            fresh[cut] = new
            gathered[here, cut] = shown
            out_across.append(start(gathered.at[here, cut], gathered.at[here, cut], 3, at, beside))
            out_direct.append(start(gathered.at[here, cut], gathered.at[here, cut], 4, at, other))
        if at >= 1:
            cut = cuts[at - 1]
            out_across[at - 1].wait_recv()
            onward.append(start(gathered.at[there, cut], gathered.at[there, cut], 5, at - 1, other))
    for made in handed + direct + across + out_across:
        made.wait_send()
    for made in out_direct + onward:
        made.wait()
    for one in cargo:
        one.wait()


def turn(parts, rows, gain, collective_id, rounded, passed=None, cargo=None):
    parts = parts.reshape(4, -1, D)
    _, count, width = parts.shape
    backward = passed is not None
    shapes = [
        jax.ShapeDtypeStruct((4, count, width), bf16),
        jax.ShapeDtypeStruct((count, width), f32),
    ]
    operands = [parts, rows, gain.reshape(1, width)]
    if backward:
        shapes.append(jax.ShapeDtypeStruct((1, width), f32))
        operands.append(passed)
    return comm_call(
        functools.partial(turn_kernel, backward, rounded),
        shapes,
        [
            pltpu.VMEM((2, count, width), bf16),
            pltpu.VMEM((count, width), bf16),
            pltpu.VMEM((count, width), bf16),
        ]
        + [pltpu.SemaphoreType.DMA((6 * PIECES,))] * 2,
        collective_id,
        *operands,
        cargo=cargo,
    )


def plane_peers():
    core, y, x, tensor = place()
    return [
        {"section": 1 - core},
        {"tensor": tensor + 1 - 2 * x},
        {"tensor": tensor + 2 - 4 * y},
    ]


def plane_gather_kernel(own, out, send, recv):
    greet(plane_peers())
    plane_exchange(own, out, send, recv)


class Chores:
    def __init__(self, units=()):
        self.units = list(units)

    def some(self, count):
        for _ in range(min(count, len(self.units))):
            self.units.pop(0)()

    def rest(self):
        self.some(len(self.units))


def stream(count, source_at, buffers, sems, work):
    def fetch(at):
        return pltpu.make_async_copy(source_at(at), buffers.at[at % 2], sems.at[at % 2])

    def unit(at):
        fetch(at).wait()
        work(at, buffers.at[at % 2])
        if at + 2 < count:
            fetch(at + 2).start()

    for at in range(min(2, count)):
        fetch(at).start()
    return [functools.partial(unit, at) for at in range(count)]


def plane_steps(own, out, send, recv):
    core, y, x, _ = place()
    other, beside, above = plane_peers()
    half = own.shape[0] // 2
    cut = [pl.ds(0, half), pl.ds(half, half)]

    def slot(along_y, along_x):
        return 4 * along_y + 2 * core + along_x

    me = slot(y, x)
    at_x, at_y, at_both = slot(y, 1 - x), slot(1 - y, x), slot(1 - y, 1 - x)

    def copy(src, where, index, device):
        made = remote(src, out.at[where], send.at[index], recv.at[index], device)
        made.start()
        return made

    to_x = [remote(own.at[cut[h]], out.at[me, cut[h]], send.at[h], recv.at[h], beside) for h in (0, 1)]
    to_y = [remote(own.at[cut[h]], out.at[me, cut[h]], send.at[2 + h], recv.at[2 + h], above) for h in (0, 1)]
    to_x[0].start()
    to_y[1].start()
    to_x[1].start()
    to_y[0].start()
    pending = [copy(own, me, 4, other)]
    out[me] = own[...]

    def onward(where, h, index, device):
        made = remote(
            out.at[where, cut[h]], out.at[where, cut[h]], send.at[index], recv.at[index], device
        )
        made.start()
        return made

    yield
    to_x[0].wait_recv()
    diag_y = onward(at_x, 0, 5, above)
    pending.append(onward(at_x, 0, 6, other))
    to_y[1].wait_recv()
    diag_x = onward(at_y, 1, 7, beside)
    pending.append(onward(at_y, 1, 8, other))
    yield
    to_x[1].wait_recv()
    pending.append(onward(at_x, 1, 9, other))
    to_y[0].wait_recv()
    pending.append(onward(at_y, 0, 10, other))
    yield
    diag_y.wait_recv()
    pending.append(onward(at_both, 0, 11, other))
    diag_x.wait_recv()
    pending.append(onward(at_both, 1, 12, other))
    yield
    for made in to_x + to_y + [diag_x, diag_y]:
        made.wait_send()
    for made in pending:
        made.wait()


def plane_exchange(own, out, send, recv, chores=Chores()):
    for _ in plane_steps(own, out, send, recv):
        chores.some(2)
    chores.rest()


def head_gather_kernel(own, table, grads, out, parts, buffers, sems, send, recv):
    greet(plane_peers())
    rows = own.shape[0]

    def work(at, block):
        parts[at] = mm(block[...], table[...], 1, 1).astype(bf16)

    chores = Chores(
        stream(8, lambda at: grads.at[pl.ds(rows * at, rows)], buffers, sems, work)
    )
    plane_exchange(own, out, send, recv, chores)


def head_gather(rows, table, grads):
    count, width = rows.shape
    return comm_call(
        head_gather_kernel,
        [jax.ShapeDtypeStruct((8, count, width), bf16)] * 2,
        [
            pltpu.VMEM((2, count, grads.shape[1]), bf16),
            pltpu.SemaphoreType.DMA((2,)),
        ]
        + [pltpu.SemaphoreType.DMA((13,))] * 2,
        7,
        rows,
        table,
        streamed=[grads],
        room=40,
    )


def plane_sum(
    parts,
    out,
    near,
    mixed,
    via_x,
    via_y,
    from_x,
    from_y,
    hop_x,
    hop_y,
    send,
    recv,
    chores=Chores(),
    make=None,
):
    core, y, x, _ = place()
    other, beside, above = plane_peers()
    half = out.shape[0] // 2
    cut = [pl.ds(0, half), pl.ds(half, half)]

    def slot(at_core, along_y, along_x):
        return 4 * along_y + 2 * at_core + along_x

    targets = [(1 - y, 1 - x), (y, 1 - x), (1 - y, x), (y, x)]
    handed = []

    def hand(index):
        along_y, along_x = targets[index]
        if make is not None:
            make(slot(1 - core, along_y, along_x))
        made = remote(
            parts.at[slot(1 - core, along_y, along_x)],
            near.at[index],
            send.at[index],
            recv.at[index],
            other,
        )
        made.start()
        handed.append(made)
        if make is not None:
            make(slot(core, along_y, along_x))

    for index in range(1 if make is not None else 4):
        hand(index)

    def hand_next(index):
        if make is not None:
            hand(index)

    def joined(index, where=slice(None)):
        along_y, along_x = targets[index]
        mine = parts[slot(core, along_y, along_x), where]
        return mine.astype(f32) + near[index, where].astype(f32)

    def start(src, dst, index, device):
        made = remote(src, dst, send.at[index], recv.at[index], device)
        made.start()
        return made

    handed[0].wait_recv()
    mixed[0] = joined(0).astype(bf16)
    diag_x = start(mixed.at[0, cut[0]], via_x, 4, beside)
    diag_y = start(mixed.at[0, cut[1]], via_y, 5, above)
    hand_next(1)
    handed[1].wait_recv()
    mixed[1] = joined(1).astype(bf16)
    straight_x = start(mixed.at[1, cut[0]], from_x.at[cut[0]], 6, beside)
    hand_next(2)
    handed[2].wait_recv()
    mixed[2] = joined(2).astype(bf16)
    straight_y = start(mixed.at[2, cut[1]], from_y.at[cut[1]], 7, above)
    chores.some(2)
    diag_x.wait_recv()
    hop_y[...] = (mixed[2, cut[0]].astype(f32) + via_x[...].astype(f32)).astype(bf16)
    turned_y = start(hop_y, from_y.at[cut[0]], 8, above)
    diag_y.wait_recv()
    hop_x[...] = (mixed[1, cut[1]].astype(f32) + via_y[...].astype(f32)).astype(bf16)
    turned_x = start(hop_x, from_x.at[cut[1]], 9, beside)
    hand_next(3)
    chores.rest()
    handed[3].wait_recv()
    straight_x.wait_recv()
    turned_y.wait_recv()
    out[cut[0]] = joined(3, cut[0]) + from_x[cut[0]].astype(f32) + from_y[cut[0]].astype(f32)
    straight_y.wait_recv()
    turned_x.wait_recv()
    out[cut[1]] = joined(3, cut[1]) + from_x[cut[1]].astype(f32) + from_y[cut[1]].astype(f32)
    for made in handed + [diag_x, diag_y, straight_x, straight_y, turned_x, turned_y]:
        made.wait_send()


def plane_scratch(shape):
    half = (shape[0] // 2,) + shape[1:]
    shapes = [(4,) + shape, (3,) + shape, half, half, shape, shape, half, half]
    return [pltpu.VMEM(one, bf16) for one in shapes] + [pltpu.SemaphoreType.DMA((10,))] * 2


LOOK = 512


def lookup_reduce_kernel(ids, table, out, parts, *scratch):
    greet(plane_peers())
    batches, depth, slots = out.shape
    row = lax.broadcasted_iota(jnp.int32, (LOOK, slots), 0)

    def make(part):
        def step(batch, carry):
            wanted = ids[batch * 8 + part]
            total = jnp.zeros((depth, slots), f32)
            for lead in range(0, table.shape[1], LOOK):
                hit = jnp.where(row == wanted - lead, 1.0, 0.0).astype(bf16)
                total += jnp.dot(table[:, lead : lead + LOOK], hit, preferred_element_type=f32)
            parts[part, batch] = total.astype(bf16)
            return carry

        if batches > 4:
            lax.fori_loop(0, batches, step, 0)
        else:
            for batch in range(batches):
                step(batch, 0)

    plane_sum(parts, out, *scratch, make=make)


def lookup_reduce(table, ids):
    batches, parts, _, slots = ids.shape
    block = (batches, table.shape[0], slots)
    return comm_call(
        lookup_reduce_kernel,
        jax.ShapeDtypeStruct(block, f32),
        [pltpu.VMEM((parts,) + block, bf16)] + plane_scratch(block),
        3,
        ids.reshape(batches * parts, 1, slots),
        table,
        room=14,
    )


def head_reduce_kernel(parts, rows, valid, grads, out, table_grad, held, buffers, sems, *scratch):
    greet(plane_peers())
    width = buffers.shape[2]
    for lead in range(0, rows.shape[1], 128):
        held[:, lead : lead + 128] = rows[:, lead : lead + 128] * valid[...]

    def work(at, block):
        table_grad[:, width * at : width * at + width] = mm(held[...], block[...], 0, 0).astype(bf16)

    steps = grads.shape[1] // width
    chores = Chores(
        stream(steps, lambda at: grads.at[:, pl.ds(width * at, width)], buffers, sems, work)
    )
    plane_sum(parts, out, *scratch, chores=chores)


def head_reduce(parts, rows, valid, grads):
    _, count, width = parts.shape
    step = 512
    return comm_call(
        head_reduce_kernel,
        [
            jax.ShapeDtypeStruct((count, width), f32),
            jax.ShapeDtypeStruct((width, grads.shape[1]), bf16),
        ],
        [
            pltpu.VMEM(rows.shape, bf16),
            pltpu.VMEM((2, rows.shape[0], step), bf16),
            pltpu.SemaphoreType.DMA((2,)),
        ]
        + plane_scratch((count, width)),
        4,
        parts,
        rows,
        valid,
        streamed=[grads],
        room=42,
    )


def batch_peers(count):
    me = lax.axis_index("batch")
    return [{"batch": lax.rem(me + step, count)} for step in range(1, count)]


def batch_exchange(count, ins, outs, send, recv):
    me = lax.axis_index("batch")
    copies = []
    for index, peer in enumerate(batch_peers(count)):
        for kind in range(len(ins)):
            at = index * len(ins) + kind
            copies.append(remote(ins[kind], outs[kind].at[me], send.at[at], recv.at[at], peer))
            copies[-1].start()
    for kind in range(len(ins)):
        outs[kind][me] = ins[kind][...]
    return copies


def batch_gather_kernel(count, *refs):
    kinds = (len(refs) - 2) // 2
    greet(batch_peers(count))
    for copy in batch_exchange(count, refs[:kinds], refs[kinds : 2 * kinds], *refs[2 * kinds :]):
        copy.wait()


def batch_gather(blocks, collective_id):
    count = lax.axis_size("batch")
    return comm_call(
        functools.partial(batch_gather_kernel, count),
        [jax.ShapeDtypeStruct((count,) + block.shape, block.dtype) for block in blocks],
        [pltpu.SemaphoreType.DMA(((count - 1) * len(blocks),))] * 2,
        collective_id,
        *blocks,
    )


def tail_gather_kernel(count, leads, *refs):
    blocks, refs = refs[:count], refs[count:]
    pieces, refs = refs[: len(leads)], refs[len(leads) :]
    out, few_out, own, few, send, recv, few_send, few_recv = refs
    me = lax.axis_index("batch")
    for step, block in enumerate(blocks):
        own[lax.rem(me + count - step, count)] = block[...]
    few[...] = jnp.zeros(few.shape, few.dtype)
    for lead, piece in zip(leads, pieces):
        few[lead : lead + piece.shape[0], : piece.shape[1]] = piece[...]
    greet(plane_peers())
    both = [plane_steps(few, few_out, few_send, few_recv), plane_steps(own, out, send, recv)]
    for _ in itertools.zip_longest(*both):
        pass


def tail_gather(blocks, pieces, rows):
    count = len(blocks)
    own = (count,) + blocks[0].shape
    return comm_call(
        functools.partial(tail_gather_kernel, count, [lead for lead, _ in pieces]),
        [
            jax.ShapeDtypeStruct((8,) + own, blocks[0].dtype),
            jax.ShapeDtypeStruct((8, rows, D), f32),
        ],
        [pltpu.VMEM(own, blocks[0].dtype), pltpu.VMEM((rows, D), f32)]
        + [pltpu.SemaphoreType.DMA((13,))] * 4,
        10,
        *blocks,
        *[piece for _, piece in pieces],
    )


def batch_trade_kernel(count, leads, parts, *refs, load=None):
    pieces, refs = refs[: len(leads)], refs[len(leads) :]
    out, few_out, few, send, recv, few_send, few_recv = refs
    few[...] = jnp.zeros(few.shape, few.dtype)
    for lead, piece in zip(leads, pieces):
        few[lead : lead + piece.shape[0], : piece.shape[1]] = piece[...]
    me = lax.axis_index("batch")
    core, y, _, tensor = place()
    peers = plane_peers() + batch_peers(count)
    if load is not None:
        peers.append({"section": 1 - core, "tensor": tensor + 2 - 4 * y})
    greet(peers)
    cargo = load() if load is not None else []
    for one in cargo:
        one.start()
    copies = []
    for index, peer in enumerate(batch_peers(count)):
        copies.append(
            remote(parts.at[peer["batch"]], out.at[me], send.at[index], recv.at[index], peer)
        )
        copies[-1].start()
    out[me] = parts[me]
    plane_exchange(few, few_out, few_send, few_recv)
    for copy in copies:
        copy.wait()
    for one in cargo:
        one.wait()


def batch_trade(parts, pieces, rows, collective_id, cargo=None):
    count = parts.shape[0]
    return comm_call(
        functools.partial(batch_trade_kernel, count, [lead for lead, _ in pieces]),
        [
            jax.ShapeDtypeStruct(parts.shape, parts.dtype),
            jax.ShapeDtypeStruct((8, rows, D), f32),
        ],
        [pltpu.VMEM((rows, D), f32)]
        + [pltpu.SemaphoreType.DMA((count - 1,))] * 2
        + [pltpu.SemaphoreType.DMA((13,))] * 2,
        collective_id,
        parts,
        *[piece for _, piece in pieces],
        cargo=cargo,
    )


ROWS = 256

PACKED = ((0, 0), (0, 1), (1, 0), (1, 1), (2, 0), (2, 1), (0, 2), (1, 2), (2, 2))


def packed(blocks, out):
    cuts = [blocks[:, kind, HEAD * head : HEAD * head + HEAD] for kind, head in PACKED]
    return jnp.concatenate(cuts + [out[:, 2 * HEAD :], out[:, : 2 * HEAD]], 1)


def unpacked(block):
    place_of = {pair: at * HEAD for at, pair in enumerate(PACKED)}
    kinds = []
    for kind in range(3):
        cuts = [
            block[:, place_of[kind, head] : place_of[kind, head] + HEAD] for head in range(3)
        ]
        kinds.append(jnp.concatenate(cuts, 1))
    return jnp.stack(kinds, 1)


def attention_heads(mixed, queries, keys, values):
    low = lax.broadcasted_iota(jnp.int32, (mixed.shape[0], 128), 1) < HEAD
    tile = [mixed[:, 128 * at : 128 * at + 128] for at in range(5)]
    scaled = tile[0] * (HEAD**-0.5)
    queries[0] = jnp.where(low, scaled, 0.0).astype(bf16)
    queries[1] = jnp.where(low, 0.0, scaled).astype(bf16)
    queries[2] = jnp.where(low, tile[3] * (HEAD**-0.5), 0.0).astype(bf16)
    keys[0] = tile[1].astype(bf16)
    keys[1] = pltpu.roll(tile[3], HEAD, 1).astype(bf16)
    values[0] = tile[2].astype(bf16)
    values[1] = tile[4].astype(bf16)


def key_bias(length, total):
    at = lax.broadcasted_iota(jnp.int32, (1, total), 1)
    return jnp.where(at < length, 0.0, masked_score)


def masked(scores, bias, lead):
    scores = scores + bias
    row = lax.broadcasted_iota(jnp.int32, (ROWS, ROWS), 0)
    column = lax.broadcasted_iota(jnp.int32, (ROWS, ROWS), 1)
    last = jnp.where(column <= row, scores[:, lead:], masked_score)
    return last if lead == 0 else jnp.concatenate([scores[:, :lead], last], 1)


def attention_forward_kernel(
    length, x, weight, taps, partial, mixed_out, projected_out, context, totals, projected, queries, keys, values
):
    total = x.shape[0]
    width = 5 * 128
    projected[:8] = jnp.zeros((8, width), f32)
    for lead in range(0, total, ROWS):
        block = jnp.dot(x[lead : lead + ROWS], weight[:, :width], preferred_element_type=f32)
        projected[lead + 8 : lead + 8 + ROWS] = block
        projected_out[lead : lead + ROWS] = block.astype(bf16)
    for lead in range(0, total, ROWS):
        mixed = taps[0:1] * projected[lead + 8 : lead + 8 + ROWS]
        mixed += taps[1:2] * projected[lead + 7 : lead + 7 + ROWS]
        mixed += taps[2:3] * projected[lead + 6 : lead + 6 + ROWS]
        mixed = mixed.astype(bf16)
        mixed_out[lead : lead + ROWS] = mixed
        rows = pl.ds(lead, ROWS)
        attention_heads(
            mixed.astype(f32), queries.at[:, rows], keys.at[:, rows], values.at[:, rows]
        )
    bias = key_bias(length[0], total)
    lane = lax.broadcasted_iota(jnp.int32, (ROWS, 128), 1)
    low = lane < HEAD
    for lead in range(0, total, ROWS):
        reach = lead + ROWS
        found = []
        log_sums = jnp.zeros((ROWS, 128), f32)
        for head in range(3):
            scores = mm(queries[head, lead:reach], keys[head // 2, :reach], 1, 1)
            scores = masked(scores, bias[:, :reach], lead)
            peak = jnp.max(scores, axis=1, keepdims=True)
            raised = jnp.exp(scores - peak)
            weight_sum = jnp.sum(raised, axis=1, keepdims=True)
            probs = (raised * (1.0 / weight_sum)).astype(bf16)
            found.append(
                jnp.dot(probs, values[head // 2, :reach], preferred_element_type=f32)
            )
            log_sums = jnp.where(lane == head, peak + jnp.log(weight_sum), log_sums)
        totals[lead:reach] = log_sums
        joined = jnp.concatenate(
            [
                jnp.where(low, 0.0, pltpu.roll(found[2], HEAD, 1)),
                jnp.where(low, found[0], found[1]),
            ],
            1,
        ).astype(bf16)
        context[lead:reach] = joined
        partial[lead:reach] = mm(joined, weight[:, 512:768], 1, 1).astype(bf16)


def attention_call(body, out_shape, scratch, room, length, *operands):
    whole = pl.BlockSpec(memory_space=pltpu.VMEM)
    return pl.pallas_call(
        body,
        out_shape=out_shape,
        in_specs=[pl.BlockSpec(memory_space=pltpu.SMEM)] + [whole] * len(operands),
        out_specs=[whole] * len(out_shape),
        scratch_shapes=scratch,
        compiler_params=pltpu.CompilerParams(vmem_limit_bytes=room << 20),
    )(length.reshape(1), *operands)


def attention_forward(x, length, weight, taps):
    total = x.shape[0]
    partial, *kept = attention_call(
        attention_forward_kernel,
        [
            jax.ShapeDtypeStruct((total, D), bf16),
            jax.ShapeDtypeStruct((total, 640), bf16),
            jax.ShapeDtypeStruct((total, 640), bf16),
            jax.ShapeDtypeStruct((total, 256), bf16),
            jax.ShapeDtypeStruct((total, 128), f32),
        ],
        [
            pltpu.VMEM((total + 8, 640), f32),
            pltpu.VMEM((3, total, 128), bf16),
            pltpu.VMEM((2, total, 128), bf16),
            pltpu.VMEM((2, total, 128), bf16),
        ],
        14,
        length,
        x,
        weight,
        taps,
    )
    return partial, (x, *kept)


def attention_backward_kernel(
    length,
    grads,
    x,
    weight,
    taps,
    mixed,
    projected,
    context,
    totals,
    partial,
    weight_grad,
    taps_grad,
    queries,
    keys,
    values,
    outer,
    key_grad,
    value_grad,
    mixed_grad,
    projected_grad,
    turned,
):
    total = x.shape[0]
    width = 5 * 128
    low = lax.broadcasted_iota(jnp.int32, (ROWS, 128), 1) < HEAD
    for lead in range(0, total, ROWS):
        rows = pl.ds(lead, ROWS)
        attention_heads(
            mixed[lead : lead + ROWS].astype(f32),
            queries.at[:, rows],
            keys.at[:, rows],
            values.at[:, rows],
        )
        block = jnp.dot(grads[lead : lead + ROWS], weight[:, 512:768], preferred_element_type=f32)
        third, pair = block[:, :128], block[:, 128:]
        outer[0, lead : lead + ROWS] = jnp.where(low, pair, 0.0).astype(bf16)
        outer[1, lead : lead + ROWS] = jnp.where(low, 0.0, pair).astype(bf16)
        outer[2, lead : lead + ROWS] = jnp.where(low, pltpu.roll(third, HEAD, 1), 0.0).astype(bf16)
    mixed_grad[total:] = jnp.zeros((8, width), f32)
    bias = key_bias(length[0], total)
    for lead in reversed(range(0, total, ROWS)):
        reach = lead + ROWS
        query_grad = []
        for head in range(3):
            its_keys, its_values = keys[head // 2, :reach], values[head // 2, :reach]
            scores = mm(queries[head, lead:reach], its_keys, 1, 1)
            scores = masked(scores, bias[:, :reach], lead)
            probs = jnp.exp(scores - totals[lead:reach, head : head + 1])
            grad_probs = mm(outer[head, lead:reach], its_values, 1, 1)
            product = probs * grad_probs
            inner = jnp.sum(product, axis=1, keepdims=True)
            grad_scores = (product - probs * inner).astype(bf16)
            query_grad.append(jnp.dot(grad_scores, its_keys, preferred_element_type=f32))
            value_part = mm(probs.astype(bf16), outer[head, lead:reach], 0, 0)
            key_part = mm(grad_scores, queries[head, lead:reach], 0, 0)
            if lead + ROWS == total and head != 1:
                value_grad[head // 2] = value_part
                key_grad[head // 2] = key_part
            else:
                value_grad[head // 2, :reach] += value_part
                key_grad[head // 2, :reach] += key_part
        scale = HEAD**-0.5
        mixed_grad[lead:reach, 0:128] = jnp.where(low, query_grad[0], query_grad[1]) * scale
        mixed_grad[lead:reach, 384:512] = query_grad[2] * scale
    grown = jnp.zeros((8, width), f32)
    for lead in reversed(range(0, total, ROWS)):
        reach = lead + ROWS
        mixed_grad[lead:reach, 128:256] = key_grad[0, lead:reach]
        mixed_grad[lead:reach, 256:384] = value_grad[0, lead:reach]
        mixed_grad[lead:reach, 384:512] = jnp.where(
            low, mixed_grad[lead:reach, 384:512], pltpu.roll(key_grad[1, lead:reach], HEAD, 1)
        )
        mixed_grad[lead:reach, 512:640] = value_grad[1, lead:reach]
        here = projected[lead:reach].astype(f32)
        back = jnp.zeros((ROWS, width), f32)
        parts = []
        for tap in range(3):
            ahead = mixed_grad[lead + tap : reach + tap]
            back += taps[tap : tap + 1] * ahead
            parts.append(jnp.sum(ahead * here, axis=0, keepdims=True))
        grown += jnp.concatenate(parts + [jnp.zeros((5, width), f32)], 0)
        back = back.astype(bf16)
        partial[lead:reach] = mm(back, weight[:, :width], 1, 1).astype(bf16)
        projected_grad[lead:reach] = back
    taps_grad[...] = grown
    turned[0] = x[...].T
    turned[1] = grads[...].T
    for lead in range(0, D, ROWS):
        reach = lead + ROWS
        across = jnp.dot(turned[0, lead:reach], projected_grad[...], preferred_element_type=f32)
        outward = jnp.dot(turned[1, lead:reach], context[...], preferred_element_type=f32)
        weight_grad[lead:reach, :512] = across[:, :512].astype(bf16)
        weight_grad[lead:reach, 512:640] = (across[:, 512:] + outward[:, :128]).astype(bf16)
        weight_grad[lead:reach, 640:] = outward[:, 128:].astype(bf16)


def attention_backward(grads, length, weight, taps, kept):
    x, mixed, projected, context, totals = kept
    total = x.shape[0]
    return attention_call(
        attention_backward_kernel,
        [
            jax.ShapeDtypeStruct((total, D), bf16),
            jax.ShapeDtypeStruct((D, 768), bf16),
            jax.ShapeDtypeStruct((8, 640), f32),
        ],
        [
            pltpu.VMEM((3, total, 128), bf16),
            pltpu.VMEM((2, total, 128), bf16),
            pltpu.VMEM((2, total, 128), bf16),
            pltpu.VMEM((3, total, 128), bf16),
            pltpu.VMEM((2, total, 128), f32),
            pltpu.VMEM((2, total, 128), f32),
            pltpu.VMEM((total + 8, 640), f32),
            pltpu.VMEM((total, 640), bf16),
            pltpu.VMEM((2, D, total), bf16),
        ],
        20,
        length,
        grads,
        x,
        weight,
        taps,
        mixed,
        projected,
        context,
        totals,
    )


def ffn_forward_kernel(x, up, *refs):
    downs, partial = refs[:-1], refs[-1]
    for lead in range(0, x.shape[0], ROWS):
        hidden = jnp.dot(x[lead : lead + ROWS], up[...], preferred_element_type=f32)
        active = jnp.square(jnp.maximum(hidden, 0.0)).astype(bf16)
        total, first = 0.0, 0
        for down in downs:
            width = down.shape[1]
            total += mm(active[:, first : first + width], down[...], 1, 1)
            first += width
        partial[lead : lead + ROWS] = total.astype(bf16)


def ffn_backward_kernel(grads, x, up, *refs):
    downs = refs[:-6]
    partial, up_grad, down_grad, hidden_grad, active, turned = refs[-6:]
    for lead in range(0, x.shape[0], ROWS):
        rows = pl.ds(lead, ROWS)
        hidden = jnp.dot(x[rows], up[...], preferred_element_type=f32)
        positive = jnp.maximum(hidden, 0.0)
        active[rows] = jnp.square(positive).astype(bf16)
        back = [jnp.dot(grads[rows], down[...], preferred_element_type=f32) for down in downs]
        back = back[0] if len(back) == 1 else jnp.concatenate(back, 1)
        back = (back * 2.0 * positive).astype(bf16)
        hidden_grad[rows] = back
        partial[rows] = mm(back, up[...], 1, 1).astype(bf16)
    turned[0] = x[...].T
    turned[1] = grads[...].T
    for lead in range(0, D, ROWS):
        rows = pl.ds(lead, ROWS)
        up_grad[rows] = jnp.dot(
            turned[0, rows], hidden_grad[...], preferred_element_type=f32
        ).astype(bf16)
        down_grad[rows] = jnp.dot(
            turned[1, rows], active[...], preferred_element_type=f32
        ).astype(bf16)


def local_call(body, out_shape, scratch, *operands):
    whole = pl.BlockSpec(memory_space=pltpu.VMEM)
    return pl.pallas_call(
        body,
        out_shape=out_shape,
        in_specs=[whole] * len(operands),
        out_specs=[whole] * len(out_shape),
        scratch_shapes=scratch,
        compiler_params=pltpu.CompilerParams(vmem_limit_bytes=14 << 20),
    )(*operands)


def ffn_forward(x, weights):
    up, downs = weights
    (partial,) = local_call(
        ffn_forward_kernel, [jax.ShapeDtypeStruct(x.shape, bf16)], [], x, up, *downs
    )
    return partial


def ffn_backward(grads, weights, x):
    up, downs = weights
    return local_call(
        ffn_backward_kernel,
        [
            jax.ShapeDtypeStruct(x.shape, bf16),
            jax.ShapeDtypeStruct(up.shape, bf16),
            jax.ShapeDtypeStruct(up.shape, bf16),
        ],
        [
            pltpu.VMEM((x.shape[0], up.shape[1]), bf16),
            pltpu.VMEM((x.shape[0], up.shape[1]), bf16),
            pltpu.VMEM((2, D, x.shape[0]), bf16),
        ],
        grads,
        x,
        up,
        *downs,
    )


def spread_kernel(ids, grads, base, out, wanted):
    at = pl.program_id(0)
    columns = out.shape[1]
    parts, batches, _, slots = grads.shape

    @pl.when(at == 0)
    def _():
        def turned(group, carry):
            across = ids[pl.ds(pl.multiple_of(group * 8, 8), 8)].T
            for part in range(8):
                wanted[group * 8 + part] = jnp.broadcast_to(
                    across[:, part : part + 1], (slots, 128)
                ).astype(jnp.int16)
            return carry

        lax.fori_loop(0, batches * parts // 8, turned, 0)

    lane = lax.broadcasted_iota(jnp.int16, (slots, 128), 1) + (at * columns).astype(jnp.int16)
    together = min(batches, 4)

    def step(index, total):
        for inner in range(together):
            batch = index * together + inner
            for part in range(parts):
                here = wanted[batch * parts + part]
                hit = jnp.concatenate(
                    [
                        jnp.where(here == lane + jnp.int16(lead), bf16(1), bf16(0))
                        for lead in range(0, columns, 128)
                    ],
                    1,
                )
                total += jnp.dot(grads[part, batch], hit, preferred_element_type=f32)
        return total

    out[...] = lax.fori_loop(0, batches // together, step, base[...].astype(f32))


def spread(grads, ids, base):
    parts, batches, depth, slots = grads.shape
    vocab_rows = base.shape[1]
    columns = 256
    return pl.pallas_call(
        spread_kernel,
        grid=(vocab_rows // columns,),
        out_shape=jax.ShapeDtypeStruct((depth, vocab_rows), f32),
        in_specs=[
            pl.BlockSpec((batches * parts, slots), lambda at: (0, 0)),
            pl.BlockSpec((parts, batches, depth, slots), lambda at: (0, 0, 0, 0)),
            pl.BlockSpec((depth, columns), lambda at: (0, at)),
        ],
        out_specs=pl.BlockSpec((depth, columns), lambda at: (0, at)),
        scratch_shapes=[pltpu.VMEM((batches * parts, slots, 128), jnp.int16)],
        compiler_params=pltpu.CompilerParams(vmem_limit_bytes=32 << 20),
    )(ids.reshape(batches * parts, slots), grads, base)


def summed(landed):
    sums = [
        (one.astype(f32) + two.astype(f32)).astype(bf16)
        for one, two in zip(landed[::2], landed[1::2])
    ]
    return jnp.concatenate(sums, -1)


def over_batch(block):
    return lax.psum_scatter(block, "batch", scatter_dimension=0, tiled=False)


def tie(*values):
    return lax.optimization_barrier(values)


def on_device(
    token_ids,
    seq_lengths,
    embed_table,
    norm_gains,
    final_gain,
    qkv_weight,
    qkv_conv,
    out_weight,
    up_weight,
    down_weight,
    logit_grad,
):
    section = lax.axis_index("section")
    first = section == 0
    core, seq_at, x_at, _ = place()
    quarter = 2 * core + x_at
    me = lax.axis_index("tensor")
    at_batch = lax.axis_index("batch")
    tensor_count = lax.axis_size("tensor")
    batch_count = lax.axis_size("batch")
    section_count = lax.axis_size("section")
    slot_length = token_ids.shape[1]
    shard_rows = slot_length // tensor_count
    local_width = out_weight.shape[1]
    heads_here = local_width // HEAD
    hidden_width = up_weight.shape[2]
    root_scale = math.sqrt(D)
    depth = D // batch_count
    length = seq_lengths[seq_at]
    sequences = token_ids.shape[0]

    table_own = embed_table.astype(bf16).T
    attn_own = packed(qkv_weight[0].astype(bf16), out_weight[0].astype(bf16).T)
    ffn_own = jnp.concatenate([up_weight[0].astype(bf16), down_weight[0].astype(bf16).T], 1)
    attn_all = lax.all_gather(attn_own, "batch", axis=0, tiled=True)
    ffn_all = lax.all_gather(ffn_own, "batch", axis=0, tiled=True)
    table_turned = lax.all_gather(table_own, "batch", axis=0, tiled=True)

    gain_width = final_gain.shape[0]
    whole_at = (section * batch_count + at_batch) * tensor_count + me
    gains_own = jnp.concatenate([norm_gains.reshape(4, gain_width), final_gain[None]])
    gains_own = lax.dynamic_update_slice_in_dim(
        jnp.zeros((5, D), f32), gains_own.astype(bf16).astype(f32), whole_at * gain_width, 1
    )
    taps_own = qkv_conv[0].astype(bf16).astype(f32).transpose(1, 0, 2, 3)
    taps_own = lax.dynamic_update_slice_in_dim(
        jnp.zeros((3, 3, heads_here, HEAD), f32), taps_own, at_batch * qkv_conv.shape[4], 3
    ).reshape(3, 3, local_width)
    small = jnp.concatenate([gains_own, packed(taps_own, jnp.zeros((3, local_width), f32))])
    all_ids, small = batch_gather([token_ids.reshape(-1, 128), small], 5)
    small = jnp.sum(small, 0)

    vocab_rows = embed_table.shape[0]
    owner_start = (section * tensor_count + me) * vocab_rows
    local_ids = all_ids.reshape(batch_count, sequences * 4, 1, shard_rows) - owner_start
    total = lookup_reduce(table_own, local_ids).astype(bf16)
    embedded, small = batch_trade(total, [(0, small)], 16, 8)
    gains_all = jnp.sum(small[:, :5], 0)
    final_scale = gains_all[4]
    taps_here = [
        lax.dynamic_index_in_dim(
            small, 4 * (quarter // 2) + 2 * layer + quarter % 2, 0, keepdims=False
        )[5:8, :640]
        for layer in range(section_count)
    ]
    embedded = embedded.reshape(D, shard_rows).T

    part = hidden_width // 2
    first_rows = embedded.astype(f32) * root_scale
    normed = (first_rows * norm_factor(first_rows) * gains_all[0]).astype(bf16)
    gathered, attn_first = group_gather(normed, 1, cargo=("out", [(0, attn_all, 0, D)]))
    partial, attn_kept_first = attention_forward(gathered.reshape(-1, D), length, attn_first, taps_here[0])
    gathered, first_middle, up, down = turn(
        partial,
        first_rows,
        gains_all[1],
        20,
        False,
        cargo=("out", [(0, ffn_all, 0, hidden_width), (0, ffn_all, hidden_width, hidden_width)]),
    )
    ffn_first = (up, [down])
    ffn_kept_first = gathered.reshape(-1, D)
    partial = ffn_forward(ffn_kept_first, ffn_first)
    gathered, second_rows, attn_second, down_one = turn(
        partial,
        first_middle,
        gains_all[2],
        21,
        True,
        cargo=("out", [(1, attn_all, 0, D), (1, ffn_all, hidden_width, part)]),
    )
    partial, attn_kept_second = attention_forward(
        gathered.reshape(-1, D), length, attn_second, taps_here[1]
    )
    gathered, second_middle, up, down_two = turn(
        partial,
        second_rows,
        gains_all[3],
        24,
        False,
        cargo=("out", [(1, ffn_all, 0, hidden_width), (1, ffn_all, hidden_width + part, part)]),
    )
    ffn_second = (up, [down_one, down_two])
    ffn_kept_second = gathered.reshape(-1, D)
    partial = ffn_forward(ffn_kept_second, ffn_second)

    def halves(blob):
        return blob.reshape(batch_count, 2, depth // 2, blob.shape[1])

    final_rows = (second_middle + group_reduce(partial, 2)).astype(bf16).astype(f32)
    normed_final = (final_rows * norm_factor(final_rows) * final_scale).astype(bf16)
    grads_flat = logit_grad.reshape(-1, vocab_rows)
    final_both, grad_parts = head_gather(normed_final, table_turned, grads_flat)
    final_both = final_both.reshape(-1, D)
    valid = (jnp.arange(slot_length)[None, :] < seq_lengths[:, None]).reshape(-1, 1)
    valid = jnp.broadcast_to(valid, (valid.shape[0], 128)).astype(bf16)
    grad_final, head_table = head_reduce(grad_parts, final_both, valid, grads_flat)
    own_at = quarter * shard_rows + jnp.arange(shard_rows)
    grad_final = jnp.where((own_at < length)[:, None], grad_final, 0.0)
    logits = mm(final_both, table_turned, 1, 0).astype(bf16).reshape(sequences, slot_length, -1)
    head_done = lax.psum_scatter(head_table, "batch", scatter_dimension=0, tiled=True)

    grad_rows, grad_final_gain = norm_back(grad_final, final_rows, final_scale)
    gathered = group_gather(grad_rows.astype(bf16), 13).reshape(-1, D)
    partial, up, down = ffn_backward(gathered, ffn_second, ffn_kept_second)
    up, down = halves(up), halves(down)
    gathered, grad_rows, gain_2f, *landed_second = turn(
        partial,
        second_middle,
        gains_all[3],
        22,
        False,
        passed=grad_rows,
        cargo=("in", [(1, up, 0, hidden_width), (1, down, 0, part)]),
    )
    partial, blob, taps_second = attention_backward(
        gathered.reshape(-1, D), length, attn_second, taps_here[1], attn_kept_second
    )
    gathered, grad_rows, gain_2a, *landed = turn(
        partial,
        second_rows,
        gains_all[2],
        23,
        True,
        passed=grad_rows,
        cargo=("in", [(1, down, part, part), (1, halves(blob), 0, D)]),
    )
    second_sum = summed(landed_second + landed)
    partial, up, down = ffn_backward(gathered.reshape(-1, D), ffn_first, ffn_kept_first)
    up, down = halves(up), halves(down)
    gathered, grad_rows, gain_1f, *landed_first = turn(
        partial,
        first_middle,
        gains_all[1],
        25,
        False,
        passed=grad_rows,
        cargo=("in", [(0, up, 0, hidden_width), (0, down, 0, part)]),
    )
    taps_again, second_sum, head_done, gain_1f = tie(
        taps_here[0], second_sum, head_done, gain_1f
    )
    partial, blob, taps_first = attention_backward(
        gathered.reshape(-1, D), length, attn_first, taps_again, attn_kept_first
    )
    second_done = over_batch(second_sum)
    grad_norm, *landed = group_reduce(
        partial, 14, cargo=("in", [(0, down, part, part), (0, halves(blob), 0, D)])
    )
    first_sum = summed(landed_first + landed)
    grad_norm, gain_1a = norm_back(grad_norm, first_rows, gains_all[0])
    grad_rows = grad_rows + grad_norm

    spread_own = (grad_rows * root_scale).astype(bf16).T.reshape(batch_count, depth, shard_rows)
    blocks = []
    for step in range(batch_count):
        block = lax.dynamic_index_in_dim(
            spread_own, lax.rem(at_batch + step, batch_count), 0, keepdims=False
        )
        if step > 0:
            pairs = [(at, (at + step) % batch_count) for at in range(batch_count)]
            block = lax.ppermute(block, "batch", pairs)
        blocks.append(block)
    gain_1a, second_done = tie(gain_1a, second_done)
    first_done = over_batch(first_sum)
    pieces = [(0, gain_1a), (1, gain_1f), (2, gain_2a), (3, gain_2f), (4, grad_final_gain)]
    every, rows = tail_gather(blocks, pieces + [(8, taps_first), (16, taps_second)], 32)

    gain_sums = jnp.sum(rows[:, :5], 0)
    holders = rows.reshape(2, 4, 32, D)[:, :, 8:24].reshape(2, 4, 2, 8, D)
    taps_sums = jnp.sum(lax.dynamic_index_in_dim(holders, me, 1, keepdims=False), 0)
    taps_sums = lax.dynamic_index_in_dim(taps_sums, section, 0, keepdims=False)[:3]
    own_sums = jnp.concatenate([gain_sums, taps_sums])
    own_sums, first_done = tie(own_sums, first_done)
    sums = own_sums
    for step in range(1, batch_count):
        pairs = [(at, (at + step) % batch_count) for at in range(batch_count)]
        sums = sums + lax.ppermute(own_sums, "batch", pairs)
    table_done = spread(every, local_ids, head_done).T
    gain_part = lax.dynamic_slice_in_dim(sums[:5], whole_at * gain_width, gain_width, 1)
    gains_done = gain_part[:4].reshape(2, 2, gain_width)
    final_done = gain_part[4]
    conv_part = unpacked(sums[5:8]).reshape(3, 3, heads_here, HEAD).transpose(1, 0, 2, 3)
    conv_done = lax.dynamic_slice_in_dim(
        conv_part, at_batch * qkv_conv.shape[4], qkv_conv.shape[4], 3
    )[None]
    def placed(first_part, second_part):
        keep = jnp.where(first, first_part, second_part)
        got = lax.ppermute(jnp.where(first, second_part, first_part), "section", [(0, 1), (1, 0)])
        return jnp.where(
            first, jnp.concatenate([keep, got], 0), jnp.concatenate([got, keep], 0)
        ).astype(f32)

    done = placed(first_done, second_done)
    up_done = done[:, :hidden_width][None]
    down_done = done[:, hidden_width : 2 * hidden_width].T[None]
    attn_done = done[:, 2 * hidden_width :]
    qkv_done = unpacked(attn_done)[None]
    out_done = jnp.concatenate([attn_done[:, 640:], attn_done[:, 576:640]], 1).T[None]
    return (
        logits,
        table_done,
        gains_done,
        final_done,
        qkv_done,
        conv_done,
        out_done,
        up_done,
        down_done,
    )


def solution(mesh):
    in_specs = (
        P("batch", None),
        P("batch"),
        P(("section", "tensor"), "batch"),
        P(None, None, ("section", "batch", "tensor")),
        P(("section", "batch", "tensor")),
        P("section", "batch", None, "tensor"),
        P("section", None, None, "tensor", "batch"),
        P("section", "tensor", "batch"),
        P("section", "batch", "tensor"),
        P("section", "tensor", "batch"),
        P("batch", None, ("section", "tensor")),
    )
    out_specs = (
        P("batch", None, ("section", "tensor")),
        P(("section", "tensor"), "batch"),
        P(None, None, ("section", "batch", "tensor")),
        P(("section", "batch", "tensor")),
        P("section", "batch", None, "tensor"),
        P("section", None, None, "tensor", "batch"),
        P("section", "tensor", "batch"),
        P("section", "batch", "tensor"),
        P("section", "tensor", "batch"),
    )
    return jax.shard_map(
        on_device, mesh=mesh, in_specs=in_specs, out_specs=out_specs, check_vma=False
    )
```
